32 devices in a mesh: items: 16 (over z, y, core), blk: 2 (over x).
Axes of the slice: x: 2, y: 2, z: 4, core: 2. Of those that a mesh axis runs over, the one named last changes fastest.
Arguments:
- patches: bfloat16 [16, 1024, 768], P('items', 'blk'), may hold values from -6 to 6
- grid: int32 [16, 2], P('items'), may hold values from 8 to 128, as said below
- norm_attn: float32 [768], replicated, may hold values from 0.1 to 1.9
- w_query: bfloat16 [768, 768], P('items', 'blk'), may hold values from -0.0546875 to 0.0546875
- w_key: bfloat16 [768, 768], P('items', 'blk'), may hold values from -0.21875 to 0.21875
- w_value: bfloat16 [768, 768], P('items', 'blk'), may hold values from -0.21875 to 0.21875
- w_out: bfloat16 [768, 768], P('items', 'blk'), may hold values from -0.875 to 0.875
- norm_mlp: float32 [768], replicated, may hold values from 0.1 to 1.9
- w_gate: bfloat16 [768, 2048], P('items', 'blk'), may hold values from -0.21875 to 0.21875
- w_up: bfloat16 [768, 2048], P('items', 'blk'), may hold values from -0.21875 to 0.21875
- w_down: bfloat16 [2048, 768], P('items', 'blk'), may hold values from -0.125 to 0.125
- cotangent: bfloat16 [16, 1024, 768], P('items', 'blk'), may hold values from -6 to 6
Outputs:
- output: bfloat16 [16, 1024, 768], P('items', 'blk')
- grad_patches: bfloat16 [16, 1024, 768], P('items', 'blk')
- grad_norm_attn: float32 [768], replicated
- grad_w_query: float32 [768, 768], P('items', 'blk')
- grad_w_key: float32 [768, 768], P('items', 'blk')
- grad_w_value: float32 [768, 768], P('items', 'blk')
- grad_w_out: float32 [768, 768], P('items', 'blk')
- grad_norm_mlp: float32 [768], replicated
- grad_w_gate: float32 [768, 2048], P('items', 'blk')
- grad_w_up: float32 [768, 2048], P('items', 'blk')
- grad_w_down: float32 [2048, 768], P('items', 'blk')
The draws below stay inside these ranges and needn't reach their ends.
Inputs may be any that keep to these rules, and one draw needn't show every extreme that they name: `grid`: for every plot height * width <= 1024 and 2 * height * width >= 1024; widths are (8) times 1, 2, 4 or 8; in every aligned group of 1 plots one has height * width = 1024.
All inputs are finite; a program needn't handle non-finite values.
Results may differ from the reference program's by a relative error of at most 0.02.
Values may be sent and summed in bfloat16 or wider, within the bound.
No kernel may reach another device: no remote copies, remote signals or barrier semaphores. Data moves between devices by JAX's collectives and lax.ppermute only.
A program may use at most 128 MiB of HBM per device.

```python
import jax
import jax.numpy as jnp
from jax import lax

D = 768
HEADS = 12
HEAD = 64
FF = 2048
LENGTH = 1024
ITEMS_DEV = 1
ITEMS = 16


def draw_grid(key, part):
    key = jax.random.fold_in(key, 7)
    key_power, key_cut, key_pick = jax.random.split(key, 3)
    power = jax.random.randint(key_power, (ITEMS,), 0, 4)
    factor = jnp.left_shift(jnp.ones((ITEMS,), jnp.int32), power)
    widths = LENGTH // 128 * factor
    tallest = 128 // factor
    cutting = jax.random.randint(key_cut, (ITEMS,), 0, 65536) % (tallest // 2 + 1)
    picked = jax.random.randint(key_pick, (ITEMS // ITEMS_DEV, 1), 0, ITEMS_DEV)
    slots = jnp.arange(ITEMS_DEV, dtype=jnp.int32)[None, :]
    chosen = (slots == picked).reshape(ITEMS)
    heights = jnp.where(chosen, tallest, tallest - cutting)
    return jnp.stack([heights, widths], -1).astype(jnp.int32)


def level_of(stream_key, dims, shards, least, largest):
    def one(dim, shards_of):
        steps = jax.random.uniform(jax.random.fold_in(jax.random.fold_in(stream_key, 6), dim), (shards_of,), jnp.float32, least / len(shards), largest / len(shards))
        return jnp.repeat(jnp.exp(steps), dims[dim] // shards_of).reshape((-1,) + (1,) * (len(dims) - dim - 1))

    level = one(*shards[0])
    for cut in shards[1:]:
        level = level * one(*cut)
    return level


def scatter_about(stream_key, extent, width, limit, cuts=(), held_as=jnp.bfloat16):
    entries = width * jax.random.normal(stream_key, extent, jnp.float32)
    if cuts:
        entries = entries * level_of(stream_key, extent, cuts, -0.22, 0.18)
    return jnp.clip(entries, -limit, limit).astype(held_as)


def setup_inputs(seed: int = 0) -> dict:
    key_list = jax.random.split(jax.random.key(seed), 13)
    return {
        "patches": scatter_about(key_list[0], (ITEMS, LENGTH, D), 1.0, 6.0, ((0, 16), (1, 2))),
        "grid": draw_grid(jax.random.fold_in(key_list[12], 71), 0),
        "norm_attn": jnp.clip(1.0 + 0.18 * jax.random.normal(key_list[2], (D,), jnp.float32), 0.1, 1.9),
        "w_query": scatter_about(key_list[3], (D, D), (D * 16) ** -0.5, 0.0546875, ((0, 16), (1, 2))),
        "w_key": scatter_about(key_list[4], (D, D), D ** -0.5, 0.21875, ((0, 16), (1, 2))),
        "w_value": scatter_about(key_list[5], (D, D), D ** -0.5, 0.21875, ((0, 16), (1, 2))),
        "w_out": scatter_about(key_list[6], (D, D), (D // 16) ** -0.5, 0.875, ((0, 16), (1, 2))),
        "norm_mlp": jnp.clip(1.0 + 0.18 * jax.random.normal(key_list[7], (D,), jnp.float32), 0.1, 1.9),
        "w_gate": scatter_about(key_list[8], (D, FF), D ** -0.5, 0.21875, ((0, 16), (1, 2))),
        "w_up": scatter_about(key_list[9], (D, FF), D ** -0.5, 0.21875, ((0, 16), (1, 2))),
        "w_down": scatter_about(key_list[10], (FF, D), FF ** -0.5, 0.125, ((0, 16), (1, 2))),
        "cotangent": scatter_about(key_list[11], (ITEMS, LENGTH, D), 1.0, 6.0, ((0, 16), (1, 2))),
    }


EPSILON = 1e-06

@jax.custom_vjp
def low(v):
    return lax.optimization_barrier(v.astype(jnp.bfloat16)).astype(jnp.float32)

@jax.custom_vjp
def low_back(v):
    return v

def low_keep(v):
    return (low(v), None)

def low_pass(kept, grad):
    return (grad,)

def back_keep(v):
    return (v, None)

def back_low(kept, grad):
    return (low(grad),)
low.defvjp(low_keep, low_pass)
low_back.defvjp(back_keep, back_low)

def matmul(left, right):
    return jnp.dot(left, right, precision=lax.Precision.HIGHEST, preferred_element_type=jnp.float32)

def rms_norm(values, gain):
    return values * lax.rsqrt(lax.optimization_barrier(jnp.mean(values * values, -1, keepdims=True)) + EPSILON) * gain

def block_layer(patch_rows, key_valid, norm_attn, w_query, w_key, w_value, w_out, norm_mlp, w_gate, w_up, w_down):
    normed = low(rms_norm(patch_rows, norm_attn))
    queries = low_back(low(matmul(normed, w_query))).reshape(LENGTH, HEADS, HEAD).transpose(1, 0, 2)
    key_rows = low_back(low(matmul(normed, w_key))).reshape(LENGTH, HEADS, HEAD).transpose(1, 0, 2)
    value_rows = low_back(low(matmul(normed, w_value))).reshape(LENGTH, HEADS, HEAD).transpose(1, 0, 2)

    def one_head(operands):
        head_queries, head_keys, head_values = operands
        scores = low_back(matmul(head_queries, head_keys.T))
        scores = jnp.where(key_valid[None, :], scores, -1000000000.0)
        shifted = jnp.exp(scores - lax.optimization_barrier(jnp.max(scores, -1, keepdims=True)))
        chances = shifted / lax.optimization_barrier(jnp.sum(shifted, -1, keepdims=True))
        return matmul(low(chances), head_values)
    heads_out = lax.map(jax.checkpoint(one_head), (queries, key_rows, value_rows))
    attended = low_back(low(heads_out.transpose(1, 0, 2).reshape(LENGTH, D)))
    middle = patch_rows + low_back(matmul(attended, w_out))
    normed_mlp = low(rms_norm(middle, norm_mlp))
    gate_in = low_back(matmul(normed_mlp, w_gate))
    upward = low_back(matmul(normed_mlp, w_up))
    hidden = low(jax.nn.gelu(gate_in, approximate=True) * upward)
    return middle + low_back(matmul(hidden, w_down))

def reference(patches, grid, norm_attn, w_query, w_key, w_value, w_out, norm_mlp, w_gate, w_up, w_down, cotangent):
    params = tuple((weight.astype(jnp.float32) for weight in (norm_attn, w_query, w_key, w_value, w_out, norm_mlp, w_gate, w_up, w_down)))
    positions = jnp.arange(LENGTH, dtype=jnp.int32)

    def per_item(totals, item_data):
        patch_rows, shape_pair, item_cot = item_data
        key_valid = positions < (shape_pair[0] * shape_pair[1]).astype(jnp.int32)

        def forward(rows_in, *weight_list):
            return block_layer(rows_in, key_valid, *weight_list)
        result, backward = jax.vjp(forward, patch_rows.astype(jnp.float32), *params)
        gradients = backward(item_cot.astype(jnp.float32))
        totals = tuple((prior + fresh for prior, fresh in zip(totals, gradients[1:])))
        return (totals, (result.astype(jnp.bfloat16), gradients[0].astype(jnp.bfloat16)))
    zeros_init = tuple((jnp.zeros_like(weight) for weight in params))
    totals, outputs = lax.scan(per_item, zeros_init, (patches, grid, cotangent))
    return (outputs[0], outputs[1], totals[0], totals[1], totals[2], totals[3], totals[4], totals[5], totals[6], totals[7], totals[8])
```

```python
import functools

import jax
import jax.numpy as jnp
from jax import lax
from jax.experimental import pallas as pl
from jax.experimental.pallas import tpu as pltpu
from jax.sharding import PartitionSpec as P

HEAD = 64


EPSILON = 1e-06


def rms_norm(values, gain):
    return values * lax.rsqrt(jnp.mean(values * values, -1, keepdims=True) + EPSILON) * gain


def product(formula, left, right):
    return jnp.einsum(formula, left, right, preferred_element_type=jnp.float32)


def masked_scores(query_heads, key_part, first_key, counts):
    scores = product("iqhd,ikhd->ihqk", query_heads, key_part)
    places = first_key + jnp.arange(key_part.shape[1], dtype=jnp.int32)
    allowed = places[None, :] < counts[:, None]
    return jnp.where(allowed[:, None, None, :], scores, -1000000000.0)


def general(
    patches,
    grid,
    norm_attn,
    w_query,
    w_key,
    w_value,
    w_out,
    norm_mlp,
    w_gate,
    w_up,
    w_down,
    cotangent,
):
    columns = (
        lax.all_gather(w_query, "blk", axis=1, tiled=True),
        lax.all_gather(w_key, "blk", axis=1, tiled=True),
        lax.all_gather(w_value, "blk", axis=1, tiled=True),
        lax.all_gather(w_out, "blk", axis=1, tiled=True),
        lax.all_gather(w_gate, "blk", axis=1, tiled=True),
        lax.all_gather(w_up, "blk", axis=1, tiled=True),
        lax.all_gather(w_down, "blk", axis=1, tiled=True),
    )
    full_query, full_key, full_value, full_out, full_gate, full_up, full_down = (
        lax.all_gather(columns[0], "items", axis=0, tiled=True),
        lax.all_gather(columns[1], "items", axis=0, tiled=True),
        lax.all_gather(columns[2], "items", axis=0, tiled=True),
        lax.all_gather(columns[3], "items", axis=0, tiled=True),
        lax.all_gather(columns[4], "items", axis=0, tiled=True),
        lax.all_gather(columns[5], "items", axis=0, tiled=True),
        lax.all_gather(columns[6], "items", axis=0, tiled=True),
    )
    items_here, row_count, model_width = patches.shape
    head_count = model_width // HEAD
    blocks = lax.axis_size("blk")
    counts = grid[:, 0] * grid[:, 1]
    patch_rows = patches.astype(jnp.float32)
    normed = rms_norm(patch_rows, norm_attn).astype(jnp.bfloat16)
    queries = product("ird,de->ire", normed, full_query).astype(jnp.bfloat16)
    key_rows = product("ird,de->ire", normed, full_key).astype(jnp.bfloat16)
    value_rows = product("ird,de->ire", normed, full_value).astype(jnp.bfloat16)
    query_heads = queries.reshape(items_here, row_count, head_count, HEAD)

    def split_part(piece, shard_index):
        part_rows = lax.dynamic_slice_in_dim(piece, shard_index * row_count, row_count, 1)
        return part_rows.reshape(items_here, row_count, head_count, HEAD)

    stat_shape = (items_here, head_count, row_count)
    start_stats = (jnp.full(stat_shape, -1e30, jnp.float32), jnp.zeros(stat_shape, jnp.float32))
    carried = start_stats
    key_piece = lax.all_gather(key_rows, "blk", axis=1, tiled=True)
    shards = key_piece.shape[1] // row_count

    def stats_one_shard(running, shard_index):
        running_max, running_sum = running
        key_part = split_part(key_piece, shard_index)
        scores = masked_scores(query_heads, key_part, shard_index * row_count, counts)
        new_max = jnp.maximum(running_max, jnp.max(scores, -1))
        new_sum = running_sum * jnp.exp(running_max - new_max) + jnp.sum(
            jnp.exp(scores - new_max[..., None]), -1
        )
        return ((new_max, new_sum), None)

    carried, unused = lax.scan(stats_one_shard, carried, jnp.arange(shards, dtype=jnp.int32))
    totals = carried
    log_total = totals[0] + jnp.log(totals[1])
    start_values = jnp.zeros((items_here, head_count, row_count, HEAD), jnp.float32)
    carried = start_values
    values_key_piece = lax.all_gather(key_rows, "blk", axis=1, tiled=True)
    value_piece = lax.all_gather(value_rows, "blk", axis=1, tiled=True)
    shards = values_key_piece.shape[1] // row_count

    def values_one_shard(accumulated, shard_index):
        key_part = split_part(values_key_piece, shard_index)
        value_part = split_part(value_piece, shard_index)
        scores = masked_scores(query_heads, key_part, shard_index * row_count, counts)
        weights_low = jnp.exp(scores - log_total[..., None]).astype(jnp.bfloat16)
        return (accumulated + product("ihqk,ikhd->ihqd", weights_low, value_part), None)

    carried, unused = lax.scan(values_one_shard, carried, jnp.arange(shards, dtype=jnp.int32))
    attended = carried.transpose(0, 2, 1, 3).reshape(items_here, row_count, model_width)
    attended_low = attended.astype(jnp.bfloat16)
    middle = patch_rows + product("ird,de->ire", attended_low, full_out)
    normed_mlp = rms_norm(middle, norm_mlp).astype(jnp.bfloat16)
    gate_in = product("ird,df->irf", normed_mlp, full_gate)
    upward = product("ird,df->irf", normed_mlp, full_up)
    activated = jax.nn.gelu(gate_in, approximate=True)
    hidden = (activated * upward).astype(jnp.bfloat16)
    output = (middle + product("irf,fd->ird", hidden, full_down)).astype(jnp.bfloat16)
    grad_down = product("irf,ird->fd", hidden, cotangent)
    grad_hidden = product("ird,fd->irf", cotangent, full_down)
    unused_gelu, gelu_back = jax.vjp(lambda inner: jax.nn.gelu(inner, approximate=True), gate_in)
    grad_gate_in = gelu_back(grad_hidden * upward)[0].astype(jnp.bfloat16)
    grad_upward = (grad_hidden * activated).astype(jnp.bfloat16)
    grad_gate = product("ird,irf->df", normed_mlp, grad_gate_in)
    grad_up = product("ird,irf->df", normed_mlp, grad_upward)
    grad_normed_mlp = product("irf,df->ird", grad_gate_in, full_gate) + product(
        "irf,df->ird", grad_upward, full_up
    )
    unused_norm, second_back = jax.vjp(rms_norm, middle, norm_mlp)
    grad_middle_part, grad_norm_mlp = second_back(grad_normed_mlp)
    grad_middle = cotangent.astype(jnp.float32) + grad_middle_part
    branch_grad = grad_middle.astype(jnp.bfloat16)
    grad_out = product("ird,ire->de", attended_low, branch_grad)
    grad_attended = product("ire,de->ird", branch_grad, full_out).astype(jnp.bfloat16)
    grad_heads = grad_attended.reshape(items_here, row_count, head_count, HEAD)
    delta = jnp.einsum(
        "iqhd,iqhd->ihq",
        grad_heads.astype(jnp.float32),
        attended.reshape(items_here, row_count, head_count, HEAD),
    )
    gathered_keys, gathered_values = (
        lax.all_gather(key_rows, "blk", axis=1, tiled=True),
        lax.all_gather(value_rows, "blk", axis=1, tiled=True),
    )
    query_start = jnp.zeros((items_here, row_count, head_count, HEAD), jnp.float32)

    def back_shard(grad_query, shard_index):
        key_part = split_part(gathered_keys, shard_index)
        value_part = split_part(gathered_values, shard_index)
        scores = masked_scores(query_heads, key_part, shard_index * row_count, counts)
        chances = jnp.exp(scores - log_total[..., None])
        grad_chances = product("iqhd,ikhd->ihqk", grad_heads, value_part)
        grad_scores = (chances * (grad_chances - delta[..., None])).astype(jnp.bfloat16)
        grad_query = grad_query + product("ihqk,ikhd->iqhd", grad_scores, key_part)
        key_term = product("ihqk,iqhd->ikhd", grad_scores, query_heads)
        value_term = product("ihqk,iqhd->ikhd", chances.astype(jnp.bfloat16), grad_heads)
        return (
            grad_query,
            (
                key_term.reshape(items_here, row_count, model_width),
                value_term.reshape(items_here, row_count, model_width),
            ),
        )

    grad_query, key_value_terms = lax.scan(
        back_shard, query_start, jnp.arange(blocks, dtype=jnp.int32)
    )
    key_sum, value_sum = (
        lax.psum_scatter(
            key_value_terms[0].astype(jnp.bfloat16), "blk", scatter_dimension=0, tiled=True
        ).astype(jnp.float32),
        lax.psum_scatter(
            key_value_terms[1].astype(jnp.bfloat16), "blk", scatter_dimension=0, tiled=True
        ).astype(jnp.float32),
    )
    grad_keys = key_sum[0].astype(jnp.bfloat16)
    grad_values = value_sum[0].astype(jnp.bfloat16)
    grad_queries = grad_query.reshape(items_here, row_count, model_width).astype(jnp.bfloat16)
    grad_wq = product("ird,ire->de", normed, grad_queries)
    grad_wk = product("ird,ire->de", normed, grad_keys)
    grad_wv = product("ird,ire->de", normed, grad_values)
    grad_normed = (
        product("ire,de->ird", grad_queries, full_query)
        + product("ire,de->ird", grad_keys, full_key)
        + product("ire,de->ird", grad_values, full_value)
    )
    unused_first, first_back = jax.vjp(rms_norm, patch_rows, norm_attn)
    grad_rows_part, grad_norm_attn = first_back(grad_normed)
    grad_patches = (grad_middle + grad_rows_part).astype(jnp.bfloat16)
    gain_total = lax.psum((grad_norm_attn, grad_norm_mlp), ("items", "blk"))
    by_rows = (
        lax.psum_scatter(
            grad_wq.astype(jnp.bfloat16), "items", scatter_dimension=0, tiled=True
        ).astype(jnp.float32),
        lax.psum_scatter(
            grad_wk.astype(jnp.bfloat16), "items", scatter_dimension=0, tiled=True
        ).astype(jnp.float32),
        lax.psum_scatter(
            grad_wv.astype(jnp.bfloat16), "items", scatter_dimension=0, tiled=True
        ).astype(jnp.float32),
        lax.psum_scatter(
            grad_out.astype(jnp.bfloat16), "items", scatter_dimension=0, tiled=True
        ).astype(jnp.float32),
        lax.psum_scatter(
            grad_gate.astype(jnp.bfloat16), "items", scatter_dimension=0, tiled=True
        ).astype(jnp.float32),
        lax.psum_scatter(
            grad_up.astype(jnp.bfloat16), "items", scatter_dimension=0, tiled=True
        ).astype(jnp.float32),
        lax.psum_scatter(
            grad_down.astype(jnp.bfloat16), "items", scatter_dimension=0, tiled=True
        ).astype(jnp.float32),
    )
    final_shards = (
        lax.psum_scatter(
            by_rows[0].astype(jnp.bfloat16), "blk", scatter_dimension=1, tiled=True
        ).astype(jnp.float32),
        lax.psum_scatter(
            by_rows[1].astype(jnp.bfloat16), "blk", scatter_dimension=1, tiled=True
        ).astype(jnp.float32),
        lax.psum_scatter(
            by_rows[2].astype(jnp.bfloat16), "blk", scatter_dimension=1, tiled=True
        ).astype(jnp.float32),
        lax.psum_scatter(
            by_rows[3].astype(jnp.bfloat16), "blk", scatter_dimension=1, tiled=True
        ).astype(jnp.float32),
        lax.psum_scatter(
            by_rows[4].astype(jnp.bfloat16), "blk", scatter_dimension=1, tiled=True
        ).astype(jnp.float32),
        lax.psum_scatter(
            by_rows[5].astype(jnp.bfloat16), "blk", scatter_dimension=1, tiled=True
        ).astype(jnp.float32),
        lax.psum_scatter(
            by_rows[6].astype(jnp.bfloat16), "blk", scatter_dimension=1, tiled=True
        ).astype(jnp.float32),
    )
    return (
        output,
        grad_patches,
        gain_total[0],
        final_shards[0],
        final_shards[1],
        final_shards[2],
        final_shards[3],
        gain_total[1],
        final_shards[4],
        final_shards[5],
        final_shards[6],
    )


def swap_items(values, items, bit):
    return lax.ppermute(values, "items", [(place, place ^ bit) for place in range(items)])


def swap_blocks(values):
    return lax.ppermute(values, "blk", [(0, 1), (1, 0)])


def join(own, other, axis, later):
    width = own.shape[axis]
    shape = list(own.shape)
    shape[axis] = 2 * width
    whole = jnp.zeros(shape, own.dtype)
    whole = lax.dynamic_update_slice_in_dim(whole, own, later * width, axis)
    return lax.dynamic_update_slice_in_dim(whole, other, (1 - later) * width, axis)


class Place:
    def __init__(self, items):
        self.items = items
        self.levels = items.bit_length() - 1
        self.index = lax.axis_index("items")
        self.block = lax.axis_index("blk")

    def bit(self, level):
        return (self.index >> (self.levels - 1 - level)) & 1

    def gather(self, shard, order):
        rows, columns = shard.shape
        whole = shard.reshape((1,) * self.levels + (rows, columns))
        for step in order:
            if step == "blk":
                whole = join(whole, swap_blocks(whole), self.levels + 1, self.block)
            else:
                other = swap_items(whole, self.items, 1 << (self.levels - 1 - step))
                whole = join(whole, other, step, self.bit(step))
        return whole.reshape(-1, whole.shape[-1])

    def scatter(self, whole, rows, order):
        part = whole.reshape((2,) * self.levels + (rows, whole.shape[-1]))
        for step in order:
            if step == "blk":
                axis, mine = self.levels + 1, self.block
            else:
                axis, mine = step, self.bit(step)
            width = part.shape[axis] // 2
            kept = lax.dynamic_slice_in_dim(part, mine * width, width, axis)
            sent = lax.dynamic_slice_in_dim(part, (1 - mine) * width, width, axis)
            if step == "blk":
                other = swap_blocks(sent)
            else:
                other = swap_items(sent, self.items, 1 << (self.levels - 1 - step))
            part = (kept.astype(jnp.float32) + other.astype(jnp.float32)).astype(jnp.bfloat16)
        return part.reshape(rows, -1).astype(jnp.float32)

    def total(self, values):
        for level in range(self.levels):
            values = values + swap_items(values, self.items, 1 << level)
        return values + swap_blocks(values)


def own_lanes(values, head):
    lanes = lax.broadcasted_iota(jnp.int32, values.shape, 1)
    return jnp.where(lanes // HEAD == head, values, jnp.zeros_like(values))


def dot_nt(left, right):
    return lax.dot_general(left, right, (((1,), (1,)), ((), ())), preferred_element_type=jnp.float32)


def dot_tn(left, right):
    return lax.dot_general(left, right, (((0,), (0,)), ((), ())), preferred_element_type=jnp.float32)


def dot_nn(left, right):
    return jnp.dot(left, right, preferred_element_type=jnp.float32)


def attend_kernel(count_ref, q_ref, k_ref, v_ref, out_ref):
    keys, values = k_ref[...], v_ref[...]
    places = lax.broadcasted_iota(jnp.int32, (1, keys.shape[0]), 1)
    bias = jnp.where(places < count_ref[0], 0.0, -1000000000.0)
    total = None
    for head in range(out_ref.shape[1] // HEAD):
        scores = dot_nt(own_lanes(q_ref[...], head), keys) + bias
        shifted = jnp.exp(scores - jnp.max(scores, -1, keepdims=True))
        inverse = 1.0 / jnp.sum(shifted, -1, keepdims=True)
        term = dot_nn((shifted * inverse).astype(jnp.bfloat16), values)
        total = term if total is None else jnp.where(
            lax.broadcasted_iota(jnp.int32, term.shape, 1) // HEAD == head, term, total
        )
    out_ref[...] = total.astype(jnp.bfloat16)


def attend(count, qkv, rows=256):
    length, width = qkv.shape[0], qkv.shape[1] // 3
    groups = width // 128
    return pl.pallas_call(
        attend_kernel,
        grid=(groups, length // rows),
        in_specs=[
            pl.BlockSpec(memory_space=pltpu.SMEM),
            pl.BlockSpec((rows, 128), lambda g, r: (r, g)),
            pl.BlockSpec((length, 128), lambda g, r: (0, groups + g)),
            pl.BlockSpec((length, 128), lambda g, r: (0, 2 * groups + g)),
        ],
        out_specs=pl.BlockSpec((rows, 128), lambda g, r: (r, g)),
        out_shape=jax.ShapeDtypeStruct((length, width), jnp.bfloat16),
        compiler_params=pltpu.CompilerParams(vmem_limit_bytes=40 << 20),
        name="attend",
    )(count, qkv, qkv, qkv)


def attend_back_kernel(count_ref, q_ref, k_ref, v_ref, grad_ref, dq_ref, dk_ref, dv_ref, dk_sum, dv_sum):
    keys, values = k_ref[...], v_ref[...]
    places = lax.broadcasted_iota(jnp.int32, (1, keys.shape[0]), 1)
    bias = jnp.where(places < count_ref[0], 0.0, -1000000000.0)
    grad_q = grad_k = grad_v = 0.0
    for head in range(dq_ref.shape[1] // HEAD):
        q_head = own_lanes(q_ref[...], head)
        grad_head = own_lanes(grad_ref[...], head)
        scores = dot_nt(q_head, keys) + bias
        shifted = jnp.exp(scores - jnp.max(scores, -1, keepdims=True))
        chances = shifted * (1.0 / jnp.sum(shifted, -1, keepdims=True))
        grad_chances = dot_nt(grad_head, values)
        weighed = chances * grad_chances
        grad_scores = (weighed - chances * jnp.sum(weighed, -1, keepdims=True)).astype(jnp.bfloat16)
        grad_q = grad_q + dot_nn(grad_scores, own_lanes(keys, head))
        grad_k = grad_k + dot_tn(grad_scores, q_head)
        grad_v = grad_v + dot_tn(chances.astype(jnp.bfloat16), grad_head)
    dq_ref[...] = grad_q.astype(jnp.bfloat16)

    @pl.when(pl.program_id(1) == 0)
    def _():
        dk_sum[...] = grad_k
        dv_sum[...] = grad_v

    @pl.when(pl.program_id(1) > 0)
    def _():
        dk_sum[...] += grad_k
        dv_sum[...] += grad_v

    @pl.when(pl.program_id(1) == pl.num_programs(1) - 1)
    def _():
        dk_ref[...] = dk_sum[...].astype(jnp.bfloat16)
        dv_ref[...] = dv_sum[...].astype(jnp.bfloat16)


def attend_back(count, qkv, grad, rows=256):
    length, width = grad.shape
    groups = width // 128
    shape = jax.ShapeDtypeStruct((length, width), jnp.bfloat16)
    return pl.pallas_call(
        attend_back_kernel,
        grid=(groups, length // rows),
        in_specs=[
            pl.BlockSpec(memory_space=pltpu.SMEM),
            pl.BlockSpec((rows, 128), lambda g, r: (r, g)),
            pl.BlockSpec((length, 128), lambda g, r: (0, groups + g)),
            pl.BlockSpec((length, 128), lambda g, r: (0, 2 * groups + g)),
            pl.BlockSpec((rows, 128), lambda g, r: (r, g)),
        ],
        out_specs=[
            pl.BlockSpec((rows, 128), lambda g, r: (r, g)),
            pl.BlockSpec((length, 128), lambda g, r: (0, g)),
            pl.BlockSpec((length, 128), lambda g, r: (0, g)),
        ],
        out_shape=[shape, shape, shape],
        scratch_shapes=[pltpu.VMEM((length, 128), jnp.float32), pltpu.VMEM((length, 128), jnp.float32)],
        compiler_params=pltpu.CompilerParams(vmem_limit_bytes=40 << 20),
        name="attend_back",
    )(count, qkv, qkv, qkv, grad)


def by_heads(
    items,
    patches,
    grid,
    norm_attn,
    w_query,
    w_key,
    w_value,
    w_out,
    norm_mlp,
    w_gate,
    w_up,
    w_down,
    cotangent,
):
    place = Place(items)
    levels, block = place.levels, place.block
    far = list(range(levels - 2))
    row_count, model_width = patches.shape[1:]
    length = 2 * row_count
    half = model_width // 2
    count = (grid[:, 0] * grid[:, 1]).astype(jnp.int32)
    own_rows, own_cot = patches[0], cotangent[0]
    shard_rows, down_rows = w_query.shape[0], w_down.shape[0]

    all_rows = join(own_rows, swap_blocks(own_rows), 0, block)
    attn_weights = place.gather(
        jnp.concatenate([w_query, w_key, w_value, w_out], 1), far + [levels - 2, levels - 1]
    )
    w_qkv, out_half = attn_weights[:, : 3 * half], attn_weights[:, 3 * half :]
    full_gate = place.gather(w_gate, far + ["blk", levels - 2, levels - 1])
    full_up = place.gather(w_up, far + [levels - 2, "blk", levels - 1])
    full_down = place.gather(w_down, ["blk"] + far + [levels - 2, levels - 1])
    full_out = join(out_half, swap_blocks(out_half), 1, block)

    all_normed = rms_norm(all_rows.astype(jnp.float32), norm_attn).astype(jnp.bfloat16)
    qkv = dot_nn(all_normed, w_qkv).astype(jnp.bfloat16)
    attended_heads = attend(count, qkv)

    def exchange_rows(values):
        kept = lax.dynamic_slice_in_dim(values, block * row_count, row_count, 0)
        sent = lax.dynamic_slice_in_dim(values, (1 - block) * row_count, row_count, 0)
        return join(kept, swap_blocks(sent), 1, block)

    def exchange_heads(values):
        kept = lax.dynamic_slice_in_dim(values, block * half, half, 1)
        sent = lax.dynamic_slice_in_dim(values, (1 - block) * half, half, 1)
        return join(kept, swap_blocks(sent), 0, block)

    attended = exchange_rows(attended_heads)
    patch_rows = own_rows.astype(jnp.float32)
    middle = patch_rows + dot_nn(attended, full_out)
    normed_mlp = rms_norm(middle, norm_mlp).astype(jnp.bfloat16)
    gate_in = dot_nn(normed_mlp, full_gate)
    upward = dot_nn(normed_mlp, full_up)
    activated = jax.nn.gelu(gate_in, approximate=True)
    hidden = (activated * upward).astype(jnp.bfloat16)
    output = (middle + dot_nn(hidden, full_down)).astype(jnp.bfloat16)
    grad_down = dot_tn(hidden, own_cot).astype(jnp.bfloat16)
    grad_hidden = dot_nt(own_cot, full_down)
    unused_gelu, gelu_back = jax.vjp(lambda inner: jax.nn.gelu(inner, approximate=True), gate_in)
    grad_gate_in = gelu_back(grad_hidden * upward)[0].astype(jnp.bfloat16)
    grad_upward = (grad_hidden * activated).astype(jnp.bfloat16)
    grad_gate = dot_tn(normed_mlp, grad_gate_in).astype(jnp.bfloat16)
    grad_up = dot_tn(normed_mlp, grad_upward).astype(jnp.bfloat16)
    grad_normed_mlp = dot_nt(grad_gate_in, full_gate) + dot_nt(grad_upward, full_up)
    unused_norm, second_back = jax.vjp(rms_norm, middle, norm_mlp)
    grad_middle_part, gain_mlp = second_back(grad_normed_mlp)
    grad_middle = own_cot.astype(jnp.float32) + grad_middle_part
    branch_grad = grad_middle.astype(jnp.bfloat16)
    grad_attended = dot_nt(branch_grad, full_out).astype(jnp.bfloat16)
    grad_out = dot_tn(attended, branch_grad).astype(jnp.bfloat16)
    grad_heads = exchange_heads(grad_attended)
    grad_qkv = jnp.concatenate(attend_back(count, qkv, grad_heads), 1)
    grad_w_qkv = dot_tn(all_normed, grad_qkv).astype(jnp.bfloat16)
    grad_all_normed = dot_nt(grad_qkv, w_qkv)
    kept = lax.dynamic_slice_in_dim(grad_all_normed, block * row_count, row_count, 0)
    sent = lax.dynamic_slice_in_dim(grad_all_normed, (1 - block) * row_count, row_count, 0)
    grad_normed = kept + swap_blocks(sent.astype(jnp.bfloat16)).astype(jnp.float32)
    unused_first, first_back = jax.vjp(rms_norm, patch_rows, norm_attn)
    grad_rows_part, gain_attn = first_back(grad_normed)
    grad_patches = (grad_middle + grad_rows_part).astype(jnp.bfloat16)

    near = far[::-1]
    shard_down = place.scatter(grad_down, down_rows, [levels - 1, levels - 2] + near + ["blk"])
    shard_gate = place.scatter(grad_gate, shard_rows, [levels - 1, levels - 2, "blk"] + near)
    shard_up = place.scatter(grad_up, shard_rows, [levels - 1, "blk", levels - 2] + near)
    shard_out = place.scatter(grad_out, shard_rows, [levels - 1, "blk", levels - 2] + near)
    shard_qkv = place.scatter(grad_w_qkv, shard_rows, [levels - 1, levels - 2] + near)
    gains = lax.psum((gain_attn, gain_mlp), ("items", "blk"))
    return (
        output[None],
        grad_patches[None],
        gains[0],
        shard_qkv[:, :half],
        shard_qkv[:, half : 2 * half],
        shard_qkv[:, 2 * half :],
        shard_out,
        gains[1],
        shard_gate,
        shard_up,
        shard_down,
    )


def local(items, blocks, patches, *rest):
    items_here, row_count, model_width = patches.shape
    fits = (
        blocks == 2
        and items_here == 1
        and items >= 8
        and items & (items - 1) == 0
        and row_count % 128 == 0
        and model_width % 256 == 0
    )
    if fits:
        return by_heads(items, patches, *rest)
    return general(patches, *rest)


def solution(mesh):
    placed = (
        P("items", "blk", None),
        P("items", None),
        P(),
        P("items", "blk"),
        P("items", "blk"),
        P("items", "blk"),
        P("items", "blk"),
        P(),
        P("items", "blk"),
        P("items", "blk"),
        P("items", "blk"),
        P("items", "blk", None),
    )
    return jax.shard_map(
        functools.partial(local, mesh.shape["items"], mesh.shape["blk"]),
        mesh=mesh,
        in_specs=placed,
        out_specs=(
            P("items", "blk", None),
            P("items", "blk", None),
            P(),
            P("items", "blk"),
            P("items", "blk"),
            P("items", "blk"),
            P("items", "blk"),
            P(),
            P("items", "blk"),
            P("items", "blk"),
            P("items", "blk"),
        ),
        check_vma=False,
    )
```

```python
import functools

import jax
import jax.numpy as jnp
from jax import lax
from jax.experimental import pallas as pl
from jax.experimental.pallas import tpu as pltpu
from jax.sharding import PartitionSpec as P

HEAD = 64


EPSILON = 1e-06


def rms_norm(values, gain):
    return values * lax.rsqrt(jnp.mean(values * values, -1, keepdims=True) + EPSILON) * gain


def product(formula, left, right):
    return jnp.einsum(formula, left, right, preferred_element_type=jnp.float32)


def masked_scores(query_heads, key_part, first_key, counts):
    scores = product("iqhd,ikhd->ihqk", query_heads, key_part)
    places = first_key + jnp.arange(key_part.shape[1], dtype=jnp.int32)
    allowed = places[None, :] < counts[:, None]
    return jnp.where(allowed[:, None, None, :], scores, -1000000000.0)


def general(
    patches,
    grid,
    norm_attn,
    w_query,
    w_key,
    w_value,
    w_out,
    norm_mlp,
    w_gate,
    w_up,
    w_down,
    cotangent,
):
    columns = (
        lax.all_gather(w_query, "blk", axis=1, tiled=True),
        lax.all_gather(w_key, "blk", axis=1, tiled=True),
        lax.all_gather(w_value, "blk", axis=1, tiled=True),
        lax.all_gather(w_out, "blk", axis=1, tiled=True),
        lax.all_gather(w_gate, "blk", axis=1, tiled=True),
        lax.all_gather(w_up, "blk", axis=1, tiled=True),
        lax.all_gather(w_down, "blk", axis=1, tiled=True),
    )
    full_query, full_key, full_value, full_out, full_gate, full_up, full_down = (
        lax.all_gather(columns[0], "items", axis=0, tiled=True),
        lax.all_gather(columns[1], "items", axis=0, tiled=True),
        lax.all_gather(columns[2], "items", axis=0, tiled=True),
        lax.all_gather(columns[3], "items", axis=0, tiled=True),
        lax.all_gather(columns[4], "items", axis=0, tiled=True),
        lax.all_gather(columns[5], "items", axis=0, tiled=True),
        lax.all_gather(columns[6], "items", axis=0, tiled=True),
    )
    items_here, row_count, model_width = patches.shape
    head_count = model_width // HEAD
    blocks = lax.axis_size("blk")
    counts = grid[:, 0] * grid[:, 1]
    patch_rows = patches.astype(jnp.float32)
    normed = rms_norm(patch_rows, norm_attn).astype(jnp.bfloat16)
    queries = product("ird,de->ire", normed, full_query).astype(jnp.bfloat16)
    key_rows = product("ird,de->ire", normed, full_key).astype(jnp.bfloat16)
    value_rows = product("ird,de->ire", normed, full_value).astype(jnp.bfloat16)
    query_heads = queries.reshape(items_here, row_count, head_count, HEAD)

    def split_part(piece, shard_index):
        part_rows = lax.dynamic_slice_in_dim(piece, shard_index * row_count, row_count, 1)
        return part_rows.reshape(items_here, row_count, head_count, HEAD)

    stat_shape = (items_here, head_count, row_count)
    start_stats = (jnp.full(stat_shape, -1e30, jnp.float32), jnp.zeros(stat_shape, jnp.float32))
    carried = start_stats
    key_piece = lax.all_gather(key_rows, "blk", axis=1, tiled=True)
    shards = key_piece.shape[1] // row_count

    def stats_one_shard(running, shard_index):
        running_max, running_sum = running
        key_part = split_part(key_piece, shard_index)
        scores = masked_scores(query_heads, key_part, shard_index * row_count, counts)
        new_max = jnp.maximum(running_max, jnp.max(scores, -1))
        new_sum = running_sum * jnp.exp(running_max - new_max) + jnp.sum(
            jnp.exp(scores - new_max[..., None]), -1
        )
        return ((new_max, new_sum), None)

    carried, unused = lax.scan(stats_one_shard, carried, jnp.arange(shards, dtype=jnp.int32))
    totals = carried
    log_total = totals[0] + jnp.log(totals[1])
    start_values = jnp.zeros((items_here, head_count, row_count, HEAD), jnp.float32)
    carried = start_values
    values_key_piece = lax.all_gather(key_rows, "blk", axis=1, tiled=True)
    value_piece = lax.all_gather(value_rows, "blk", axis=1, tiled=True)
    shards = values_key_piece.shape[1] // row_count

    def values_one_shard(accumulated, shard_index):
        key_part = split_part(values_key_piece, shard_index)
        value_part = split_part(value_piece, shard_index)
        scores = masked_scores(query_heads, key_part, shard_index * row_count, counts)
        weights_low = jnp.exp(scores - log_total[..., None]).astype(jnp.bfloat16)
        return (accumulated + product("ihqk,ikhd->ihqd", weights_low, value_part), None)

    carried, unused = lax.scan(values_one_shard, carried, jnp.arange(shards, dtype=jnp.int32))
    attended = carried.transpose(0, 2, 1, 3).reshape(items_here, row_count, model_width)
    attended_low = attended.astype(jnp.bfloat16)
    middle = patch_rows + product("ird,de->ire", attended_low, full_out)
    normed_mlp = rms_norm(middle, norm_mlp).astype(jnp.bfloat16)
    gate_in = product("ird,df->irf", normed_mlp, full_gate)
    upward = product("ird,df->irf", normed_mlp, full_up)
    activated = jax.nn.gelu(gate_in, approximate=True)
    hidden = (activated * upward).astype(jnp.bfloat16)
    output = (middle + product("irf,fd->ird", hidden, full_down)).astype(jnp.bfloat16)
    grad_down = product("irf,ird->fd", hidden, cotangent)
    grad_hidden = product("ird,fd->irf", cotangent, full_down)
    unused_gelu, gelu_back = jax.vjp(lambda inner: jax.nn.gelu(inner, approximate=True), gate_in)
    grad_gate_in = gelu_back(grad_hidden * upward)[0].astype(jnp.bfloat16)
    grad_upward = (grad_hidden * activated).astype(jnp.bfloat16)
    grad_gate = product("ird,irf->df", normed_mlp, grad_gate_in)
    grad_up = product("ird,irf->df", normed_mlp, grad_upward)
    grad_normed_mlp = product("irf,df->ird", grad_gate_in, full_gate) + product(
        "irf,df->ird", grad_upward, full_up
    )
    unused_norm, second_back = jax.vjp(rms_norm, middle, norm_mlp)
    grad_middle_part, grad_norm_mlp = second_back(grad_normed_mlp)
    grad_middle = cotangent.astype(jnp.float32) + grad_middle_part
    branch_grad = grad_middle.astype(jnp.bfloat16)
    grad_out = product("ird,ire->de", attended_low, branch_grad)
    grad_attended = product("ire,de->ird", branch_grad, full_out).astype(jnp.bfloat16)
    grad_heads = grad_attended.reshape(items_here, row_count, head_count, HEAD)
    delta = jnp.einsum(
        "iqhd,iqhd->ihq",
        grad_heads.astype(jnp.float32),
        attended.reshape(items_here, row_count, head_count, HEAD),
    )
    gathered_keys, gathered_values = (
        lax.all_gather(key_rows, "blk", axis=1, tiled=True),
        lax.all_gather(value_rows, "blk", axis=1, tiled=True),
    )
    query_start = jnp.zeros((items_here, row_count, head_count, HEAD), jnp.float32)

    def back_shard(grad_query, shard_index):
        key_part = split_part(gathered_keys, shard_index)
        value_part = split_part(gathered_values, shard_index)
        scores = masked_scores(query_heads, key_part, shard_index * row_count, counts)
        chances = jnp.exp(scores - log_total[..., None])
        grad_chances = product("iqhd,ikhd->ihqk", grad_heads, value_part)
        grad_scores = (chances * (grad_chances - delta[..., None])).astype(jnp.bfloat16)
        grad_query = grad_query + product("ihqk,ikhd->iqhd", grad_scores, key_part)
        key_term = product("ihqk,iqhd->ikhd", grad_scores, query_heads)
        value_term = product("ihqk,iqhd->ikhd", chances.astype(jnp.bfloat16), grad_heads)
        return (
            grad_query,
            (
                key_term.reshape(items_here, row_count, model_width),
                value_term.reshape(items_here, row_count, model_width),
            ),
        )

    grad_query, key_value_terms = lax.scan(
        back_shard, query_start, jnp.arange(blocks, dtype=jnp.int32)
    )
    key_sum, value_sum = (
        lax.psum_scatter(
            key_value_terms[0].astype(jnp.bfloat16), "blk", scatter_dimension=0, tiled=True
        ).astype(jnp.float32),
        lax.psum_scatter(
            key_value_terms[1].astype(jnp.bfloat16), "blk", scatter_dimension=0, tiled=True
        ).astype(jnp.float32),
    )
    grad_keys = key_sum[0].astype(jnp.bfloat16)
    grad_values = value_sum[0].astype(jnp.bfloat16)
    grad_queries = grad_query.reshape(items_here, row_count, model_width).astype(jnp.bfloat16)
    grad_wq = product("ird,ire->de", normed, grad_queries)
    grad_wk = product("ird,ire->de", normed, grad_keys)
    grad_wv = product("ird,ire->de", normed, grad_values)
    grad_normed = (
        product("ire,de->ird", grad_queries, full_query)
        + product("ire,de->ird", grad_keys, full_key)
        + product("ire,de->ird", grad_values, full_value)
    )
    unused_first, first_back = jax.vjp(rms_norm, patch_rows, norm_attn)
    grad_rows_part, grad_norm_attn = first_back(grad_normed)
    grad_patches = (grad_middle + grad_rows_part).astype(jnp.bfloat16)
    gain_total = lax.psum((grad_norm_attn, grad_norm_mlp), ("items", "blk"))
    by_rows = (
        lax.psum_scatter(
            grad_wq.astype(jnp.bfloat16), "items", scatter_dimension=0, tiled=True
        ).astype(jnp.float32),
        lax.psum_scatter(
            grad_wk.astype(jnp.bfloat16), "items", scatter_dimension=0, tiled=True
        ).astype(jnp.float32),
        lax.psum_scatter(
            grad_wv.astype(jnp.bfloat16), "items", scatter_dimension=0, tiled=True
        ).astype(jnp.float32),
        lax.psum_scatter(
            grad_out.astype(jnp.bfloat16), "items", scatter_dimension=0, tiled=True
        ).astype(jnp.float32),
        lax.psum_scatter(
            grad_gate.astype(jnp.bfloat16), "items", scatter_dimension=0, tiled=True
        ).astype(jnp.float32),
        lax.psum_scatter(
            grad_up.astype(jnp.bfloat16), "items", scatter_dimension=0, tiled=True
        ).astype(jnp.float32),
        lax.psum_scatter(
            grad_down.astype(jnp.bfloat16), "items", scatter_dimension=0, tiled=True
        ).astype(jnp.float32),
    )
    final_shards = (
        lax.psum_scatter(
            by_rows[0].astype(jnp.bfloat16), "blk", scatter_dimension=1, tiled=True
        ).astype(jnp.float32),
        lax.psum_scatter(
            by_rows[1].astype(jnp.bfloat16), "blk", scatter_dimension=1, tiled=True
        ).astype(jnp.float32),
        lax.psum_scatter(
            by_rows[2].astype(jnp.bfloat16), "blk", scatter_dimension=1, tiled=True
        ).astype(jnp.float32),
        lax.psum_scatter(
            by_rows[3].astype(jnp.bfloat16), "blk", scatter_dimension=1, tiled=True
        ).astype(jnp.float32),
        lax.psum_scatter(
            by_rows[4].astype(jnp.bfloat16), "blk", scatter_dimension=1, tiled=True
        ).astype(jnp.float32),
        lax.psum_scatter(
            by_rows[5].astype(jnp.bfloat16), "blk", scatter_dimension=1, tiled=True
        ).astype(jnp.float32),
        lax.psum_scatter(
            by_rows[6].astype(jnp.bfloat16), "blk", scatter_dimension=1, tiled=True
        ).astype(jnp.float32),
    )
    return (
        output,
        grad_patches,
        gain_total[0],
        final_shards[0],
        final_shards[1],
        final_shards[2],
        final_shards[3],
        gain_total[1],
        final_shards[4],
        final_shards[5],
        final_shards[6],
    )


def swap_items(values, items, bit):
    return lax.ppermute(values, "items", [(place, place ^ bit) for place in range(items)])


def swap_blocks(values):
    return lax.ppermute(values, "blk", [(0, 1), (1, 0)])


def join(own, other, axis, later):
    width = own.shape[axis]
    shape = list(own.shape)
    shape[axis] = 2 * width
    whole = jnp.zeros(shape, own.dtype)
    whole = lax.dynamic_update_slice_in_dim(whole, own, later * width, axis)
    return lax.dynamic_update_slice_in_dim(whole, other, (1 - later) * width, axis)


def add(kept, other):
    return (kept.astype(jnp.float32) + other.astype(jnp.float32)).astype(jnp.bfloat16)


def after(*values):
    return lax.optimization_barrier(values)


class Place:
    def __init__(self, items):
        self.items = items
        self.levels = items.bit_length() - 1
        self.index = lax.axis_index("items")
        self.block = lax.axis_index("blk")

    def bit(self, level):
        return (self.index >> (self.levels - 1 - level)) & 1

    def shaped(self, shard):
        return shard.reshape((1,) * self.levels + shard.shape)

    def flat(self, whole):
        return whole.reshape(-1, whole.shape[-1])

    def send(self, whole, step):
        if step == "blk":
            return swap_blocks(whole)
        return swap_items(whole, self.items, 1 << (self.levels - 1 - step))

    def meet(self, whole, other, step):
        if step == "blk":
            return join(whole, other, self.levels + 1, self.block)
        return join(whole, other, step, self.bit(step))

    def gather(self, whole, order):
        for step in order:
            whole = self.meet(whole, self.send(whole, step), step)
        return whole

    def part_of(self, whole, rows):
        return whole.reshape((2,) * self.levels + (rows, whole.shape[-1]))

    def halves(self, part, step):
        axis, mine = (self.levels + 1, self.block) if step == "blk" else (step, self.bit(step))
        width = part.shape[axis] // 2
        kept = lax.dynamic_slice_in_dim(part, mine * width, width, axis)
        sent = lax.dynamic_slice_in_dim(part, (1 - mine) * width, width, axis)
        return kept, self.send(sent, step)

    def scatter(self, part, order):
        for step in order:
            part = add(*self.halves(part, step))
        return part


def own_lanes(values, head):
    lanes = lax.broadcasted_iota(jnp.int32, values.shape, 1)
    return jnp.where(lanes // HEAD == head, values, jnp.zeros_like(values))


def dot_nt(left, right):
    return lax.dot_general(left, right, (((1,), (1,)), ((), ())), preferred_element_type=jnp.float32)


def dot_tn(left, right):
    return lax.dot_general(left, right, (((0,), (0,)), ((), ())), preferred_element_type=jnp.float32)


def dot_nn(left, right):
    return jnp.dot(left, right, preferred_element_type=jnp.float32)


def attend_kernel(count_ref, q_ref, k_ref, v_ref, out_ref):
    keys, values = k_ref[...], v_ref[...]
    places = lax.broadcasted_iota(jnp.int32, (1, keys.shape[0]), 1)
    bias = jnp.where(places < count_ref[0], 0.0, -1000000000.0)
    total = None
    for head in range(out_ref.shape[1] // HEAD):
        scores = dot_nt(own_lanes(q_ref[...], head), keys) + bias
        shifted = jnp.exp(scores - jnp.max(scores, -1, keepdims=True))
        inverse = 1.0 / jnp.sum(shifted, -1, keepdims=True)
        term = dot_nn((shifted * inverse).astype(jnp.bfloat16), values)
        total = term if total is None else jnp.where(
            lax.broadcasted_iota(jnp.int32, term.shape, 1) // HEAD == head, term, total
        )
    out_ref[...] = total.astype(jnp.bfloat16)


def attend(count, qkv, first, some, rows=256):
    length, groups = qkv.shape[0], qkv.shape[1] // 384
    width = some * 128
    return pl.pallas_call(
        attend_kernel,
        grid=(some, length // rows),
        in_specs=[
            pl.BlockSpec(memory_space=pltpu.SMEM),
            pl.BlockSpec((rows, 128), lambda g, r: (r, first + g)),
            pl.BlockSpec((length, 128), lambda g, r: (0, groups + first + g)),
            pl.BlockSpec((length, 128), lambda g, r: (0, 2 * groups + first + g)),
        ],
        out_specs=pl.BlockSpec((rows, 128), lambda g, r: (r, g)),
        out_shape=jax.ShapeDtypeStruct((length, width), jnp.bfloat16),
        compiler_params=pltpu.CompilerParams(vmem_limit_bytes=16 << 20),
        cost_estimate=pl.CostEstimate(flops=16 * length * length * width, bytes_accessed=8 * length * width, transcendentals=length * length * width // HEAD),
        name="attend",
    )(count, qkv, qkv, qkv)


def attend_back_kernel(count_ref, q_ref, k_ref, v_ref, grad_ref, dq_ref, dk_ref, dv_ref, dk_sum, dv_sum):
    keys, values = k_ref[...], v_ref[...]
    places = lax.broadcasted_iota(jnp.int32, (1, keys.shape[0]), 1)
    bias = jnp.where(places < count_ref[0], 0.0, -1000000000.0)
    grad_q = grad_k = grad_v = 0.0
    for head in range(dq_ref.shape[1] // HEAD):
        q_head = own_lanes(q_ref[...], head)
        grad_head = own_lanes(grad_ref[...], head)
        scores = dot_nt(q_head, keys) + bias
        shifted = jnp.exp(scores - jnp.max(scores, -1, keepdims=True))
        chances = shifted * (1.0 / jnp.sum(shifted, -1, keepdims=True))
        grad_chances = dot_nt(grad_head, values)
        weighed = chances * grad_chances
        grad_scores = (weighed - chances * jnp.sum(weighed, -1, keepdims=True)).astype(jnp.bfloat16)
        grad_q = grad_q + dot_nn(grad_scores, own_lanes(keys, head))
        grad_k = grad_k + dot_tn(grad_scores, q_head)
        grad_v = grad_v + dot_tn(chances.astype(jnp.bfloat16), grad_head)
    dq_ref[...] = grad_q.astype(jnp.bfloat16)

    @pl.when(pl.program_id(1) == 0)
    def _():
        dk_sum[...] = grad_k
        dv_sum[...] = grad_v

    @pl.when(pl.program_id(1) > 0)
    def _():
        dk_sum[...] += grad_k
        dv_sum[...] += grad_v

    @pl.when(pl.program_id(1) == pl.num_programs(1) - 1)
    def _():
        dk_ref[...] = dk_sum[...].astype(jnp.bfloat16)
        dv_ref[...] = dv_sum[...].astype(jnp.bfloat16)


def attend_back(count, qkv, grad, group, rows=256):
    length, groups = qkv.shape[0], qkv.shape[1] // 384
    shape = jax.ShapeDtypeStruct((length, 128), jnp.bfloat16)
    return pl.pallas_call(
        attend_back_kernel,
        grid=(1, length // rows),
        in_specs=[
            pl.BlockSpec(memory_space=pltpu.SMEM),
            pl.BlockSpec((rows, 128), lambda g, r: (r, group)),
            pl.BlockSpec((length, 128), lambda g, r: (0, groups + group)),
            pl.BlockSpec((length, 128), lambda g, r: (0, 2 * groups + group)),
            pl.BlockSpec((rows, 128), lambda g, r: (r, group)),
        ],
        out_specs=[
            pl.BlockSpec((rows, 128), lambda g, r: (r, 0)),
            pl.BlockSpec((length, 128), lambda g, r: (0, 0)),
            pl.BlockSpec((length, 128), lambda g, r: (0, 0)),
        ],
        out_shape=[shape, shape, shape],
        scratch_shapes=[pltpu.VMEM((length, 128), jnp.float32), pltpu.VMEM((length, 128), jnp.float32)],
        compiler_params=pltpu.CompilerParams(vmem_limit_bytes=16 << 20),
        cost_estimate=pl.CostEstimate(flops=5000 * length * length, bytes_accessed=14 * length * 128, transcendentals=2 * length * length),
        name="attend_back",
    )(count, qkv, qkv, qkv, grad)


def by_heads(
    items,
    patches,
    grid,
    norm_attn,
    w_query,
    w_key,
    w_value,
    w_out,
    norm_mlp,
    w_gate,
    w_up,
    w_down,
    cotangent,
):
    place = Place(items)
    levels, block = place.levels, place.block
    far = list(range(levels - 2))
    row_count, model_width = patches.shape[1:]
    length = 2 * row_count
    half = model_width // 2
    count = (grid[:, 0] * grid[:, 1]).astype(jnp.int32)
    own_rows, own_cot = patches[0], cotangent[0]
    shard_rows, down_rows = w_query.shape[0], w_down.shape[0]

    y, core = levels - 2, levels - 1
    groups = half // 128
    other_rows = swap_blocks(own_rows)
    w_qkv = place.shaped(jnp.concatenate([w_query, w_key, w_value], 1))
    gate, up, down, out = [place.shaped(shard) for shard in (w_gate, w_up, w_down, w_out)]

    def advance(held, steps):
        moved = [whole if step is None else place.send(whole, step) for whole, step in zip(held, steps)]
        moved = after(*moved)
        return [
            other if step is None else place.meet(whole, other, step)
            for whole, other, step in zip(held, moved, steps)
        ]

    w_qkv, down = advance([w_qkv, down], [far[0], "blk"])
    w_qkv, gate, up, down = advance([w_qkv, gate, up, down], [far[1], far[0], far[0], y])
    w_qkv, gate, up, out, down = advance([w_qkv, gate, up, out, down], [y, far[1], far[1], far[0], None])
    for step in far[2:]:
        w_qkv, gate, up = advance([w_qkv, gate, up], [step] * 3)
    w_qkv, out, down = advance([w_qkv, out, down], [core, far[1], None])
    w_qkv = place.flat(w_qkv)

    sent = place.send(gate, "blk"), place.send(up, y), place.send(down, far[0]), place.send(out, "blk")
    all_rows = join(own_rows, other_rows, 0, block)
    all_normed = rms_norm(all_rows.astype(jnp.float32), norm_attn).astype(jnp.bfloat16)
    qkv = dot_nn(all_normed, w_qkv).astype(jnp.bfloat16)
    early = attend(count, qkv, 0, groups - 1)
    early, qkv_late, sent = after(early, qkv, sent)
    gate = place.meet(gate, sent[0], "blk")
    up = place.meet(up, sent[1], y)
    down = place.meet(down, sent[2], far[0])
    out = place.meet(out, sent[3], "blk")

    def exchange_rows(values):
        kept = lax.dynamic_slice_in_dim(values, block * row_count, row_count, 0)
        sent = lax.dynamic_slice_in_dim(values, (1 - block) * row_count, row_count, 0)
        return kept, swap_blocks(sent)

    early_kept, early_other = exchange_rows(early)
    sent = place.send(out, y), place.send(gate, y), place.send(down, far[1])
    late = attend(count, qkv_late, groups - 1, 1)
    early_other, up = after(early_other, up)
    sent += (place.send(up, "blk"),)
    late_kept, late_other = exchange_rows(late)
    late_other, sent = after(late_other, sent)
    out = place.meet(out, sent[0], y)
    gate = place.meet(gate, sent[1], y)
    down = place.meet(down, sent[2], far[1])
    up = place.meet(up, sent[3], "blk")
    out, gate, up, down = [place.gather(whole, far[2:]) for whole in (out, gate, up, down)]
    full_out = place.flat(place.gather(out, [core]))
    full_gate = place.flat(place.gather(gate, [core]))
    full_up = place.flat(place.gather(up, [core]))
    full_down = place.flat(place.gather(down, [core]))
    attended = join(
        jnp.concatenate([early_kept, late_kept], 1), jnp.concatenate([early_other, late_other], 1), 1, block
    )
    near = far[::-1]
    patch_rows = own_rows.astype(jnp.float32)
    middle = patch_rows + dot_nn(attended, full_out)
    normed_mlp = rms_norm(middle, norm_mlp).astype(jnp.bfloat16)
    gate_in = dot_nn(normed_mlp, full_gate)
    upward = dot_nn(normed_mlp, full_up)
    activated = jax.nn.gelu(gate_in, approximate=True)
    hidden = (activated * upward).astype(jnp.bfloat16)
    output = (middle + dot_nn(hidden, full_down)).astype(jnp.bfloat16)
    grad_down = dot_tn(hidden, own_cot).astype(jnp.bfloat16)
    moving = place.halves(place.part_of(grad_down, down_rows), core)
    grad_hidden = dot_nt(own_cot, full_down)
    unused_gelu, gelu_back = jax.vjp(lambda inner: jax.nn.gelu(inner, approximate=True), gate_in)
    grad_gate_in = gelu_back(grad_hidden * upward)[0].astype(jnp.bfloat16)
    grad_upward = (grad_hidden * activated).astype(jnp.bfloat16)
    grad_normed_mlp = dot_nt(grad_gate_in, full_gate) + dot_nt(grad_upward, full_up)
    grad_normed_mlp, moving = after(grad_normed_mlp, moving)
    moving = place.halves(add(*moving), near[0])
    unused_norm, second_back = jax.vjp(rms_norm, middle, norm_mlp)
    grad_middle_part, gain_mlp = second_back(grad_normed_mlp)
    grad_middle = own_cot.astype(jnp.float32) + grad_middle_part
    branch_grad = grad_middle.astype(jnp.bfloat16)
    grad_attended = dot_nt(branch_grad, full_out).astype(jnp.bfloat16)
    heads_kept = lax.dynamic_slice_in_dim(grad_attended, block * half, half, 1)
    heads_sent = lax.dynamic_slice_in_dim(grad_attended, (1 - block) * half, half, 1)
    heads_other = swap_blocks(heads_sent)
    normed_mlp, attended, heads_sent = after(normed_mlp, attended, heads_sent)
    grad_gate = dot_tn(normed_mlp, grad_gate_in).astype(jnp.bfloat16)
    grad_up = dot_tn(normed_mlp, grad_upward).astype(jnp.bfloat16)
    grad_out = dot_tn(attended, branch_grad).astype(jnp.bfloat16)
    cores = [place.halves(place.part_of(grad, shard_rows), core) for grad in (grad_gate, grad_up, grad_out)]
    heads_other, grad_gate, grad_up, grad_out = after(heads_other, grad_gate, grad_up, grad_out)
    grad_heads = join(heads_kept, heads_other, 0, block)
    part_gate, part_up, part_out = [add(*pair) for pair in cores]

    wide = place.halves(part_gate, y), place.halves(part_up, "blk")
    backs = attend_back(count, qkv, grad_heads, 0)
    backs, grad_heads, moving = after(backs, grad_heads, moving)
    backs = [backs]
    moving = place.halves(add(*moving), near[1])
    for group in range(1, groups - 1):
        backs.append(attend_back(count, qkv, grad_heads, group))
    backs, grad_heads, wide = after(backs, grad_heads, wide)
    part_gate, part_up = [add(*pair) for pair in wide]
    wide = place.halves(part_gate, "blk"), place.halves(part_up, y), place.halves(part_out, y)
    last = attend_back(count, qkv, grad_heads, groups - 1)
    last, wide, moving = after(last, wide, moving)
    backs = backs + [last]
    part_gate, part_up, part_out = [add(*pair) for pair in wide]
    part_down = add(*moving)
    part_gate = jnp.concatenate([part_gate, part_up], -1)

    grad_qkv = jnp.concatenate([back[kind] for kind in range(3) for back in backs], 1)
    grad_all_normed = dot_nt(grad_qkv, w_qkv)
    unused_all, gain_back = jax.vjp(lambda gain: rms_norm(all_rows.astype(jnp.float32), gain), norm_attn)
    gains = jnp.stack([gain_back(grad_all_normed)[0], gain_mlp])
    gains = gains + swap_blocks(gains)
    rows_kept = lax.dynamic_slice_in_dim(grad_all_normed, block * row_count, row_count, 0)
    rows_sent = lax.dynamic_slice_in_dim(grad_all_normed, (1 - block) * row_count, row_count, 0)
    rows_sent, gains = after(rows_sent.astype(jnp.bfloat16), gains)
    rows_other = swap_blocks(rows_sent)
    grad_w_qkv = dot_tn(all_normed, grad_qkv).astype(jnp.bfloat16)
    moving = place.halves(place.part_of(grad_w_qkv, shard_rows), core)
    other_gains = place.send(gains, core)
    moving, other_gains = after(moving, other_gains)
    part_qkv, gains = add(*moving), gains + other_gains

    moving = place.halves(part_qkv, y), place.halves(part_gate, near[0])
    other_gains = place.send(gains, y)
    rows_other, moving, other_gains = after(rows_other, moving, other_gains)
    part_qkv, part_gate = [add(*pair) for pair in moving]
    gains = gains + other_gains

    moving = place.halves(part_qkv, near[0]), place.halves(part_gate, near[1]), place.halves(part_out, "blk"), place.halves(part_down, y)
    other_gains = place.send(gains, near[0])
    moving, other_gains = after(moving, other_gains)
    part_qkv, part_gate, part_out, part_down = [add(*pair) for pair in moving]
    gains = gains + other_gains
    for step in near[1:]:
        gains = gains + place.send(gains, step)

    grad_normed = rows_kept + rows_other.astype(jnp.float32)
    unused_first, first_back = jax.vjp(rms_norm, patch_rows, norm_attn)
    grad_rows_part, unused_gain = first_back(grad_normed)
    grad_patches = (grad_middle + grad_rows_part).astype(jnp.bfloat16)

    shard_qkv = place.scatter(part_qkv, near[1:]).reshape(shard_rows, -1).astype(jnp.float32)
    shard_down = place.scatter(part_down, ["blk"] + near[2:]).reshape(down_rows, half).astype(jnp.float32)
    shard_out = place.scatter(part_out, near).reshape(shard_rows, half).astype(jnp.float32)
    shard_gate = place.scatter(part_gate, near[2:]).reshape(shard_rows, -1).astype(jnp.float32)
    inner = shard_gate.shape[1] // 2
    return (
        output[None],
        grad_patches[None],
        gains[0],
        shard_qkv[:, :half],
        shard_qkv[:, half : 2 * half],
        shard_qkv[:, 2 * half :],
        shard_out,
        gains[1],
        shard_gate[:, :inner],
        shard_gate[:, inner:],
        shard_down,
    )


def local(items, blocks, patches, *rest):
    items_here, row_count, model_width = patches.shape
    fits = (
        blocks == 2
        and items_here == 1
        and items >= 8
        and items & (items - 1) == 0
        and row_count % 128 == 0
        and model_width % 256 == 0
    )
    if fits:
        return by_heads(items, patches, *rest)
    return general(patches, *rest)


def solution(mesh):
    placed = (
        P("items", "blk", None),
        P("items", None),
        P(),
        P("items", "blk"),
        P("items", "blk"),
        P("items", "blk"),
        P("items", "blk"),
        P(),
        P("items", "blk"),
        P("items", "blk"),
        P("items", "blk"),
        P("items", "blk", None),
    )
    return jax.shard_map(
        functools.partial(local, mesh.shape["items"], mesh.shape["blk"]),
        mesh=mesh,
        in_specs=placed,
        out_specs=(
            P("items", "blk", None),
            P("items", "blk", None),
            P(),
            P("items", "blk"),
            P("items", "blk"),
            P("items", "blk"),
            P("items", "blk"),
            P(),
            P("items", "blk"),
            P("items", "blk"),
            P("items", "blk"),
        ),
        check_vma=False,
    )
```

```python
import functools

import jax
import jax.numpy as jnp
from jax import lax
from jax.experimental import pallas as pl
from jax.experimental.pallas import tpu as pltpu
from jax.sharding import PartitionSpec as P

HEAD = 64


EPSILON = 1e-06


def rms_norm(values, gain):
    return values * lax.rsqrt(jnp.mean(values * values, -1, keepdims=True) + EPSILON) * gain


def product(formula, left, right):
    return jnp.einsum(formula, left, right, preferred_element_type=jnp.float32)


def masked_scores(query_heads, key_part, first_key, counts):
    scores = product("iqhd,ikhd->ihqk", query_heads, key_part)
    places = first_key + jnp.arange(key_part.shape[1], dtype=jnp.int32)
    allowed = places[None, :] < counts[:, None]
    return jnp.where(allowed[:, None, None, :], scores, -1000000000.0)


def general(
    patches,
    grid,
    norm_attn,
    w_query,
    w_key,
    w_value,
    w_out,
    norm_mlp,
    w_gate,
    w_up,
    w_down,
    cotangent,
):
    columns = (
        lax.all_gather(w_query, "blk", axis=1, tiled=True),
        lax.all_gather(w_key, "blk", axis=1, tiled=True),
        lax.all_gather(w_value, "blk", axis=1, tiled=True),
        lax.all_gather(w_out, "blk", axis=1, tiled=True),
        lax.all_gather(w_gate, "blk", axis=1, tiled=True),
        lax.all_gather(w_up, "blk", axis=1, tiled=True),
        lax.all_gather(w_down, "blk", axis=1, tiled=True),
    )
    full_query, full_key, full_value, full_out, full_gate, full_up, full_down = (
        lax.all_gather(columns[0], "items", axis=0, tiled=True),
        lax.all_gather(columns[1], "items", axis=0, tiled=True),
        lax.all_gather(columns[2], "items", axis=0, tiled=True),
        lax.all_gather(columns[3], "items", axis=0, tiled=True),
        lax.all_gather(columns[4], "items", axis=0, tiled=True),
        lax.all_gather(columns[5], "items", axis=0, tiled=True),
        lax.all_gather(columns[6], "items", axis=0, tiled=True),
    )
    items_here, row_count, model_width = patches.shape
    head_count = model_width // HEAD
    blocks = lax.axis_size("blk")
    counts = grid[:, 0] * grid[:, 1]
    patch_rows = patches.astype(jnp.float32)
    normed = rms_norm(patch_rows, norm_attn).astype(jnp.bfloat16)
    queries = product("ird,de->ire", normed, full_query).astype(jnp.bfloat16)
    key_rows = product("ird,de->ire", normed, full_key).astype(jnp.bfloat16)
    value_rows = product("ird,de->ire", normed, full_value).astype(jnp.bfloat16)
    query_heads = queries.reshape(items_here, row_count, head_count, HEAD)

    def split_part(piece, shard_index):
        part_rows = lax.dynamic_slice_in_dim(piece, shard_index * row_count, row_count, 1)
        return part_rows.reshape(items_here, row_count, head_count, HEAD)

    stat_shape = (items_here, head_count, row_count)
    start_stats = (jnp.full(stat_shape, -1e30, jnp.float32), jnp.zeros(stat_shape, jnp.float32))
    carried = start_stats
    key_piece = lax.all_gather(key_rows, "blk", axis=1, tiled=True)
    shards = key_piece.shape[1] // row_count

    def stats_one_shard(running, shard_index):
        running_max, running_sum = running
        key_part = split_part(key_piece, shard_index)
        scores = masked_scores(query_heads, key_part, shard_index * row_count, counts)
        new_max = jnp.maximum(running_max, jnp.max(scores, -1))
        new_sum = running_sum * jnp.exp(running_max - new_max) + jnp.sum(
            jnp.exp(scores - new_max[..., None]), -1
        )
        return ((new_max, new_sum), None)

    carried, unused = lax.scan(stats_one_shard, carried, jnp.arange(shards, dtype=jnp.int32))
    totals = carried
    log_total = totals[0] + jnp.log(totals[1])
    start_values = jnp.zeros((items_here, head_count, row_count, HEAD), jnp.float32)
    carried = start_values
    values_key_piece = lax.all_gather(key_rows, "blk", axis=1, tiled=True)
    value_piece = lax.all_gather(value_rows, "blk", axis=1, tiled=True)
    shards = values_key_piece.shape[1] // row_count

    def values_one_shard(accumulated, shard_index):
        key_part = split_part(values_key_piece, shard_index)
        value_part = split_part(value_piece, shard_index)
        scores = masked_scores(query_heads, key_part, shard_index * row_count, counts)
        weights_low = jnp.exp(scores - log_total[..., None]).astype(jnp.bfloat16)
        return (accumulated + product("ihqk,ikhd->ihqd", weights_low, value_part), None)

    carried, unused = lax.scan(values_one_shard, carried, jnp.arange(shards, dtype=jnp.int32))
    attended = carried.transpose(0, 2, 1, 3).reshape(items_here, row_count, model_width)
    attended_low = attended.astype(jnp.bfloat16)
    middle = patch_rows + product("ird,de->ire", attended_low, full_out)
    normed_mlp = rms_norm(middle, norm_mlp).astype(jnp.bfloat16)
    gate_in = product("ird,df->irf", normed_mlp, full_gate)
    upward = product("ird,df->irf", normed_mlp, full_up)
    activated = jax.nn.gelu(gate_in, approximate=True)
    hidden = (activated * upward).astype(jnp.bfloat16)
    output = (middle + product("irf,fd->ird", hidden, full_down)).astype(jnp.bfloat16)
    grad_down = product("irf,ird->fd", hidden, cotangent)
    grad_hidden = product("ird,fd->irf", cotangent, full_down)
    unused_gelu, gelu_back = jax.vjp(lambda inner: jax.nn.gelu(inner, approximate=True), gate_in)
    grad_gate_in = gelu_back(grad_hidden * upward)[0].astype(jnp.bfloat16)
    grad_upward = (grad_hidden * activated).astype(jnp.bfloat16)
    grad_gate = product("ird,irf->df", normed_mlp, grad_gate_in)
    grad_up = product("ird,irf->df", normed_mlp, grad_upward)
    grad_normed_mlp = product("irf,df->ird", grad_gate_in, full_gate) + product(
        "irf,df->ird", grad_upward, full_up
    )
    unused_norm, second_back = jax.vjp(rms_norm, middle, norm_mlp)
    grad_middle_part, grad_norm_mlp = second_back(grad_normed_mlp)
    grad_middle = cotangent.astype(jnp.float32) + grad_middle_part
    branch_grad = grad_middle.astype(jnp.bfloat16)
    grad_out = product("ird,ire->de", attended_low, branch_grad)
    grad_attended = product("ire,de->ird", branch_grad, full_out).astype(jnp.bfloat16)
    grad_heads = grad_attended.reshape(items_here, row_count, head_count, HEAD)
    delta = jnp.einsum(
        "iqhd,iqhd->ihq",
        grad_heads.astype(jnp.float32),
        attended.reshape(items_here, row_count, head_count, HEAD),
    )
    gathered_keys, gathered_values = (
        lax.all_gather(key_rows, "blk", axis=1, tiled=True),
        lax.all_gather(value_rows, "blk", axis=1, tiled=True),
    )
    query_start = jnp.zeros((items_here, row_count, head_count, HEAD), jnp.float32)

    def back_shard(grad_query, shard_index):
        key_part = split_part(gathered_keys, shard_index)
        value_part = split_part(gathered_values, shard_index)
        scores = masked_scores(query_heads, key_part, shard_index * row_count, counts)
        chances = jnp.exp(scores - log_total[..., None])
        grad_chances = product("iqhd,ikhd->ihqk", grad_heads, value_part)
        grad_scores = (chances * (grad_chances - delta[..., None])).astype(jnp.bfloat16)
        grad_query = grad_query + product("ihqk,ikhd->iqhd", grad_scores, key_part)
        key_term = product("ihqk,iqhd->ikhd", grad_scores, query_heads)
        value_term = product("ihqk,iqhd->ikhd", chances.astype(jnp.bfloat16), grad_heads)
        return (
            grad_query,
            (
                key_term.reshape(items_here, row_count, model_width),
                value_term.reshape(items_here, row_count, model_width),
            ),
        )

    grad_query, key_value_terms = lax.scan(
        back_shard, query_start, jnp.arange(blocks, dtype=jnp.int32)
    )
    key_sum, value_sum = (
        lax.psum_scatter(
            key_value_terms[0].astype(jnp.bfloat16), "blk", scatter_dimension=0, tiled=True
        ).astype(jnp.float32),
        lax.psum_scatter(
            key_value_terms[1].astype(jnp.bfloat16), "blk", scatter_dimension=0, tiled=True
        ).astype(jnp.float32),
    )
    grad_keys = key_sum[0].astype(jnp.bfloat16)
    grad_values = value_sum[0].astype(jnp.bfloat16)
    grad_queries = grad_query.reshape(items_here, row_count, model_width).astype(jnp.bfloat16)
    grad_wq = product("ird,ire->de", normed, grad_queries)
    grad_wk = product("ird,ire->de", normed, grad_keys)
    grad_wv = product("ird,ire->de", normed, grad_values)
    grad_normed = (
        product("ire,de->ird", grad_queries, full_query)
        + product("ire,de->ird", grad_keys, full_key)
        + product("ire,de->ird", grad_values, full_value)
    )
    unused_first, first_back = jax.vjp(rms_norm, patch_rows, norm_attn)
    grad_rows_part, grad_norm_attn = first_back(grad_normed)
    grad_patches = (grad_middle + grad_rows_part).astype(jnp.bfloat16)
    gain_total = lax.psum((grad_norm_attn, grad_norm_mlp), ("items", "blk"))
    by_rows = (
        lax.psum_scatter(
            grad_wq.astype(jnp.bfloat16), "items", scatter_dimension=0, tiled=True
        ).astype(jnp.float32),
        lax.psum_scatter(
            grad_wk.astype(jnp.bfloat16), "items", scatter_dimension=0, tiled=True
        ).astype(jnp.float32),
        lax.psum_scatter(
            grad_wv.astype(jnp.bfloat16), "items", scatter_dimension=0, tiled=True
        ).astype(jnp.float32),
        lax.psum_scatter(
            grad_out.astype(jnp.bfloat16), "items", scatter_dimension=0, tiled=True
        ).astype(jnp.float32),
        lax.psum_scatter(
            grad_gate.astype(jnp.bfloat16), "items", scatter_dimension=0, tiled=True
        ).astype(jnp.float32),
        lax.psum_scatter(
            grad_up.astype(jnp.bfloat16), "items", scatter_dimension=0, tiled=True
        ).astype(jnp.float32),
        lax.psum_scatter(
            grad_down.astype(jnp.bfloat16), "items", scatter_dimension=0, tiled=True
        ).astype(jnp.float32),
    )
    final_shards = (
        lax.psum_scatter(
            by_rows[0].astype(jnp.bfloat16), "blk", scatter_dimension=1, tiled=True
        ).astype(jnp.float32),
        lax.psum_scatter(
            by_rows[1].astype(jnp.bfloat16), "blk", scatter_dimension=1, tiled=True
        ).astype(jnp.float32),
        lax.psum_scatter(
            by_rows[2].astype(jnp.bfloat16), "blk", scatter_dimension=1, tiled=True
        ).astype(jnp.float32),
        lax.psum_scatter(
            by_rows[3].astype(jnp.bfloat16), "blk", scatter_dimension=1, tiled=True
        ).astype(jnp.float32),
        lax.psum_scatter(
            by_rows[4].astype(jnp.bfloat16), "blk", scatter_dimension=1, tiled=True
        ).astype(jnp.float32),
        lax.psum_scatter(
            by_rows[5].astype(jnp.bfloat16), "blk", scatter_dimension=1, tiled=True
        ).astype(jnp.float32),
        lax.psum_scatter(
            by_rows[6].astype(jnp.bfloat16), "blk", scatter_dimension=1, tiled=True
        ).astype(jnp.float32),
    )
    return (
        output,
        grad_patches,
        gain_total[0],
        final_shards[0],
        final_shards[1],
        final_shards[2],
        final_shards[3],
        gain_total[1],
        final_shards[4],
        final_shards[5],
        final_shards[6],
    )


VMEM = 24 << 20


def swap_items(values, items, bits):
    return lax.ppermute(values, "items", [(place, place ^ bits) for place in range(items)])


def swap_blocks(values):
    return lax.ppermute(values, "blk", [(0, 1), (1, 0)])


def join(own, other, axis, later):
    width = own.shape[axis]
    shape = list(own.shape)
    shape[axis] = 2 * width
    whole = jnp.zeros(shape, own.dtype)
    whole = lax.dynamic_update_slice_in_dim(whole, own, later * width, axis)
    return lax.dynamic_update_slice_in_dim(whole, other, (1 - later) * width, axis)


def after(*values):
    return lax.optimization_barrier(values)


class Place:
    def __init__(self, items):
        self.items = items
        self.levels = items.bit_length() - 1
        self.index = lax.axis_index("items")
        self.block = lax.axis_index("blk")
        self.far = list(range(self.levels - 2))

    def find(self, step):
        if step == "blk":
            return self.levels + 1, self.block
        return step, (self.index >> (self.levels - 1 - step)) & 1

    def shaped(self, shard):
        return shard.reshape((1,) * self.levels + shard.shape)

    def send(self, values, step):
        return swap_blocks(values) if step == "blk" else swap_items(values, self.items, 1 << (self.levels - 1 - step))

    def meet(self, whole, other, step):
        axis, mine = self.find(step)
        return join(whole, other, axis, mine)

    def send_far(self, whole):
        return [swap_items(whole, self.items, 4 * apart) for apart in range(1, self.items // 4)]

    def meet_far(self, whole, others):
        deep, mine = self.items // 4, self.index // 4
        joined = jnp.zeros((deep,) + whole.shape[len(self.far) :], whole.dtype)
        for apart, part in enumerate([whole] + list(others)):
            part = part.reshape((1,) + joined.shape[1:])
            joined = lax.dynamic_update_slice_in_dim(joined, part, mine ^ apart, 0)
        return joined.reshape((2,) * len(self.far) + joined.shape[1:])

    def part_of(self, whole, rows):
        return whole.reshape((2,) * self.levels + (rows, whole.shape[-1]))

    def halves(self, part, step):
        axis, mine = self.find(step)
        width = part.shape[axis] // 2
        kept = lax.dynamic_slice_in_dim(part, mine * width, width, axis)
        sent = lax.dynamic_slice_in_dim(part, (1 - mine) * width, width, axis)
        return kept, self.send(sent, step)


def flat(whole):
    return whole.reshape(-1, whole.shape[-1])


def add(kept, other):
    return (kept.astype(jnp.float32) + other.astype(jnp.float32)).astype(jnp.bfloat16)


def own_lanes(values, head):
    lanes = lax.broadcasted_iota(jnp.int32, values.shape, 1)
    return jnp.where(lanes // HEAD == head, values, jnp.zeros_like(values))


def dot_nt(left, right):
    return lax.dot_general(left, right, (((1,), (1,)), ((), ())), preferred_element_type=jnp.float32)


def dot_tn(left, right):
    return lax.dot_general(left, right, (((0,), (0,)), ((), ())), preferred_element_type=jnp.float32)


def dot_nn(left, right):
    return jnp.dot(left, right, preferred_element_type=jnp.float32)


def turned(values):
    return values.astype(jnp.float32).T


def key_bias(where_ref, length):
    places = lax.broadcasted_iota(jnp.int32, (length, 1), 0) + where_ref[1]
    places = jnp.where(places < length, places, places - length)
    return jnp.where(places < where_ref[0], 0.0, -1000000000.0)


def attend_kernel(count_ref, q_ref, k_ref, v_ref, out_ref, log_ref):
    keys, values = k_ref[...], turned(v_ref[...])
    bias = key_bias(count_ref, keys.shape[0])
    lanes = lax.broadcasted_iota(jnp.int32, values.shape, 0)
    total = 0.0
    for head in range(out_ref.shape[1] // HEAD):
        scores = dot_nt(keys, own_lanes(q_ref[...], head)) + bias
        largest = jnp.max(scores, 0, keepdims=True)
        shifted = jnp.exp(scores - largest)
        summed = jnp.sum(shifted, 0, keepdims=True)
        head_values = jnp.where(lanes // HEAD == head, values, 0.0).astype(jnp.bfloat16)
        total = total + dot_nn(head_values, shifted.astype(jnp.bfloat16)) * (1.0 / summed)
        log_ref[0, head : head + 1, :] = largest + jnp.log(summed)
    out_ref[...] = total.T.astype(jnp.bfloat16)


def attend(where, qkv, part):
    length, groups = qkv.shape[0], qkv.shape[1] // 384
    rows, width = length // 2, groups * 128
    return pl.pallas_call(
        attend_kernel,
        grid=(groups,),
        in_specs=[
            pl.BlockSpec(memory_space=pltpu.SMEM),
            pl.BlockSpec((rows, 128), lambda g: (part, g)),
            pl.BlockSpec((length, 128), lambda g: (0, groups + g)),
            pl.BlockSpec((length, 128), lambda g: (0, 2 * groups + g)),
        ],
        out_specs=[
            pl.BlockSpec((rows, 128), lambda g: (0, g)),
            pl.BlockSpec((1, 128 // HEAD, rows), lambda g: (g, 0, 0)),
        ],
        out_shape=[
            jax.ShapeDtypeStruct((rows, width), jnp.bfloat16),
            jax.ShapeDtypeStruct((groups, 128 // HEAD, rows), jnp.float32),
        ],
        compiler_params=pltpu.CompilerParams(vmem_limit_bytes=VMEM),
        cost_estimate=pl.CostEstimate(flops=4 * rows * length * width, bytes_accessed=4 * length * width, transcendentals=rows * length),
        name="attend",
    )(where, qkv, qkv, qkv)


def attend_back_kernel(where_ref, q_ref, k_ref, v_ref, out_ref, log_ref, grad_ref, *refs):
    keys, values = k_ref[...], v_ref[...]
    dq_ref, dk_ref, dv_ref = refs[-3:]
    bias = key_bias(where_ref, keys.shape[0])
    turned_keys = turned(keys)
    lanes = lax.broadcasted_iota(jnp.int32, turned_keys.shape, 0)
    weighed = (grad_ref[...].astype(jnp.float32) * out_ref[...].astype(jnp.float32)).T
    grad_q = 0.0
    grad_k, grad_v = [ref[...] for ref in refs[:-3]] or (0.0, 0.0)
    for head in range(dq_ref.shape[1] // HEAD):
        q_head = own_lanes(q_ref[...], head)
        grad_head = own_lanes(grad_ref[...], head)
        delta = jnp.sum(weighed[head * HEAD : (head + 1) * HEAD], 0, keepdims=True)
        scores = dot_nt(keys, q_head) + bias
        chances = jnp.exp(scores - log_ref[0, head : head + 1, :])
        grad_scores = (chances * (dot_nt(values, grad_head) - delta)).astype(jnp.bfloat16)
        head_keys = jnp.where(lanes // HEAD == head, turned_keys, 0.0).astype(jnp.bfloat16)
        grad_q = grad_q + dot_nn(head_keys, grad_scores)
        grad_k = grad_k + dot_nn(grad_scores, q_head)
        grad_v = grad_v + dot_nn(chances.astype(jnp.bfloat16), grad_head)
    dq_ref[...] = grad_q.T.astype(jnp.bfloat16)
    dk_ref[...] = grad_k.astype(dk_ref.dtype)
    dv_ref[...] = grad_v.astype(dv_ref.dtype)


def attend_back(where, qkv, attended, logs, grad, part, *sums):
    length, groups = qkv.shape[0], qkv.shape[1] // 384
    rows, width = grad.shape
    kind = jnp.bfloat16 if sums else jnp.float32
    tall = pl.BlockSpec((length, 128), lambda g: (0, g))
    wide = pl.BlockSpec((rows, 128), lambda g: (0, g))
    return pl.pallas_call(
        attend_back_kernel,
        grid=(groups,),
        in_specs=[
            pl.BlockSpec(memory_space=pltpu.SMEM),
            pl.BlockSpec((rows, 128), lambda g: (part, g)),
            pl.BlockSpec((length, 128), lambda g: (0, groups + g)),
            pl.BlockSpec((length, 128), lambda g: (0, 2 * groups + g)),
            wide,
            pl.BlockSpec((1, 128 // HEAD, rows), lambda g: (g, 0, 0)),
            wide,
        ]
        + [tall] * len(sums),
        out_specs=[wide, tall, tall],
        out_shape=[
            jax.ShapeDtypeStruct((rows, width), jnp.bfloat16),
            jax.ShapeDtypeStruct((length, width), kind),
            jax.ShapeDtypeStruct((length, width), kind),
        ],
        compiler_params=pltpu.CompilerParams(vmem_limit_bytes=VMEM),
        cost_estimate=pl.CostEstimate(flops=4 * rows * length * width, bytes_accessed=4 * length * width, transcendentals=rows * length),
        name="attend_back",
    )(where, qkv, qkv, qkv, attended, logs, grad, *sums)


def by_heads(
    items,
    patches,
    grid,
    norm_attn,
    w_query,
    w_key,
    w_value,
    w_out,
    norm_mlp,
    w_gate,
    w_up,
    w_down,
    cotangent,
):
    place = Place(items)
    block, far, y, core = place.block, place.far, place.levels - 2, place.levels - 1
    row_count, model_width = patches.shape[1:]
    half = model_width // 2
    count = (grid[0, 0] * grid[0, 1]).astype(jnp.int32)
    where = jnp.stack([count, block * row_count])
    own_rows, own_cot = patches[0], cotangent[0]
    shard_rows, down_rows = w_query.shape[0], w_down.shape[0]

    def advance(held, steps):
        moved = [whole if step is None else place.send(whole, step) for whole, step in zip(held, steps)]
        moved = after(*moved)
        return [
            other if step is None else place.meet(whole, other, step)
            for whole, other, step in zip(held, moved, steps)
        ]

    other_rows = swap_blocks(own_rows)
    w_qkv = jnp.concatenate([w_query, w_key, w_value], 1)
    w_qkv, gate, up, down, out = [place.shaped(shard) for shard in (w_qkv, w_gate, w_up, w_down, w_out)]

    far_qkv, down_blk, gate, up, out = after(place.send_far(w_qkv), place.send(down, "blk"), gate, up, out)
    w_qkv = place.meet_far(w_qkv, far_qkv)
    down = place.meet(down, down_blk, "blk")
    qkv_y, down_y = place.send(w_qkv, y), place.send(down, y)
    gate, up = advance([gate, up], [far[0], far[0]])
    gate_far, up_far = place.send(gate, far[1]), place.send(up, far[1])
    qkv_y, down_y, gate_far, up_far, out = after(qkv_y, down_y, gate_far, up_far, out)
    w_qkv = place.meet(w_qkv, qkv_y, y)
    down = place.meet(down, down_y, y)
    gate, up = place.meet(gate, gate_far, far[1]), place.meet(up, up_far, far[1])
    for step in far[2:]:
        gate, up = advance([gate, up], [step, step])
    w_qkv, out = advance([w_qkv, out], [core, far[0]])
    w_qkv = flat(w_qkv)

    moved = place.send(gate, "blk"), place.send(up, y), place.send(out, far[1])
    down_far = place.send(down, far[0])
    all_rows = jnp.concatenate([own_rows, other_rows], 0)
    all_normed = rms_norm(all_rows.astype(jnp.float32), norm_attn).astype(jnp.bfloat16)
    qkv = dot_nn(all_normed, w_qkv).astype(jnp.bfloat16)
    attended_there, logs_there = attend(where, qkv, 1)
    attended_there, moved, qkv_here = after(attended_there, moved, qkv)
    gate = place.meet(gate, moved[0], "blk")
    up = place.meet(up, moved[1], y)
    out = place.meet(out, moved[2], far[1])

    attended_other = swap_blocks(attended_there)
    out_blk, gate_y, up_blk = place.send(out, "blk"), place.send(gate, y), place.send(up, "blk")
    attended_here, logs_here = attend(where, qkv_here, 0)
    attended_here, out_blk, down_far = after(attended_here, out_blk, down_far)
    out = place.meet(out, out_blk, "blk")
    down = place.meet(down, down_far, far[0])
    out_y, down_far = place.send(out, y), place.send(down, far[1])
    attended_other, out_y = after(attended_other, out_y)
    attended = join(attended_here, attended_other, 1, block)
    out = place.meet(out, out_y, y)
    gate_y, up_blk = [after(moved, attended_here)[0] for moved in (gate_y, up_blk)]
    gate = place.meet(gate, gate_y, y)
    up = place.meet(up, up_blk, "blk")
    down = place.meet(down, down_far, far[1])
    for step in far[2:]:
        out, down = advance([out, down], [step, step])
    full_out, full_gate, full_up, full_down = [
        flat(place.meet(whole, place.send(whole, core), core)) for whole in (out, gate, up, down)
    ]
    patch_rows = own_rows.astype(jnp.float32)
    middle = patch_rows + dot_nn(attended, full_out)
    normed_mlp = rms_norm(middle, norm_mlp).astype(jnp.bfloat16)
    gate_in = dot_nn(normed_mlp, full_gate)
    upward = dot_nn(normed_mlp, full_up)
    activated = jax.nn.gelu(gate_in, approximate=True)
    hidden = (activated * upward).astype(jnp.bfloat16)
    output = (middle + dot_nn(hidden, full_down)).astype(jnp.bfloat16)
    grad_down = dot_tn(hidden, own_cot).astype(jnp.bfloat16)
    core_down = place.halves(place.part_of(grad_down, down_rows), core)
    grad_hidden = dot_nt(own_cot, full_down)
    unused_gelu, gelu_back = jax.vjp(lambda inner: jax.nn.gelu(inner, approximate=True), gate_in)
    grad_gate_in = gelu_back(grad_hidden * upward)[0].astype(jnp.bfloat16)
    grad_upward = (grad_hidden * activated).astype(jnp.bfloat16)
    grad_normed_mlp = dot_nt(grad_gate_in, full_gate) + dot_nt(grad_upward, full_up)
    grad_normed_mlp, core_down = after(grad_normed_mlp, core_down)
    far_down = place.halves(add(*core_down), far[-1])
    unused_norm, second_back = jax.vjp(rms_norm, middle, norm_mlp)
    grad_middle_part, gain_mlp = second_back(grad_normed_mlp)
    grad_middle = own_cot.astype(jnp.float32) + grad_middle_part
    branch_grad = grad_middle.astype(jnp.bfloat16)
    grad_attended = dot_nt(branch_grad, full_out).astype(jnp.bfloat16)
    heads_here = lax.dynamic_slice_in_dim(grad_attended, block * half, half, 1)
    heads_sent = lax.dynamic_slice_in_dim(grad_attended, (1 - block) * half, half, 1)
    heads_there = swap_blocks(heads_sent)
    normed_mlp, attended, heads_sent = after(normed_mlp, attended, heads_sent)
    grad_gate = dot_tn(normed_mlp, grad_gate_in).astype(jnp.bfloat16)
    grad_up = dot_tn(normed_mlp, grad_upward).astype(jnp.bfloat16)
    grad_out = dot_tn(attended, branch_grad).astype(jnp.bfloat16)
    cores = [place.halves(place.part_of(grad, shard_rows), core) for grad in (grad_gate, grad_up, grad_out)]
    heads_there, grad_gate, grad_up, grad_out = after(heads_there, grad_gate, grad_up, grad_out)
    part_gate, part_up, part_out = [add(*pair) for pair in cores]

    wide = place.halves(part_gate, y), place.halves(part_up, "blk")
    heads_here, part_out = after(heads_here, part_out)
    queries_here, *sums = attend_back(where, qkv, attended_here, logs_here, heads_here, 0)
    sums, far_down = after(sums, far_down)
    near = far[::-1]
    far_down = place.halves(add(*far_down), near[1])
    queries_there, grad_keys, grad_values = attend_back(where, qkv, attended_there, logs_there, heads_there, 1, *sums)
    queries_there, grad_keys, grad_values, wide = after(queries_there, grad_keys, grad_values, wide)
    part_gate, part_up = [add(*pair) for pair in wide]
    wide = place.halves(part_gate, "blk"), place.halves(part_up, y), place.halves(part_out, "blk")
    grad_queries = jnp.concatenate([queries_here, queries_there], 0)
    grad_qkv = jnp.concatenate([grad_queries, grad_keys, grad_values], 1)
    grad_w_qkv = dot_tn(all_normed, grad_qkv).astype(jnp.bfloat16)
    core_qkv = place.halves(place.part_of(grad_w_qkv, shard_rows), core)
    grad_all_normed = dot_nt(grad_qkv, w_qkv)
    unused_all, gain_back = jax.vjp(lambda gain: rms_norm(all_rows.astype(jnp.float32), gain), norm_attn)
    gains = jnp.stack([gain_back(grad_all_normed)[0], gain_mlp])
    gains_core = place.send(gains, core)
    core_qkv, gains_core, wide, far_down = after(core_qkv, gains_core, wide, far_down)
    gains = gains + gains_core
    part_qkv, part_down = add(*core_qkv), add(*far_down)
    part_gate, part_up, part_out = [add(*pair) for pair in wide]
    part_gate = jnp.concatenate([part_gate, part_up], -1)

    rows_other = swap_blocks(grad_all_normed[row_count:].astype(jnp.bfloat16))
    moving = place.halves(part_qkv, y), place.halves(part_gate, near[0]), place.halves(part_out, y)
    rows_other, moving, gains_y = after(rows_other, moving, place.send(gains, y))
    part_qkv, part_gate, part_out = [add(*pair) for pair in moving]
    gains = gains + gains_y

    moving = (
        place.halves(part_qkv, near[0]),
        place.halves(part_gate, near[1]),
        place.halves(part_down, y),
        place.halves(part_out, near[0]),
    )
    moving, gains_far = after(moving, place.send(gains, near[0]))
    part_qkv, part_gate, part_down, part_out = [add(*pair) for pair in moving]
    gains = gains + gains_far
    moving = place.halves(part_qkv, near[1]), place.halves(part_out, near[1]), place.halves(part_down, "blk")
    gains_far = place.send(gains, near[1])
    grad_normed = grad_all_normed[:row_count] + rows_other.astype(jnp.float32)
    unused_first, first_back = jax.vjp(rms_norm, patch_rows, norm_attn)
    grad_rows_part, unused_gain = first_back(grad_normed)
    grad_patches = (grad_middle + grad_rows_part).astype(jnp.bfloat16)
    part_qkv, part_out, part_down = [add(*pair) for pair in moving]
    gains = gains + gains_far
    for step in near[2:]:
        moving = [place.halves(part, step) for part in (part_qkv, part_gate, part_out, part_down)]
        part_qkv, part_gate, part_out, part_down = [add(*pair) for pair in moving]
        gains = gains + place.send(gains, step)
    gains = gains + swap_blocks(gains)
    shard_qkv, shard_out, shard_gate, shard_down = [
        flat(shard).astype(jnp.float32) for shard in (part_qkv, part_out, part_gate, part_down)
    ]
    inner = shard_gate.shape[1] // 2
    return (
        output[None],
        grad_patches[None],
        gains[0],
        shard_qkv[:, :half],
        shard_qkv[:, half : 2 * half],
        shard_qkv[:, 2 * half :],
        shard_out,
        gains[1],
        shard_gate[:, :inner],
        shard_gate[:, inner:],
        shard_down,
    )


def local(items, blocks, patches, *rest):
    items_here, row_count, model_width = patches.shape
    fits = (
        blocks == 2
        and items_here == 1
        and items >= 16
        and items & (items - 1) == 0
        and row_count % 128 == 0
        and model_width % 256 == 0
    )
    if fits:
        return by_heads(items, patches, *rest)
    return general(patches, *rest)


def solution(mesh):
    placed = (
        P("items", "blk", None),
        P("items", None),
        P(),
        P("items", "blk"),
        P("items", "blk"),
        P("items", "blk"),
        P("items", "blk"),
        P(),
        P("items", "blk"),
        P("items", "blk"),
        P("items", "blk"),
        P("items", "blk", None),
    )
    return jax.shard_map(
        functools.partial(local, mesh.shape["items"], mesh.shape["blk"]),
        mesh=mesh,
        in_specs=placed,
        out_specs=(
            P("items", "blk", None),
            P("items", "blk", None),
            P(),
            P("items", "blk"),
            P("items", "blk"),
            P("items", "blk"),
            P("items", "blk"),
            P(),
            P("items", "blk"),
            P("items", "blk"),
            P("items", "blk"),
        ),
        check_vma=False,
    )
```

```python
import functools

import jax
import jax.numpy as jnp
from jax import lax
from jax.experimental import pallas as pl
from jax.experimental.pallas import tpu as pltpu
from jax.sharding import PartitionSpec as P

HEAD = 64


EPSILON = 1e-06


def rms_norm(values, gain):
    return values * lax.rsqrt(jnp.mean(values * values, -1, keepdims=True) + EPSILON) * gain


def product(formula, left, right):
    return jnp.einsum(formula, left, right, preferred_element_type=jnp.float32)


def masked_scores(query_heads, key_part, first_key, counts):
    scores = product("iqhd,ikhd->ihqk", query_heads, key_part)
    places = first_key + jnp.arange(key_part.shape[1], dtype=jnp.int32)
    allowed = places[None, :] < counts[:, None]
    return jnp.where(allowed[:, None, None, :], scores, -1000000000.0)


def general(
    patches,
    grid,
    norm_attn,
    w_query,
    w_key,
    w_value,
    w_out,
    norm_mlp,
    w_gate,
    w_up,
    w_down,
    cotangent,
):
    columns = (
        lax.all_gather(w_query, "blk", axis=1, tiled=True),
        lax.all_gather(w_key, "blk", axis=1, tiled=True),
        lax.all_gather(w_value, "blk", axis=1, tiled=True),
        lax.all_gather(w_out, "blk", axis=1, tiled=True),
        lax.all_gather(w_gate, "blk", axis=1, tiled=True),
        lax.all_gather(w_up, "blk", axis=1, tiled=True),
        lax.all_gather(w_down, "blk", axis=1, tiled=True),
    )
    full_query, full_key, full_value, full_out, full_gate, full_up, full_down = (
        lax.all_gather(columns[0], "items", axis=0, tiled=True),
        lax.all_gather(columns[1], "items", axis=0, tiled=True),
        lax.all_gather(columns[2], "items", axis=0, tiled=True),
        lax.all_gather(columns[3], "items", axis=0, tiled=True),
        lax.all_gather(columns[4], "items", axis=0, tiled=True),
        lax.all_gather(columns[5], "items", axis=0, tiled=True),
        lax.all_gather(columns[6], "items", axis=0, tiled=True),
    )
    items_here, row_count, model_width = patches.shape
    head_count = model_width // HEAD
    blocks = lax.axis_size("blk")
    counts = grid[:, 0] * grid[:, 1]
    patch_rows = patches.astype(jnp.float32)
    normed = rms_norm(patch_rows, norm_attn).astype(jnp.bfloat16)
    queries = product("ird,de->ire", normed, full_query).astype(jnp.bfloat16)
    key_rows = product("ird,de->ire", normed, full_key).astype(jnp.bfloat16)
    value_rows = product("ird,de->ire", normed, full_value).astype(jnp.bfloat16)
    query_heads = queries.reshape(items_here, row_count, head_count, HEAD)

    def split_part(piece, shard_index):
        part_rows = lax.dynamic_slice_in_dim(piece, shard_index * row_count, row_count, 1)
        return part_rows.reshape(items_here, row_count, head_count, HEAD)

    stat_shape = (items_here, head_count, row_count)
    start_stats = (jnp.full(stat_shape, -1e30, jnp.float32), jnp.zeros(stat_shape, jnp.float32))
    carried = start_stats
    key_piece = lax.all_gather(key_rows, "blk", axis=1, tiled=True)
    shards = key_piece.shape[1] // row_count

    def stats_one_shard(running, shard_index):
        running_max, running_sum = running
        key_part = split_part(key_piece, shard_index)
        scores = masked_scores(query_heads, key_part, shard_index * row_count, counts)
        new_max = jnp.maximum(running_max, jnp.max(scores, -1))
        new_sum = running_sum * jnp.exp(running_max - new_max) + jnp.sum(
            jnp.exp(scores - new_max[..., None]), -1
        )
        return ((new_max, new_sum), None)

    carried, unused = lax.scan(stats_one_shard, carried, jnp.arange(shards, dtype=jnp.int32))
    totals = carried
    log_total = totals[0] + jnp.log(totals[1])
    start_values = jnp.zeros((items_here, head_count, row_count, HEAD), jnp.float32)
    carried = start_values
    values_key_piece = lax.all_gather(key_rows, "blk", axis=1, tiled=True)
    value_piece = lax.all_gather(value_rows, "blk", axis=1, tiled=True)
    shards = values_key_piece.shape[1] // row_count

    def values_one_shard(accumulated, shard_index):
        key_part = split_part(values_key_piece, shard_index)
        value_part = split_part(value_piece, shard_index)
        scores = masked_scores(query_heads, key_part, shard_index * row_count, counts)
        weights_low = jnp.exp(scores - log_total[..., None]).astype(jnp.bfloat16)
        return (accumulated + product("ihqk,ikhd->ihqd", weights_low, value_part), None)

    carried, unused = lax.scan(values_one_shard, carried, jnp.arange(shards, dtype=jnp.int32))
    attended = carried.transpose(0, 2, 1, 3).reshape(items_here, row_count, model_width)
    attended_low = attended.astype(jnp.bfloat16)
    middle = patch_rows + product("ird,de->ire", attended_low, full_out)
    normed_mlp = rms_norm(middle, norm_mlp).astype(jnp.bfloat16)
    gate_in = product("ird,df->irf", normed_mlp, full_gate)
    upward = product("ird,df->irf", normed_mlp, full_up)
    activated = jax.nn.gelu(gate_in, approximate=True)
    hidden = (activated * upward).astype(jnp.bfloat16)
    output = (middle + product("irf,fd->ird", hidden, full_down)).astype(jnp.bfloat16)
    grad_down = product("irf,ird->fd", hidden, cotangent)
    grad_hidden = product("ird,fd->irf", cotangent, full_down)
    unused_gelu, gelu_back = jax.vjp(lambda inner: jax.nn.gelu(inner, approximate=True), gate_in)
    grad_gate_in = gelu_back(grad_hidden * upward)[0].astype(jnp.bfloat16)
    grad_upward = (grad_hidden * activated).astype(jnp.bfloat16)
    grad_gate = product("ird,irf->df", normed_mlp, grad_gate_in)
    grad_up = product("ird,irf->df", normed_mlp, grad_upward)
    grad_normed_mlp = product("irf,df->ird", grad_gate_in, full_gate) + product(
        "irf,df->ird", grad_upward, full_up
    )
    unused_norm, second_back = jax.vjp(rms_norm, middle, norm_mlp)
    grad_middle_part, grad_norm_mlp = second_back(grad_normed_mlp)
    grad_middle = cotangent.astype(jnp.float32) + grad_middle_part
    branch_grad = grad_middle.astype(jnp.bfloat16)
    grad_out = product("ird,ire->de", attended_low, branch_grad)
    grad_attended = product("ire,de->ird", branch_grad, full_out).astype(jnp.bfloat16)
    grad_heads = grad_attended.reshape(items_here, row_count, head_count, HEAD)
    delta = jnp.einsum(
        "iqhd,iqhd->ihq",
        grad_heads.astype(jnp.float32),
        attended.reshape(items_here, row_count, head_count, HEAD),
    )
    gathered_keys, gathered_values = (
        lax.all_gather(key_rows, "blk", axis=1, tiled=True),
        lax.all_gather(value_rows, "blk", axis=1, tiled=True),
    )
    query_start = jnp.zeros((items_here, row_count, head_count, HEAD), jnp.float32)

    def back_shard(grad_query, shard_index):
        key_part = split_part(gathered_keys, shard_index)
        value_part = split_part(gathered_values, shard_index)
        scores = masked_scores(query_heads, key_part, shard_index * row_count, counts)
        chances = jnp.exp(scores - log_total[..., None])
        grad_chances = product("iqhd,ikhd->ihqk", grad_heads, value_part)
        grad_scores = (chances * (grad_chances - delta[..., None])).astype(jnp.bfloat16)
        grad_query = grad_query + product("ihqk,ikhd->iqhd", grad_scores, key_part)
        key_term = product("ihqk,iqhd->ikhd", grad_scores, query_heads)
        value_term = product("ihqk,iqhd->ikhd", chances.astype(jnp.bfloat16), grad_heads)
        return (
            grad_query,
            (
                key_term.reshape(items_here, row_count, model_width),
                value_term.reshape(items_here, row_count, model_width),
            ),
        )

    grad_query, key_value_terms = lax.scan(
        back_shard, query_start, jnp.arange(blocks, dtype=jnp.int32)
    )
    key_sum, value_sum = (
        lax.psum_scatter(
            key_value_terms[0].astype(jnp.bfloat16), "blk", scatter_dimension=0, tiled=True
        ).astype(jnp.float32),
        lax.psum_scatter(
            key_value_terms[1].astype(jnp.bfloat16), "blk", scatter_dimension=0, tiled=True
        ).astype(jnp.float32),
    )
    grad_keys = key_sum[0].astype(jnp.bfloat16)
    grad_values = value_sum[0].astype(jnp.bfloat16)
    grad_queries = grad_query.reshape(items_here, row_count, model_width).astype(jnp.bfloat16)
    grad_wq = product("ird,ire->de", normed, grad_queries)
    grad_wk = product("ird,ire->de", normed, grad_keys)
    grad_wv = product("ird,ire->de", normed, grad_values)
    grad_normed = (
        product("ire,de->ird", grad_queries, full_query)
        + product("ire,de->ird", grad_keys, full_key)
        + product("ire,de->ird", grad_values, full_value)
    )
    unused_first, first_back = jax.vjp(rms_norm, patch_rows, norm_attn)
    grad_rows_part, grad_norm_attn = first_back(grad_normed)
    grad_patches = (grad_middle + grad_rows_part).astype(jnp.bfloat16)
    gain_total = lax.psum((grad_norm_attn, grad_norm_mlp), ("items", "blk"))
    by_rows = (
        lax.psum_scatter(
            grad_wq.astype(jnp.bfloat16), "items", scatter_dimension=0, tiled=True
        ).astype(jnp.float32),
        lax.psum_scatter(
            grad_wk.astype(jnp.bfloat16), "items", scatter_dimension=0, tiled=True
        ).astype(jnp.float32),
        lax.psum_scatter(
            grad_wv.astype(jnp.bfloat16), "items", scatter_dimension=0, tiled=True
        ).astype(jnp.float32),
        lax.psum_scatter(
            grad_out.astype(jnp.bfloat16), "items", scatter_dimension=0, tiled=True
        ).astype(jnp.float32),
        lax.psum_scatter(
            grad_gate.astype(jnp.bfloat16), "items", scatter_dimension=0, tiled=True
        ).astype(jnp.float32),
        lax.psum_scatter(
            grad_up.astype(jnp.bfloat16), "items", scatter_dimension=0, tiled=True
        ).astype(jnp.float32),
        lax.psum_scatter(
            grad_down.astype(jnp.bfloat16), "items", scatter_dimension=0, tiled=True
        ).astype(jnp.float32),
    )
    final_shards = (
        lax.psum_scatter(
            by_rows[0].astype(jnp.bfloat16), "blk", scatter_dimension=1, tiled=True
        ).astype(jnp.float32),
        lax.psum_scatter(
            by_rows[1].astype(jnp.bfloat16), "blk", scatter_dimension=1, tiled=True
        ).astype(jnp.float32),
        lax.psum_scatter(
            by_rows[2].astype(jnp.bfloat16), "blk", scatter_dimension=1, tiled=True
        ).astype(jnp.float32),
        lax.psum_scatter(
            by_rows[3].astype(jnp.bfloat16), "blk", scatter_dimension=1, tiled=True
        ).astype(jnp.float32),
        lax.psum_scatter(
            by_rows[4].astype(jnp.bfloat16), "blk", scatter_dimension=1, tiled=True
        ).astype(jnp.float32),
        lax.psum_scatter(
            by_rows[5].astype(jnp.bfloat16), "blk", scatter_dimension=1, tiled=True
        ).astype(jnp.float32),
        lax.psum_scatter(
            by_rows[6].astype(jnp.bfloat16), "blk", scatter_dimension=1, tiled=True
        ).astype(jnp.float32),
    )
    return (
        output,
        grad_patches,
        gain_total[0],
        final_shards[0],
        final_shards[1],
        final_shards[2],
        final_shards[3],
        gain_total[1],
        final_shards[4],
        final_shards[5],
        final_shards[6],
    )


VMEM = 24 << 20


def swap_items(values, items, bits):
    return lax.ppermute(values, "items", [(place, place ^ bits) for place in range(items)])


def swap_blocks(values):
    return lax.ppermute(values, "blk", [(0, 1), (1, 0)])


def join(own, other, axis, later):
    width = own.shape[axis]
    shape = list(own.shape)
    shape[axis] = 2 * width
    whole = jnp.zeros(shape, own.dtype)
    whole = lax.dynamic_update_slice_in_dim(whole, own, later * width, axis)
    return lax.dynamic_update_slice_in_dim(whole, other, (1 - later) * width, axis)


def after(*values):
    return lax.optimization_barrier(values)


class Place:
    def __init__(self, items):
        self.items = items
        self.levels = items.bit_length() - 1
        self.index = lax.axis_index("items")
        self.block = lax.axis_index("blk")
        self.far = list(range(self.levels - 2))

    def find(self, step):
        if step == "blk":
            return self.levels + 1, self.block
        return step, (self.index >> (self.levels - 1 - step)) & 1

    def shaped(self, shard):
        return shard.reshape((1,) * self.levels + shard.shape)

    def send(self, values, step):
        return swap_blocks(values) if step == "blk" else swap_items(values, self.items, 1 << (self.levels - 1 - step))

    def meet(self, whole, other, step):
        axis, mine = self.find(step)
        return join(whole, other, axis, mine)

    def send_far(self, whole):
        return [swap_items(whole, self.items, 4 * apart) for apart in range(1, self.items // 4)]

    def meet_far(self, whole, others):
        deep, mine = self.items // 4, self.index // 4
        joined = jnp.zeros((deep,) + whole.shape[len(self.far) :], whole.dtype)
        for apart, part in enumerate([whole] + list(others)):
            part = part.reshape((1,) + joined.shape[1:])
            joined = lax.dynamic_update_slice_in_dim(joined, part, mine ^ apart, 0)
        return joined.reshape((2,) * len(self.far) + joined.shape[1:])

    def part_of(self, whole, rows):
        return whole.reshape((2,) * self.levels + (rows, whole.shape[-1]))

    def cuts(self, part, step):
        axis, mine = self.find(step)
        width = part.shape[axis] // 2
        kept = lax.dynamic_slice_in_dim(part, mine * width, width, axis)
        return kept, lax.dynamic_slice_in_dim(part, (1 - mine) * width, width, axis)

    def halves(self, part, step):
        kept, sent = self.cuts(part, step)
        return kept, self.send(sent, step)


    def halves_far(self, part):
        deep, mine = self.items // 4, self.index // 4
        part = part.reshape((deep,) + part.shape[len(self.far) :])

        def cut(spot):
            return lax.dynamic_slice_in_dim(part, spot, 1, 0)

        return cut(mine), [swap_items(cut(mine ^ apart), self.items, 4 * apart) for apart in range(1, deep)]


def flat(whole):
    return whole.reshape(-1, whole.shape[-1])


def add(kept, other):
    return (kept.astype(jnp.float32) + other.astype(jnp.float32)).astype(jnp.bfloat16)


def own_lanes(values, head):
    lanes = lax.broadcasted_iota(jnp.int32, values.shape, 1)
    return jnp.where(lanes // HEAD == head, values, jnp.zeros_like(values))


def dot_nt(left, right):
    return lax.dot_general(left, right, (((1,), (1,)), ((), ())), preferred_element_type=jnp.float32)


def dot_tn(left, right):
    return lax.dot_general(left, right, (((0,), (0,)), ((), ())), preferred_element_type=jnp.float32)


def dot_nn(left, right):
    return jnp.dot(left, right, preferred_element_type=jnp.float32)


def turned(values):
    return values.astype(jnp.float32).T


def key_bias(where_ref, length):
    places = lax.broadcasted_iota(jnp.int32, (length, 1), 0) + where_ref[1]
    places = jnp.where(places < length, places, places - length)
    return jnp.where(places < where_ref[0], 0.0, -1000000000.0)


def attend_kernel(count_ref, q_ref, k_ref, v_ref, out_ref, log_ref):
    keys, values = k_ref[...], turned(v_ref[...])
    bias = key_bias(count_ref, keys.shape[0])
    lanes = lax.broadcasted_iota(jnp.int32, values.shape, 0)
    total = 0.0
    for head in range(out_ref.shape[1] // HEAD):
        scores = dot_nt(keys, own_lanes(q_ref[...], head)) + bias
        largest = jnp.max(scores, 0, keepdims=True)
        shifted = jnp.exp(scores - largest)
        summed = jnp.sum(shifted, 0, keepdims=True)
        head_values = jnp.where(lanes // HEAD == head, values, 0.0).astype(jnp.bfloat16)
        total = total + dot_nn(head_values, shifted.astype(jnp.bfloat16)) * (1.0 / summed)
        log_ref[0, head : head + 1, :] = largest + jnp.log(summed)
    out_ref[...] = total.T.astype(jnp.bfloat16)


def attend(where, qkv, part):
    length, groups = qkv.shape[0], qkv.shape[1] // 384
    rows, width = length // 2, groups * 128
    return pl.pallas_call(
        attend_kernel,
        grid=(groups,),
        in_specs=[
            pl.BlockSpec(memory_space=pltpu.SMEM),
            pl.BlockSpec((rows, 128), lambda g: (part, g)),
            pl.BlockSpec((length, 128), lambda g: (0, groups + g)),
            pl.BlockSpec((length, 128), lambda g: (0, 2 * groups + g)),
        ],
        out_specs=[
            pl.BlockSpec((rows, 128), lambda g: (0, g)),
            pl.BlockSpec((1, 128 // HEAD, rows), lambda g: (g, 0, 0)),
        ],
        out_shape=[
            jax.ShapeDtypeStruct((rows, width), jnp.bfloat16),
            jax.ShapeDtypeStruct((groups, 128 // HEAD, rows), jnp.float32),
        ],
        compiler_params=pltpu.CompilerParams(vmem_limit_bytes=VMEM),
        cost_estimate=pl.CostEstimate(flops=4 * rows * length * width, bytes_accessed=4 * length * width, transcendentals=rows * length),
        name="attend",
    )(where, qkv, qkv, qkv)


def attend_back_kernel(where_ref, q_ref, k_ref, v_ref, out_ref, log_ref, grad_ref, *refs):
    keys, values = k_ref[...], v_ref[...]
    dq_ref, dk_ref, dv_ref = refs[-3:]
    bias = key_bias(where_ref, keys.shape[0])
    turned_keys = turned(keys)
    lanes = lax.broadcasted_iota(jnp.int32, turned_keys.shape, 0)
    weighed = (grad_ref[...].astype(jnp.float32) * out_ref[...].astype(jnp.float32)).T
    grad_q = 0.0
    grad_k, grad_v = [ref[...] for ref in refs[:-3]] or (0.0, 0.0)
    for head in range(dq_ref.shape[1] // HEAD):
        q_head = own_lanes(q_ref[...], head)
        grad_head = own_lanes(grad_ref[...], head)
        delta = jnp.sum(weighed[head * HEAD : (head + 1) * HEAD], 0, keepdims=True)
        scores = dot_nt(keys, q_head) + bias
        chances = jnp.exp(scores - log_ref[0, head : head + 1, :])
        grad_scores = (chances * (dot_nt(values, grad_head) - delta)).astype(jnp.bfloat16)
        head_keys = jnp.where(lanes // HEAD == head, turned_keys, 0.0).astype(jnp.bfloat16)
        grad_q = grad_q + dot_nn(head_keys, grad_scores)
        grad_k = grad_k + dot_nn(grad_scores, q_head)
        grad_v = grad_v + dot_nn(chances.astype(jnp.bfloat16), grad_head)
    dq_ref[...] = grad_q.T.astype(jnp.bfloat16)
    dk_ref[...] = grad_k.astype(dk_ref.dtype)
    dv_ref[...] = grad_v.astype(dv_ref.dtype)


def attend_back(where, qkv, attended, logs, grad, part, *sums):
    length, groups = qkv.shape[0], qkv.shape[1] // 384
    rows, width = grad.shape
    kind = jnp.bfloat16 if sums else jnp.float32
    tall = pl.BlockSpec((length, 128), lambda g: (0, g))
    wide = pl.BlockSpec((rows, 128), lambda g: (0, g))
    return pl.pallas_call(
        attend_back_kernel,
        grid=(groups,),
        in_specs=[
            pl.BlockSpec(memory_space=pltpu.SMEM),
            pl.BlockSpec((rows, 128), lambda g: (part, g)),
            pl.BlockSpec((length, 128), lambda g: (0, groups + g)),
            pl.BlockSpec((length, 128), lambda g: (0, 2 * groups + g)),
            wide,
            pl.BlockSpec((1, 128 // HEAD, rows), lambda g: (g, 0, 0)),
            wide,
        ]
        + [tall] * len(sums),
        out_specs=[wide, tall, tall],
        out_shape=[
            jax.ShapeDtypeStruct((rows, width), jnp.bfloat16),
            jax.ShapeDtypeStruct((length, width), kind),
            jax.ShapeDtypeStruct((length, width), kind),
        ],
        compiler_params=pltpu.CompilerParams(vmem_limit_bytes=VMEM),
        cost_estimate=pl.CostEstimate(flops=4 * rows * length * width, bytes_accessed=4 * length * width, transcendentals=rows * length),
        name="attend_back",
    )(where, qkv, qkv, qkv, attended, logs, grad, *sums)


def by_heads(
    items,
    patches,
    grid,
    norm_attn,
    w_query,
    w_key,
    w_value,
    w_out,
    norm_mlp,
    w_gate,
    w_up,
    w_down,
    cotangent,
):
    place = Place(items)
    block, far, y, core = place.block, place.far, place.levels - 2, place.levels - 1
    row_count, model_width = patches.shape[1:]
    half = model_width // 2
    count = (grid[0, 0] * grid[0, 1]).astype(jnp.int32)
    where = jnp.stack([count, block * row_count])
    own_rows, own_cot = patches[0], cotangent[0]
    shard_rows, down_rows = w_query.shape[0], w_down.shape[0]

    def advance(held, steps):
        moved = [whole if step is None else place.send(whole, step) for whole, step in zip(held, steps)]
        moved = after(*moved)
        return [
            other if step is None else place.meet(whole, other, step)
            for whole, other, step in zip(held, moved, steps)
        ]

    other_rows = swap_blocks(own_rows)
    w_qkv = sum(
        jnp.pad(shard, ((0, 0), (which * half, (2 - which) * half)))
        for which, shard in enumerate((w_query, w_key, w_value))
    )
    down = jnp.concatenate([w_down, w_out], 0)
    w_qkv, gate, up, down = [place.shaped(shard) for shard in (w_qkv, w_gate, w_up, down)]

    far_qkv, down_blk, gate, up = after(place.send_far(w_qkv), place.send(down, "blk"), gate, up)
    w_qkv = place.meet_far(w_qkv, far_qkv)
    down = place.meet(down, down_blk, "blk")
    down, out = down[..., :down_rows, :], down[..., down_rows:, :]
    qkv_y, down_y = place.send(w_qkv, y), place.send(down, y)
    gate, up = advance([gate, up], [far[0], far[0]])
    gate_far, up_far = place.send(gate, far[1]), place.send(up, far[1])
    qkv_y, down_y, gate_far, up_far, out = after(qkv_y, down_y, gate_far, up_far, out)
    w_qkv = place.meet(w_qkv, qkv_y, y)
    down = place.meet(down, down_y, y)
    gate, up = place.meet(gate, gate_far, far[1]), place.meet(up, up_far, far[1])
    for step in far[2:]:
        gate, up, out = advance([gate, up, out], [step] * 3)
    w_qkv, out = advance([w_qkv, out], [core, far[0]])
    w_qkv = flat(w_qkv)

    gate_blk, up_y, out_far = place.send(gate, "blk"), place.send(up, y), place.send(out, far[1])
    down_far = place.send(down, far[0])
    all_rows = jnp.concatenate([own_rows, other_rows], 0)
    all_normed = rms_norm(all_rows.astype(jnp.float32), norm_attn).astype(jnp.bfloat16)
    w_qkv, gate_blk, up_y = after(w_qkv, gate_blk, up_y)
    gate = place.meet(gate, gate_blk, "blk")
    up = place.meet(up, up_y, y)
    gate_y, up_blk = place.send(gate, y), place.send(up, "blk")
    qkv = dot_nn(all_normed, w_qkv).astype(jnp.bfloat16)
    attended_there, logs_there = attend(where, qkv, 1)
    attended_there, qkv_here, out_far = after(attended_there, qkv, out_far)
    out = place.meet(out, out_far, far[1])
    attended_other = swap_blocks(attended_there)
    attended_here, logs_here = attend(where, qkv_here, 0)
    out_y = place.send(out, y)
    attended_here, down_far = after(attended_here, down_far)
    down = place.meet(down, down_far, far[0])
    down_far = place.send(down, far[1])
    attended_other, out_y = after(attended_other, out_y)
    attended = join(attended_here, attended_other, 1, block)
    out = place.meet(out, out_y, y)
    gate = place.meet(gate, gate_y, y)
    up = place.meet(up, up_blk, "blk")
    full_out, full_gate, full_up = [
        flat(place.meet(whole, place.send(whole, core), core)) for whole in (out, gate, up)
    ]
    patch_rows = own_rows.astype(jnp.float32)
    middle = patch_rows + dot_nn(attended, full_out)
    normed_mlp = rms_norm(middle, norm_mlp).astype(jnp.bfloat16)
    gate_in = dot_nn(normed_mlp, full_gate)
    upward = dot_nn(normed_mlp, full_up)
    activated = jax.nn.gelu(gate_in, approximate=True)
    hidden = (activated * upward).astype(jnp.bfloat16)
    hidden, down_far = after(hidden, down_far)
    down = place.meet(down, down_far, far[1])
    for step in far[2:]:
        (down,) = advance([down], [step])
    full_down = flat(place.meet(down, place.send(down, core), core))
    output = (middle + dot_nn(hidden, full_down)).astype(jnp.bfloat16)
    grad_down = dot_tn(hidden, own_cot).astype(jnp.bfloat16)
    core_down = place.halves(place.part_of(grad_down, down_rows), core)
    grad_hidden = dot_nt(own_cot, full_down)
    unused_gelu, gelu_back = jax.vjp(lambda inner: jax.nn.gelu(inner, approximate=True), gate_in)
    grad_gate_in = gelu_back(grad_hidden * upward)[0].astype(jnp.bfloat16)
    grad_upward = (grad_hidden * activated).astype(jnp.bfloat16)
    grad_normed_mlp = dot_nt(grad_gate_in, full_gate) + dot_nt(grad_upward, full_up)
    grad_normed_mlp, core_down = after(grad_normed_mlp, core_down)
    far_down = place.halves(add(*core_down), far[-1])
    unused_norm, second_back = jax.vjp(rms_norm, middle, norm_mlp)
    grad_middle_part, gain_mlp = second_back(grad_normed_mlp)
    grad_middle = own_cot.astype(jnp.float32) + grad_middle_part
    branch_grad = grad_middle.astype(jnp.bfloat16)
    grad_attended = dot_nt(branch_grad, full_out).astype(jnp.bfloat16)
    heads_here = lax.dynamic_slice_in_dim(grad_attended, block * half, half, 1)
    heads_sent = lax.dynamic_slice_in_dim(grad_attended, (1 - block) * half, half, 1)
    heads_there = swap_blocks(heads_sent)
    normed_mlp, attended, heads_sent = after(normed_mlp, attended, heads_sent)
    grad_gate = dot_tn(normed_mlp, grad_gate_in).astype(jnp.bfloat16)
    grad_up = dot_tn(normed_mlp, grad_upward).astype(jnp.bfloat16)
    grad_out = dot_tn(attended, branch_grad).astype(jnp.bfloat16)
    cores = [place.halves(place.part_of(grad, shard_rows), core) for grad in (grad_gate, grad_up, grad_out)]
    part_gate, part_up, part_out = [add(*pair) for pair in cores]

    near = far[::-1]
    wide = place.halves(part_gate, y), place.halves(part_up, "blk"), place.halves(part_out, "blk")
    heads_here, unused_out = after(heads_here, part_out)
    queries_here, *sums = attend_back(where, qkv, attended_here, logs_here, heads_here, 0)
    sums, far_down, heads_there = after(sums, far_down, heads_there)
    far_down = place.halves(add(*far_down), near[1])
    queries_there, grad_keys, grad_values = attend_back(where, qkv, attended_there, logs_there, heads_there, 1, *sums)
    queries_there, grad_keys, grad_values, wide = after(queries_there, grad_keys, grad_values, wide)
    part_gate, part_up, part_out = [add(*pair) for pair in wide]

    wide = place.halves(part_gate, "blk"), place.halves(part_up, y)
    grad_queries = jnp.concatenate([queries_here, queries_there], 0)
    grad_qkv = jnp.concatenate([grad_queries, grad_keys, grad_values], 1)
    grad_w_qkv = dot_tn(all_normed, grad_qkv).astype(jnp.bfloat16)
    core_qkv = place.halves(place.part_of(grad_w_qkv, shard_rows), core)
    grad_all_normed = dot_nt(grad_qkv, w_qkv)
    unused_all, gain_back = jax.vjp(lambda gain: rms_norm(all_rows.astype(jnp.float32), gain), norm_attn)
    gains = jnp.stack([gain_back(grad_all_normed)[0], gain_mlp])
    core_qkv, wide, far_down, gains_core = after(core_qkv, wide, far_down, place.send(gains, core))
    gains = gains + gains_core
    part_qkv, part_down = add(*core_qkv), add(*far_down)
    part_gate = jnp.concatenate([add(*pair) for pair in wide], -1)
    out_y = place.halves(part_out, y)

    rows_other = swap_blocks(grad_all_normed[row_count:].astype(jnp.bfloat16))
    moving = place.halves(part_qkv, y), place.halves(part_gate, near[0])
    moving, gains_y = after(moving, place.send(gains, y))
    part_out = add(*out_y)
    gains = gains + gains_y
    part_qkv, part_gate = [add(*pair) for pair in moving]

    moving = place.halves(part_qkv, near[0]), place.halves(part_gate, near[1]), place.halves(part_down, y)
    out_far = place.halves(part_out, near[0])
    rows_other, moving, gains_far, out_far = after(rows_other, moving, place.send(gains, near[0]), out_far)
    part_out = add(*out_far)
    gains = gains + gains_far
    part_qkv, part_gate, part_down = [add(*pair) for pair in moving]

    for step in near[2:]:
        part_gate, part_down = [add(*place.halves(part, step)) for part in (part_gate, part_down)]
    part_down = add(*place.halves(part_down, "blk"))
    for step in near[1:]:
        part_out = add(*place.halves(part_out, step))
    for step in near[1:]:
        part_qkv = add(*place.halves(part_qkv, step))
        gains = gains + place.send(gains, step)
    gains = gains + swap_blocks(gains)
    grad_normed = grad_all_normed[:row_count] + rows_other.astype(jnp.float32)
    unused_first, first_back = jax.vjp(rms_norm, patch_rows, norm_attn)
    grad_rows_part, unused_gain = first_back(grad_normed)
    grad_patches = (grad_middle + grad_rows_part).astype(jnp.bfloat16)
    shard_qkv, shard_gate, shard_down = [flat(part).astype(jnp.float32) for part in (part_qkv, part_gate, part_down)]
    inner = w_gate.shape[1]
    return (
        output[None],
        grad_patches[None],
        gains[0],
        shard_qkv[:, :half],
        shard_qkv[:, half : 2 * half],
        shard_qkv[:, 2 * half :],
        flat(part_out).astype(jnp.float32),
        gains[1],
        shard_gate[:, :inner],
        shard_gate[:, inner : 2 * inner],
        shard_down,
    )


def local(items, blocks, patches, *rest):
    items_here, row_count, model_width = patches.shape
    fits = (
        blocks == 2
        and items_here == 1
        and items >= 16
        and items & (items - 1) == 0
        and row_count % 128 == 0
        and model_width % 256 == 0
    )
    if fits:
        return by_heads(items, patches, *rest)
    return general(patches, *rest)


def solution(mesh):
    placed = (
        P("items", "blk", None),
        P("items", None),
        P(),
        P("items", "blk"),
        P("items", "blk"),
        P("items", "blk"),
        P("items", "blk"),
        P(),
        P("items", "blk"),
        P("items", "blk"),
        P("items", "blk"),
        P("items", "blk", None),
    )
    return jax.shard_map(
        functools.partial(local, mesh.shape["items"], mesh.shape["blk"]),
        mesh=mesh,
        in_specs=placed,
        out_specs=(
            P("items", "blk", None),
            P("items", "blk", None),
            P(),
            P("items", "blk"),
            P("items", "blk"),
            P("items", "blk"),
            P("items", "blk"),
            P(),
            P("items", "blk"),
            P("items", "blk"),
            P("items", "blk"),
        ),
        check_vma=False,
    )
```

```python
import functools

import jax
import jax.numpy as jnp
from jax import lax
from jax.experimental import pallas as pl
from jax.experimental.pallas import tpu as pltpu
from jax.sharding import PartitionSpec as P

HEAD = 64


EPSILON = 1e-06


def rms_norm(values, gain):
    return values * lax.rsqrt(jnp.mean(values * values, -1, keepdims=True) + EPSILON) * gain


def product(formula, left, right):
    return jnp.einsum(formula, left, right, preferred_element_type=jnp.float32)


def masked_scores(query_heads, key_part, first_key, counts):
    scores = product("iqhd,ikhd->ihqk", query_heads, key_part)
    places = first_key + jnp.arange(key_part.shape[1], dtype=jnp.int32)
    allowed = places[None, :] < counts[:, None]
    return jnp.where(allowed[:, None, None, :], scores, -1000000000.0)


def general(
    patches,
    grid,
    norm_attn,
    w_query,
    w_key,
    w_value,
    w_out,
    norm_mlp,
    w_gate,
    w_up,
    w_down,
    cotangent,
):
    columns = (
        lax.all_gather(w_query, "blk", axis=1, tiled=True),
        lax.all_gather(w_key, "blk", axis=1, tiled=True),
        lax.all_gather(w_value, "blk", axis=1, tiled=True),
        lax.all_gather(w_out, "blk", axis=1, tiled=True),
        lax.all_gather(w_gate, "blk", axis=1, tiled=True),
        lax.all_gather(w_up, "blk", axis=1, tiled=True),
        lax.all_gather(w_down, "blk", axis=1, tiled=True),
    )
    full_query, full_key, full_value, full_out, full_gate, full_up, full_down = (
        lax.all_gather(columns[0], "items", axis=0, tiled=True),
        lax.all_gather(columns[1], "items", axis=0, tiled=True),
        lax.all_gather(columns[2], "items", axis=0, tiled=True),
        lax.all_gather(columns[3], "items", axis=0, tiled=True),
        lax.all_gather(columns[4], "items", axis=0, tiled=True),
        lax.all_gather(columns[5], "items", axis=0, tiled=True),
        lax.all_gather(columns[6], "items", axis=0, tiled=True),
    )
    items_here, row_count, model_width = patches.shape
    head_count = model_width // HEAD
    blocks = lax.axis_size("blk")
    counts = grid[:, 0] * grid[:, 1]
    patch_rows = patches.astype(jnp.float32)
    normed = rms_norm(patch_rows, norm_attn).astype(jnp.bfloat16)
    queries = product("ird,de->ire", normed, full_query).astype(jnp.bfloat16)
    key_rows = product("ird,de->ire", normed, full_key).astype(jnp.bfloat16)
    value_rows = product("ird,de->ire", normed, full_value).astype(jnp.bfloat16)
    query_heads = queries.reshape(items_here, row_count, head_count, HEAD)

    def split_part(piece, shard_index):
        part_rows = lax.dynamic_slice_in_dim(piece, shard_index * row_count, row_count, 1)
        return part_rows.reshape(items_here, row_count, head_count, HEAD)

    stat_shape = (items_here, head_count, row_count)
    start_stats = (jnp.full(stat_shape, -1e30, jnp.float32), jnp.zeros(stat_shape, jnp.float32))
    carried = start_stats
    key_piece = lax.all_gather(key_rows, "blk", axis=1, tiled=True)
    shards = key_piece.shape[1] // row_count

    def stats_one_shard(running, shard_index):
        running_max, running_sum = running
        key_part = split_part(key_piece, shard_index)
        scores = masked_scores(query_heads, key_part, shard_index * row_count, counts)
        new_max = jnp.maximum(running_max, jnp.max(scores, -1))
        new_sum = running_sum * jnp.exp(running_max - new_max) + jnp.sum(
            jnp.exp(scores - new_max[..., None]), -1
        )
        return ((new_max, new_sum), None)

    carried, unused = lax.scan(stats_one_shard, carried, jnp.arange(shards, dtype=jnp.int32))
    totals = carried
    log_total = totals[0] + jnp.log(totals[1])
    start_values = jnp.zeros((items_here, head_count, row_count, HEAD), jnp.float32)
    carried = start_values
    values_key_piece = lax.all_gather(key_rows, "blk", axis=1, tiled=True)
    value_piece = lax.all_gather(value_rows, "blk", axis=1, tiled=True)
    shards = values_key_piece.shape[1] // row_count

    def values_one_shard(accumulated, shard_index):
        key_part = split_part(values_key_piece, shard_index)
        value_part = split_part(value_piece, shard_index)
        scores = masked_scores(query_heads, key_part, shard_index * row_count, counts)
        weights_low = jnp.exp(scores - log_total[..., None]).astype(jnp.bfloat16)
        return (accumulated + product("ihqk,ikhd->ihqd", weights_low, value_part), None)

    carried, unused = lax.scan(values_one_shard, carried, jnp.arange(shards, dtype=jnp.int32))
    attended = carried.transpose(0, 2, 1, 3).reshape(items_here, row_count, model_width)
    attended_low = attended.astype(jnp.bfloat16)
    middle = patch_rows + product("ird,de->ire", attended_low, full_out)
    normed_mlp = rms_norm(middle, norm_mlp).astype(jnp.bfloat16)
    gate_in = product("ird,df->irf", normed_mlp, full_gate)
    upward = product("ird,df->irf", normed_mlp, full_up)
    activated = jax.nn.gelu(gate_in, approximate=True)
    hidden = (activated * upward).astype(jnp.bfloat16)
    output = (middle + product("irf,fd->ird", hidden, full_down)).astype(jnp.bfloat16)
    grad_down = product("irf,ird->fd", hidden, cotangent)
    grad_hidden = product("ird,fd->irf", cotangent, full_down)
    unused_gelu, gelu_back = jax.vjp(lambda inner: jax.nn.gelu(inner, approximate=True), gate_in)
    grad_gate_in = gelu_back(grad_hidden * upward)[0].astype(jnp.bfloat16)
    grad_upward = (grad_hidden * activated).astype(jnp.bfloat16)
    grad_gate = product("ird,irf->df", normed_mlp, grad_gate_in)
    grad_up = product("ird,irf->df", normed_mlp, grad_upward)
    grad_normed_mlp = product("irf,df->ird", grad_gate_in, full_gate) + product(
        "irf,df->ird", grad_upward, full_up
    )
    unused_norm, second_back = jax.vjp(rms_norm, middle, norm_mlp)
    grad_middle_part, grad_norm_mlp = second_back(grad_normed_mlp)
    grad_middle = cotangent.astype(jnp.float32) + grad_middle_part
    branch_grad = grad_middle.astype(jnp.bfloat16)
    grad_out = product("ird,ire->de", attended_low, branch_grad)
    grad_attended = product("ire,de->ird", branch_grad, full_out).astype(jnp.bfloat16)
    grad_heads = grad_attended.reshape(items_here, row_count, head_count, HEAD)
    delta = jnp.einsum(
        "iqhd,iqhd->ihq",
        grad_heads.astype(jnp.float32),
        attended.reshape(items_here, row_count, head_count, HEAD),
    )
    gathered_keys, gathered_values = (
        lax.all_gather(key_rows, "blk", axis=1, tiled=True),
        lax.all_gather(value_rows, "blk", axis=1, tiled=True),
    )
    query_start = jnp.zeros((items_here, row_count, head_count, HEAD), jnp.float32)

    def back_shard(grad_query, shard_index):
        key_part = split_part(gathered_keys, shard_index)
        value_part = split_part(gathered_values, shard_index)
        scores = masked_scores(query_heads, key_part, shard_index * row_count, counts)
        chances = jnp.exp(scores - log_total[..., None])
        grad_chances = product("iqhd,ikhd->ihqk", grad_heads, value_part)
        grad_scores = (chances * (grad_chances - delta[..., None])).astype(jnp.bfloat16)
        grad_query = grad_query + product("ihqk,ikhd->iqhd", grad_scores, key_part)
        key_term = product("ihqk,iqhd->ikhd", grad_scores, query_heads)
        value_term = product("ihqk,iqhd->ikhd", chances.astype(jnp.bfloat16), grad_heads)
        return (
            grad_query,
            (
                key_term.reshape(items_here, row_count, model_width),
                value_term.reshape(items_here, row_count, model_width),
            ),
        )

    grad_query, key_value_terms = lax.scan(
        back_shard, query_start, jnp.arange(blocks, dtype=jnp.int32)
    )
    key_sum, value_sum = (
        lax.psum_scatter(
            key_value_terms[0].astype(jnp.bfloat16), "blk", scatter_dimension=0, tiled=True
        ).astype(jnp.float32),
        lax.psum_scatter(
            key_value_terms[1].astype(jnp.bfloat16), "blk", scatter_dimension=0, tiled=True
        ).astype(jnp.float32),
    )
    grad_keys = key_sum[0].astype(jnp.bfloat16)
    grad_values = value_sum[0].astype(jnp.bfloat16)
    grad_queries = grad_query.reshape(items_here, row_count, model_width).astype(jnp.bfloat16)
    grad_wq = product("ird,ire->de", normed, grad_queries)
    grad_wk = product("ird,ire->de", normed, grad_keys)
    grad_wv = product("ird,ire->de", normed, grad_values)
    grad_normed = (
        product("ire,de->ird", grad_queries, full_query)
        + product("ire,de->ird", grad_keys, full_key)
        + product("ire,de->ird", grad_values, full_value)
    )
    unused_first, first_back = jax.vjp(rms_norm, patch_rows, norm_attn)
    grad_rows_part, grad_norm_attn = first_back(grad_normed)
    grad_patches = (grad_middle + grad_rows_part).astype(jnp.bfloat16)
    gain_total = lax.psum((grad_norm_attn, grad_norm_mlp), ("items", "blk"))
    by_rows = (
        lax.psum_scatter(
            grad_wq.astype(jnp.bfloat16), "items", scatter_dimension=0, tiled=True
        ).astype(jnp.float32),
        lax.psum_scatter(
            grad_wk.astype(jnp.bfloat16), "items", scatter_dimension=0, tiled=True
        ).astype(jnp.float32),
        lax.psum_scatter(
            grad_wv.astype(jnp.bfloat16), "items", scatter_dimension=0, tiled=True
        ).astype(jnp.float32),
        lax.psum_scatter(
            grad_out.astype(jnp.bfloat16), "items", scatter_dimension=0, tiled=True
        ).astype(jnp.float32),
        lax.psum_scatter(
            grad_gate.astype(jnp.bfloat16), "items", scatter_dimension=0, tiled=True
        ).astype(jnp.float32),
        lax.psum_scatter(
            grad_up.astype(jnp.bfloat16), "items", scatter_dimension=0, tiled=True
        ).astype(jnp.float32),
        lax.psum_scatter(
            grad_down.astype(jnp.bfloat16), "items", scatter_dimension=0, tiled=True
        ).astype(jnp.float32),
    )
    final_shards = (
        lax.psum_scatter(
            by_rows[0].astype(jnp.bfloat16), "blk", scatter_dimension=1, tiled=True
        ).astype(jnp.float32),
        lax.psum_scatter(
            by_rows[1].astype(jnp.bfloat16), "blk", scatter_dimension=1, tiled=True
        ).astype(jnp.float32),
        lax.psum_scatter(
            by_rows[2].astype(jnp.bfloat16), "blk", scatter_dimension=1, tiled=True
        ).astype(jnp.float32),
        lax.psum_scatter(
            by_rows[3].astype(jnp.bfloat16), "blk", scatter_dimension=1, tiled=True
        ).astype(jnp.float32),
        lax.psum_scatter(
            by_rows[4].astype(jnp.bfloat16), "blk", scatter_dimension=1, tiled=True
        ).astype(jnp.float32),
        lax.psum_scatter(
            by_rows[5].astype(jnp.bfloat16), "blk", scatter_dimension=1, tiled=True
        ).astype(jnp.float32),
        lax.psum_scatter(
            by_rows[6].astype(jnp.bfloat16), "blk", scatter_dimension=1, tiled=True
        ).astype(jnp.float32),
    )
    return (
        output,
        grad_patches,
        gain_total[0],
        final_shards[0],
        final_shards[1],
        final_shards[2],
        final_shards[3],
        gain_total[1],
        final_shards[4],
        final_shards[5],
        final_shards[6],
    )


VMEM = 24 << 20


def swap_items(values, items, bits):
    return lax.ppermute(values, "items", [(place, place ^ bits) for place in range(items)])


def swap_blocks(values):
    return lax.ppermute(values, "blk", [(0, 1), (1, 0)])


def join(own, other, axis, later):
    width = own.shape[axis]
    shape = list(own.shape)
    shape[axis] = 2 * width
    whole = jnp.zeros(shape, own.dtype)
    whole = lax.dynamic_update_slice_in_dim(whole, own, later * width, axis)
    return lax.dynamic_update_slice_in_dim(whole, other, (1 - later) * width, axis)


def after(*values):
    return lax.optimization_barrier(values)


class Place:
    def __init__(self, items):
        self.items = items
        self.levels = items.bit_length() - 1
        self.index = lax.axis_index("items")
        self.block = lax.axis_index("blk")
        self.far = list(range(self.levels - 2))

    def find(self, step):
        if step == "blk":
            return self.levels + 1, self.block
        return step, (self.index >> (self.levels - 1 - step)) & 1

    def shaped(self, shard):
        return shard.reshape((1,) * self.levels + shard.shape)

    def send(self, values, step):
        return swap_blocks(values) if step == "blk" else swap_items(values, self.items, 1 << (self.levels - 1 - step))

    def meet(self, whole, other, step):
        axis, mine = self.find(step)
        return join(whole, other, axis, mine)

    def send_far(self, whole):
        return [swap_items(whole, self.items, 4 * apart) for apart in range(1, self.items // 4)]

    def meet_far(self, whole, others):
        deep, mine = self.items // 4, self.index // 4
        joined = jnp.zeros((deep,) + whole.shape[len(self.far) :], whole.dtype)
        for apart, part in enumerate([whole] + list(others)):
            part = part.reshape((1,) + joined.shape[1:])
            joined = lax.dynamic_update_slice_in_dim(joined, part, mine ^ apart, 0)
        return joined.reshape((2,) * len(self.far) + joined.shape[1:])

    def part_of(self, whole, rows):
        return whole.reshape((2,) * self.levels + (rows, whole.shape[-1]))

    def cuts(self, part, step):
        axis, mine = self.find(step)
        width = part.shape[axis] // 2
        kept = lax.dynamic_slice_in_dim(part, mine * width, width, axis)
        return kept, lax.dynamic_slice_in_dim(part, (1 - mine) * width, width, axis)

    def halves(self, part, step):
        kept, sent = self.cuts(part, step)
        return kept, self.send(sent, step)


    def halves_far(self, part):
        deep, mine = self.items // 4, self.index // 4
        part = part.reshape((deep,) + part.shape[len(self.far) :])

        def cut(spot):
            return lax.dynamic_slice_in_dim(part, spot, 1, 0)

        return cut(mine), [swap_items(cut(mine ^ apart), self.items, 4 * apart) for apart in range(1, deep)]


def flat(whole):
    return whole.reshape(-1, whole.shape[-1])


def add(kept, other):
    return (kept.astype(jnp.float32) + other.astype(jnp.float32)).astype(jnp.bfloat16)


def own_lanes(values, head):
    lanes = lax.broadcasted_iota(jnp.int32, values.shape, 1)
    return jnp.where(lanes // HEAD == head, values, jnp.zeros_like(values))


def dot_nt(left, right):
    return lax.dot_general(left, right, (((1,), (1,)), ((), ())), preferred_element_type=jnp.float32)


def dot_tn(left, right):
    return lax.dot_general(left, right, (((0,), (0,)), ((), ())), preferred_element_type=jnp.float32)


def dot_nn(left, right):
    return jnp.dot(left, right, preferred_element_type=jnp.float32)


def turned(values):
    return values.astype(jnp.float32).T


def key_bias(where_ref, length):
    places = lax.broadcasted_iota(jnp.int32, (length, 1), 0) + where_ref[1]
    places = jnp.where(places < length, places, places - length)
    return jnp.where(places < where_ref[0], 0.0, -1000000000.0)


def attend_kernel(count_ref, q_ref, k_ref, v_ref, out_ref, log_ref):
    keys, values = k_ref[...], turned(v_ref[...])
    bias = key_bias(count_ref, keys.shape[0])
    lanes = lax.broadcasted_iota(jnp.int32, values.shape, 0)
    total = 0.0
    for head in range(out_ref.shape[1] // HEAD):
        scores = dot_nt(keys, own_lanes(q_ref[...], head)) + bias
        largest = jnp.max(scores, 0, keepdims=True)
        shifted = jnp.exp(scores - largest)
        summed = jnp.sum(shifted, 0, keepdims=True)
        head_values = jnp.where(lanes // HEAD == head, values, 0.0).astype(jnp.bfloat16)
        total = total + dot_nn(head_values, shifted.astype(jnp.bfloat16)) * (1.0 / summed)
        log_ref[0, head : head + 1, :] = largest + jnp.log(summed)
    out_ref[...] = total.T.astype(jnp.bfloat16)


def attend(where, qkv, part):
    length, groups = qkv.shape[0], qkv.shape[1] // 384
    rows, width = length // 2, groups * 128
    return pl.pallas_call(
        attend_kernel,
        grid=(groups,),
        in_specs=[
            pl.BlockSpec(memory_space=pltpu.SMEM),
            pl.BlockSpec((rows, 128), lambda g: (part, g)),
            pl.BlockSpec((length, 128), lambda g: (0, groups + g)),
            pl.BlockSpec((length, 128), lambda g: (0, 2 * groups + g)),
        ],
        out_specs=[
            pl.BlockSpec((rows, 128), lambda g: (0, g)),
            pl.BlockSpec((1, 128 // HEAD, rows), lambda g: (g, 0, 0)),
        ],
        out_shape=[
            jax.ShapeDtypeStruct((rows, width), jnp.bfloat16),
            jax.ShapeDtypeStruct((groups, 128 // HEAD, rows), jnp.float32),
        ],
        compiler_params=pltpu.CompilerParams(vmem_limit_bytes=VMEM),
        cost_estimate=pl.CostEstimate(flops=4 * rows * length * width, bytes_accessed=4 * length * width, transcendentals=rows * length),
        name="attend",
    )(where, qkv, qkv, qkv)


def attend_back_kernel(where_ref, q_ref, k_ref, v_ref, out_ref, log_ref, grad_ref, *refs):
    keys, values = k_ref[...], v_ref[...]
    dq_ref, dk_ref, dv_ref = refs[-3:]
    bias = key_bias(where_ref, keys.shape[0])
    turned_keys = turned(keys)
    lanes = lax.broadcasted_iota(jnp.int32, turned_keys.shape, 0)
    weighed = (grad_ref[...].astype(jnp.float32) * out_ref[...].astype(jnp.float32)).T
    grad_q = 0.0
    grad_k, grad_v = [ref[...] for ref in refs[:-3]] or (0.0, 0.0)
    for head in range(dq_ref.shape[1] // HEAD):
        q_head = own_lanes(q_ref[...], head)
        grad_head = own_lanes(grad_ref[...], head)
        delta = jnp.sum(weighed[head * HEAD : (head + 1) * HEAD], 0, keepdims=True)
        scores = dot_nt(keys, q_head) + bias
        chances = jnp.exp(scores - log_ref[0, head : head + 1, :])
        grad_scores = (chances * (dot_nt(values, grad_head) - delta)).astype(jnp.bfloat16)
        head_keys = jnp.where(lanes // HEAD == head, turned_keys, 0.0).astype(jnp.bfloat16)
        grad_q = grad_q + dot_nn(head_keys, grad_scores)
        grad_k = grad_k + dot_nn(grad_scores, q_head)
        grad_v = grad_v + dot_nn(chances.astype(jnp.bfloat16), grad_head)
    dq_ref[...] = grad_q.T.astype(jnp.bfloat16)
    dk_ref[...] = grad_k.astype(dk_ref.dtype)
    dv_ref[...] = grad_v.astype(dv_ref.dtype)


def attend_back(where, qkv, attended, logs, grad, part, *sums):
    length, groups = qkv.shape[0], qkv.shape[1] // 384
    rows, width = grad.shape
    kind = jnp.bfloat16 if sums else jnp.float32
    tall = pl.BlockSpec((length, 128), lambda g: (0, g))
    wide = pl.BlockSpec((rows, 128), lambda g: (0, g))
    return pl.pallas_call(
        attend_back_kernel,
        grid=(groups,),
        in_specs=[
            pl.BlockSpec(memory_space=pltpu.SMEM),
            pl.BlockSpec((rows, 128), lambda g: (part, g)),
            pl.BlockSpec((length, 128), lambda g: (0, groups + g)),
            pl.BlockSpec((length, 128), lambda g: (0, 2 * groups + g)),
            wide,
            pl.BlockSpec((1, 128 // HEAD, rows), lambda g: (g, 0, 0)),
            wide,
        ]
        + [tall] * len(sums),
        out_specs=[wide, tall, tall],
        out_shape=[
            jax.ShapeDtypeStruct((rows, width), jnp.bfloat16),
            jax.ShapeDtypeStruct((length, width), kind),
            jax.ShapeDtypeStruct((length, width), kind),
        ],
        compiler_params=pltpu.CompilerParams(vmem_limit_bytes=VMEM),
        cost_estimate=pl.CostEstimate(flops=rows * length * width, bytes_accessed=4 * length * width, transcendentals=rows * length // 4),
        name="attend_back",
    )(where, qkv, qkv, qkv, attended, logs, grad, *sums)


def by_heads(
    items,
    patches,
    grid,
    norm_attn,
    w_query,
    w_key,
    w_value,
    w_out,
    norm_mlp,
    w_gate,
    w_up,
    w_down,
    cotangent,
):
    place = Place(items)
    block, far, y, core = place.block, place.far, place.levels - 2, place.levels - 1
    row_count, model_width = patches.shape[1:]
    half = model_width // 2
    count = (grid[0, 0] * grid[0, 1]).astype(jnp.int32)
    where = jnp.stack([count, block * row_count])
    own_rows, own_cot = patches[0], cotangent[0]
    shard_rows, down_rows = w_query.shape[0], w_down.shape[0]

    def advance(held, steps):
        moved = [whole if step is None else place.send(whole, step) for whole, step in zip(held, steps)]
        moved = after(*moved)
        return [
            other if step is None else place.meet(whole, other, step)
            for whole, other, step in zip(held, moved, steps)
        ]

    other_rows = swap_blocks(own_rows)
    w_qkv = sum(
        jnp.pad(shard, ((0, 0), (which * half, (2 - which) * half)))
        for which, shard in enumerate((w_query, w_key, w_value))
    )
    down = jnp.concatenate([w_down, w_out], 0)
    w_qkv, gate, up, down = [place.shaped(shard) for shard in (w_qkv, w_gate, w_up, down)]

    far_qkv, down_blk, gate = after(place.send_far(w_qkv), place.send(down, "blk"), gate)
    w_qkv = place.meet_far(w_qkv, far_qkv)
    down = place.meet(down, down_blk, "blk")
    down, out = down[..., :down_rows, :], down[..., down_rows:, :]
    qkv_y, down_y = place.send(w_qkv, y), place.send(down, y)
    gate, up = advance([gate, up], [far[0], far[0]])
    gate_far, up_far = place.send(gate, far[1]), place.send(up, far[1])
    qkv_y, gate_far, up_far, down_y, out = after(qkv_y, gate_far, up_far, down_y, out)
    w_qkv = place.meet(w_qkv, qkv_y, y)
    down = place.meet(down, down_y, y)
    gate, up = place.meet(gate, gate_far, far[1]), place.meet(up, up_far, far[1])
    for step in far[2:]:
        gate, up, out = advance([gate, up, out], [step] * 3)
    w_qkv, out = advance([w_qkv, out], [core, far[0]])
    w_qkv = flat(w_qkv)

    gate_blk, up_y, out_far = place.send(gate, "blk"), place.send(up, y), place.send(out, far[1])
    down_far = place.send(down, far[0])
    all_rows = jnp.concatenate([own_rows, other_rows], 0)
    all_normed = rms_norm(all_rows.astype(jnp.float32), norm_attn).astype(jnp.bfloat16)
    w_qkv, gate_blk, up_y = after(w_qkv, gate_blk, up_y)
    gate = place.meet(gate, gate_blk, "blk")
    up = place.meet(up, up_y, y)
    gate_y, up_blk = place.send(gate, y), place.send(up, "blk")
    qkv = dot_nn(all_normed, w_qkv).astype(jnp.bfloat16)
    attended_there, logs_there = attend(where, qkv, 1)
    attended_there, qkv_here, out_far = after(attended_there, qkv, out_far)
    out = place.meet(out, out_far, far[1])
    attended_other = swap_blocks(attended_there)
    attended_here, logs_here = attend(where, qkv_here, 0)
    out_y = place.send(out, y)
    attended_here, down_far = after(attended_here, down_far)
    down = place.meet(down, down_far, far[0])
    down_far = place.send(down, far[1])
    (attended_other,) = after(attended_other)
    attended = join(attended_here, attended_other, 1, block)
    out = place.meet(out, out_y, y)
    gate = place.meet(gate, gate_y, y)
    up = place.meet(up, up_blk, "blk")
    full_out, full_gate, full_up = [
        flat(place.meet(whole, place.send(whole, core), core)) for whole in (out, gate, up)
    ]
    patch_rows = own_rows.astype(jnp.float32)
    middle = patch_rows + dot_nn(attended, full_out)
    normed_mlp = rms_norm(middle, norm_mlp).astype(jnp.bfloat16)
    gate_in = dot_nn(normed_mlp, full_gate)
    upward = dot_nn(normed_mlp, full_up)
    activated = jax.nn.gelu(gate_in, approximate=True)
    hidden = (activated * upward).astype(jnp.bfloat16)
    hidden, down_far = after(hidden, down_far)
    down = place.meet(down, down_far, far[1])
    for step in far[2:]:
        (down,) = advance([down], [step])
    full_down = flat(place.meet(down, place.send(down, core), core))
    output = (middle + dot_nn(hidden, full_down)).astype(jnp.bfloat16)
    grad_down = dot_tn(hidden, own_cot).astype(jnp.bfloat16)
    core_down = place.halves(place.part_of(grad_down, down_rows), core)
    grad_hidden = dot_nt(own_cot, full_down)
    unused_gelu, gelu_back = jax.vjp(lambda inner: jax.nn.gelu(inner, approximate=True), gate_in)
    grad_gate_in = gelu_back(grad_hidden * upward)[0].astype(jnp.bfloat16)
    grad_upward = (grad_hidden * activated).astype(jnp.bfloat16)
    grad_normed_mlp = dot_nt(grad_gate_in, full_gate) + dot_nt(grad_upward, full_up)
    unused_norm, second_back = jax.vjp(rms_norm, middle, norm_mlp)
    grad_middle_part, gain_mlp = second_back(grad_normed_mlp)
    grad_middle = own_cot.astype(jnp.float32) + grad_middle_part
    branch_grad = grad_middle.astype(jnp.bfloat16)
    grad_attended = dot_nt(branch_grad, full_out).astype(jnp.bfloat16)
    heads_here = lax.dynamic_slice_in_dim(grad_attended, block * half, half, 1)
    heads_sent = lax.dynamic_slice_in_dim(grad_attended, (1 - block) * half, half, 1)
    heads_there = swap_blocks(heads_sent)
    heads_sent, normed_mlp, attended = after(heads_sent, normed_mlp, attended)
    far_down = place.halves(add(*core_down), far[-1])
    grad_gate = dot_tn(normed_mlp, grad_gate_in).astype(jnp.bfloat16)
    grad_up = dot_tn(normed_mlp, grad_upward).astype(jnp.bfloat16)
    grad_out = dot_tn(attended, branch_grad).astype(jnp.bfloat16)
    cores = [place.halves(place.part_of(grad, shard_rows), core) for grad in (grad_gate, grad_up, grad_out)]
    part_gate, part_up, part_out = [add(*pair) for pair in cores]

    near = far[::-1]
    wide = place.halves(part_gate, y), place.halves(part_up, "blk"), place.halves(part_out, "blk")
    heads_here, unused_out = after(heads_here, part_out)
    queries_here, *sums = attend_back(where, qkv, attended_here, logs_here, heads_here, 0)
    sums, heads_there, far_down = after(sums, heads_there, far_down)
    far_down = place.halves(add(*far_down), near[1])
    queries_there, grad_keys, grad_values = attend_back(where, qkv, attended_there, logs_there, heads_there, 1, *sums)
    queries_there, grad_keys, grad_values, wide = after(queries_there, grad_keys, grad_values, wide)
    part_gate, part_up, part_out = [add(*pair) for pair in wide]

    wide = place.halves(part_gate, "blk"), place.halves(part_up, y)
    grad_queries = jnp.concatenate([queries_here, queries_there], 0)
    grad_qkv = jnp.concatenate([grad_queries, grad_keys, grad_values], 1)
    grad_w_qkv = dot_tn(all_normed, grad_qkv).astype(jnp.bfloat16)
    core_qkv = place.halves(place.part_of(grad_w_qkv, shard_rows), core)
    grad_all_normed = dot_nt(grad_qkv, w_qkv)
    unused_all, gain_back = jax.vjp(lambda gain: rms_norm(all_rows.astype(jnp.float32), gain), norm_attn)
    gains = jnp.stack([gain_back(grad_all_normed)[0], gain_mlp])
    core_qkv, wide, far_down, gains_core = after(core_qkv, wide, far_down, place.send(gains, core))
    gains = gains + gains_core
    part_qkv = add(*core_qkv)
    part_gate = jnp.concatenate([add(*pair) for pair in wide], -1)
    out_y = place.halves(part_out, y)

    rows_other = swap_blocks(grad_all_normed[row_count:].astype(jnp.bfloat16))
    moving = place.halves(part_qkv, y), place.halves(part_gate, near[0])
    moving, gains_y = after(moving, place.send(gains, y))
    part_out, part_down = add(*out_y), add(*far_down)
    gains = gains + gains_y
    part_qkv, part_gate = [add(*pair) for pair in moving]

    moving = place.halves(part_qkv, near[0]), place.halves(part_gate, near[1]), place.halves(part_down, y)
    out_far = place.halves(part_out, near[0])
    moving, rows_other, gains_far, out_far = after(moving, rows_other, place.send(gains, near[0]), out_far)
    part_out = add(*out_far)
    gains = gains + gains_far
    part_qkv, part_gate, part_down = [add(*pair) for pair in moving]

    for step in near[2:]:
        part_gate, part_down = [add(*place.halves(part, step)) for part in (part_gate, part_down)]
    part_down = add(*place.halves(part_down, "blk"))
    for step in near[1:]:
        part_out = add(*place.halves(part_out, step))
    for step in near[1:]:
        (pair,) = after(place.halves(part_qkv, step))
        part_qkv = add(*pair)
        gains = gains + place.send(gains, step)
    gains = gains + swap_blocks(gains)
    grad_normed = grad_all_normed[:row_count] + rows_other.astype(jnp.float32)
    unused_first, first_back = jax.vjp(rms_norm, patch_rows, norm_attn)
    grad_rows_part, unused_gain = first_back(grad_normed)
    grad_patches = (grad_middle + grad_rows_part).astype(jnp.bfloat16)
    shard_qkv, shard_gate, shard_down = [flat(part).astype(jnp.float32) for part in (part_qkv, part_gate, part_down)]
    inner = w_gate.shape[1]
    return (
        output[None],
        grad_patches[None],
        gains[0],
        shard_qkv[:, :half],
        shard_qkv[:, half : 2 * half],
        shard_qkv[:, 2 * half :],
        flat(part_out).astype(jnp.float32),
        gains[1],
        shard_gate[:, :inner],
        shard_gate[:, inner : 2 * inner],
        shard_down,
    )


def local(items, blocks, patches, *rest):
    items_here, row_count, model_width = patches.shape
    fits = (
        blocks == 2
        and items_here == 1
        and items >= 16
        and items & (items - 1) == 0
        and row_count % 128 == 0
        and model_width % 256 == 0
    )
    if fits:
        return by_heads(items, patches, *rest)
    return general(patches, *rest)


def solution(mesh):
    placed = (
        P("items", "blk", None),
        P("items", None),
        P(),
        P("items", "blk"),
        P("items", "blk"),
        P("items", "blk"),
        P("items", "blk"),
        P(),
        P("items", "blk"),
        P("items", "blk"),
        P("items", "blk"),
        P("items", "blk", None),
    )
    return jax.shard_map(
        functools.partial(local, mesh.shape["items"], mesh.shape["blk"]),
        mesh=mesh,
        in_specs=placed,
        out_specs=(
            P("items", "blk", None),
            P("items", "blk", None),
            P(),
            P("items", "blk"),
            P("items", "blk"),
            P("items", "blk"),
            P("items", "blk"),
            P(),
            P("items", "blk"),
            P("items", "blk"),
            P("items", "blk"),
        ),
        check_vma=False,
    )
```

```python
import functools

import jax
import jax.numpy as jnp
from jax import lax
from jax.experimental import pallas as pl
from jax.experimental.pallas import tpu as pltpu
from jax.sharding import PartitionSpec as P

HEAD = 64


EPSILON = 1e-06


def rms_norm(values, gain):
    return values * lax.rsqrt(jnp.mean(values * values, -1, keepdims=True) + EPSILON) * gain


def product(formula, left, right):
    return jnp.einsum(formula, left, right, preferred_element_type=jnp.float32)


def masked_scores(query_heads, key_part, first_key, counts):
    scores = product("iqhd,ikhd->ihqk", query_heads, key_part)
    places = first_key + jnp.arange(key_part.shape[1], dtype=jnp.int32)
    allowed = places[None, :] < counts[:, None]
    return jnp.where(allowed[:, None, None, :], scores, -1000000000.0)


def general(
    patches,
    grid,
    norm_attn,
    w_query,
    w_key,
    w_value,
    w_out,
    norm_mlp,
    w_gate,
    w_up,
    w_down,
    cotangent,
):
    columns = (
        lax.all_gather(w_query, "blk", axis=1, tiled=True),
        lax.all_gather(w_key, "blk", axis=1, tiled=True),
        lax.all_gather(w_value, "blk", axis=1, tiled=True),
        lax.all_gather(w_out, "blk", axis=1, tiled=True),
        lax.all_gather(w_gate, "blk", axis=1, tiled=True),
        lax.all_gather(w_up, "blk", axis=1, tiled=True),
        lax.all_gather(w_down, "blk", axis=1, tiled=True),
    )
    full_query, full_key, full_value, full_out, full_gate, full_up, full_down = (
        lax.all_gather(columns[0], "items", axis=0, tiled=True),
        lax.all_gather(columns[1], "items", axis=0, tiled=True),
        lax.all_gather(columns[2], "items", axis=0, tiled=True),
        lax.all_gather(columns[3], "items", axis=0, tiled=True),
        lax.all_gather(columns[4], "items", axis=0, tiled=True),
        lax.all_gather(columns[5], "items", axis=0, tiled=True),
        lax.all_gather(columns[6], "items", axis=0, tiled=True),
    )
    items_here, row_count, model_width = patches.shape
    head_count = model_width // HEAD
    blocks = lax.axis_size("blk")
    counts = grid[:, 0] * grid[:, 1]
    patch_rows = patches.astype(jnp.float32)
    normed = rms_norm(patch_rows, norm_attn).astype(jnp.bfloat16)
    queries = product("ird,de->ire", normed, full_query).astype(jnp.bfloat16)
    key_rows = product("ird,de->ire", normed, full_key).astype(jnp.bfloat16)
    value_rows = product("ird,de->ire", normed, full_value).astype(jnp.bfloat16)
    query_heads = queries.reshape(items_here, row_count, head_count, HEAD)

    def split_part(piece, shard_index):
        part_rows = lax.dynamic_slice_in_dim(piece, shard_index * row_count, row_count, 1)
        return part_rows.reshape(items_here, row_count, head_count, HEAD)

    stat_shape = (items_here, head_count, row_count)
    start_stats = (jnp.full(stat_shape, -1e30, jnp.float32), jnp.zeros(stat_shape, jnp.float32))
    carried = start_stats
    key_piece = lax.all_gather(key_rows, "blk", axis=1, tiled=True)
    shards = key_piece.shape[1] // row_count

    def stats_one_shard(running, shard_index):
        running_max, running_sum = running
        key_part = split_part(key_piece, shard_index)
        scores = masked_scores(query_heads, key_part, shard_index * row_count, counts)
        new_max = jnp.maximum(running_max, jnp.max(scores, -1))
        new_sum = running_sum * jnp.exp(running_max - new_max) + jnp.sum(
            jnp.exp(scores - new_max[..., None]), -1
        )
        return ((new_max, new_sum), None)

    carried, unused = lax.scan(stats_one_shard, carried, jnp.arange(shards, dtype=jnp.int32))
    totals = carried
    log_total = totals[0] + jnp.log(totals[1])
    start_values = jnp.zeros((items_here, head_count, row_count, HEAD), jnp.float32)
    carried = start_values
    values_key_piece = lax.all_gather(key_rows, "blk", axis=1, tiled=True)
    value_piece = lax.all_gather(value_rows, "blk", axis=1, tiled=True)
    shards = values_key_piece.shape[1] // row_count

    def values_one_shard(accumulated, shard_index):
        key_part = split_part(values_key_piece, shard_index)
        value_part = split_part(value_piece, shard_index)
        scores = masked_scores(query_heads, key_part, shard_index * row_count, counts)
        weights_low = jnp.exp(scores - log_total[..., None]).astype(jnp.bfloat16)
        return (accumulated + product("ihqk,ikhd->ihqd", weights_low, value_part), None)

    carried, unused = lax.scan(values_one_shard, carried, jnp.arange(shards, dtype=jnp.int32))
    attended = carried.transpose(0, 2, 1, 3).reshape(items_here, row_count, model_width)
    attended_low = attended.astype(jnp.bfloat16)
    middle = patch_rows + product("ird,de->ire", attended_low, full_out)
    normed_mlp = rms_norm(middle, norm_mlp).astype(jnp.bfloat16)
    gate_in = product("ird,df->irf", normed_mlp, full_gate)
    upward = product("ird,df->irf", normed_mlp, full_up)
    activated = jax.nn.gelu(gate_in, approximate=True)
    hidden = (activated * upward).astype(jnp.bfloat16)
    output = (middle + product("irf,fd->ird", hidden, full_down)).astype(jnp.bfloat16)
    grad_down = product("irf,ird->fd", hidden, cotangent)
    grad_hidden = product("ird,fd->irf", cotangent, full_down)
    unused_gelu, gelu_back = jax.vjp(lambda inner: jax.nn.gelu(inner, approximate=True), gate_in)
    grad_gate_in = gelu_back(grad_hidden * upward)[0].astype(jnp.bfloat16)
    grad_upward = (grad_hidden * activated).astype(jnp.bfloat16)
    grad_gate = product("ird,irf->df", normed_mlp, grad_gate_in)
    grad_up = product("ird,irf->df", normed_mlp, grad_upward)
    grad_normed_mlp = product("irf,df->ird", grad_gate_in, full_gate) + product(
        "irf,df->ird", grad_upward, full_up
    )
    unused_norm, second_back = jax.vjp(rms_norm, middle, norm_mlp)
    grad_middle_part, grad_norm_mlp = second_back(grad_normed_mlp)
    grad_middle = cotangent.astype(jnp.float32) + grad_middle_part
    branch_grad = grad_middle.astype(jnp.bfloat16)
    grad_out = product("ird,ire->de", attended_low, branch_grad)
    grad_attended = product("ire,de->ird", branch_grad, full_out).astype(jnp.bfloat16)
    grad_heads = grad_attended.reshape(items_here, row_count, head_count, HEAD)
    delta = jnp.einsum(
        "iqhd,iqhd->ihq",
        grad_heads.astype(jnp.float32),
        attended.reshape(items_here, row_count, head_count, HEAD),
    )
    gathered_keys, gathered_values = (
        lax.all_gather(key_rows, "blk", axis=1, tiled=True),
        lax.all_gather(value_rows, "blk", axis=1, tiled=True),
    )
    query_start = jnp.zeros((items_here, row_count, head_count, HEAD), jnp.float32)

    def back_shard(grad_query, shard_index):
        key_part = split_part(gathered_keys, shard_index)
        value_part = split_part(gathered_values, shard_index)
        scores = masked_scores(query_heads, key_part, shard_index * row_count, counts)
        chances = jnp.exp(scores - log_total[..., None])
        grad_chances = product("iqhd,ikhd->ihqk", grad_heads, value_part)
        grad_scores = (chances * (grad_chances - delta[..., None])).astype(jnp.bfloat16)
        grad_query = grad_query + product("ihqk,ikhd->iqhd", grad_scores, key_part)
        key_term = product("ihqk,iqhd->ikhd", grad_scores, query_heads)
        value_term = product("ihqk,iqhd->ikhd", chances.astype(jnp.bfloat16), grad_heads)
        return (
            grad_query,
            (
                key_term.reshape(items_here, row_count, model_width),
                value_term.reshape(items_here, row_count, model_width),
            ),
        )

    grad_query, key_value_terms = lax.scan(
        back_shard, query_start, jnp.arange(blocks, dtype=jnp.int32)
    )
    key_sum, value_sum = (
        lax.psum_scatter(
            key_value_terms[0].astype(jnp.bfloat16), "blk", scatter_dimension=0, tiled=True
        ).astype(jnp.float32),
        lax.psum_scatter(
            key_value_terms[1].astype(jnp.bfloat16), "blk", scatter_dimension=0, tiled=True
        ).astype(jnp.float32),
    )
    grad_keys = key_sum[0].astype(jnp.bfloat16)
    grad_values = value_sum[0].astype(jnp.bfloat16)
    grad_queries = grad_query.reshape(items_here, row_count, model_width).astype(jnp.bfloat16)
    grad_wq = product("ird,ire->de", normed, grad_queries)
    grad_wk = product("ird,ire->de", normed, grad_keys)
    grad_wv = product("ird,ire->de", normed, grad_values)
    grad_normed = (
        product("ire,de->ird", grad_queries, full_query)
        + product("ire,de->ird", grad_keys, full_key)
        + product("ire,de->ird", grad_values, full_value)
    )
    unused_first, first_back = jax.vjp(rms_norm, patch_rows, norm_attn)
    grad_rows_part, grad_norm_attn = first_back(grad_normed)
    grad_patches = (grad_middle + grad_rows_part).astype(jnp.bfloat16)
    gain_total = lax.psum((grad_norm_attn, grad_norm_mlp), ("items", "blk"))
    by_rows = (
        lax.psum_scatter(
            grad_wq.astype(jnp.bfloat16), "items", scatter_dimension=0, tiled=True
        ).astype(jnp.float32),
        lax.psum_scatter(
            grad_wk.astype(jnp.bfloat16), "items", scatter_dimension=0, tiled=True
        ).astype(jnp.float32),
        lax.psum_scatter(
            grad_wv.astype(jnp.bfloat16), "items", scatter_dimension=0, tiled=True
        ).astype(jnp.float32),
        lax.psum_scatter(
            grad_out.astype(jnp.bfloat16), "items", scatter_dimension=0, tiled=True
        ).astype(jnp.float32),
        lax.psum_scatter(
            grad_gate.astype(jnp.bfloat16), "items", scatter_dimension=0, tiled=True
        ).astype(jnp.float32),
        lax.psum_scatter(
            grad_up.astype(jnp.bfloat16), "items", scatter_dimension=0, tiled=True
        ).astype(jnp.float32),
        lax.psum_scatter(
            grad_down.astype(jnp.bfloat16), "items", scatter_dimension=0, tiled=True
        ).astype(jnp.float32),
    )
    final_shards = (
        lax.psum_scatter(
            by_rows[0].astype(jnp.bfloat16), "blk", scatter_dimension=1, tiled=True
        ).astype(jnp.float32),
        lax.psum_scatter(
            by_rows[1].astype(jnp.bfloat16), "blk", scatter_dimension=1, tiled=True
        ).astype(jnp.float32),
        lax.psum_scatter(
            by_rows[2].astype(jnp.bfloat16), "blk", scatter_dimension=1, tiled=True
        ).astype(jnp.float32),
        lax.psum_scatter(
            by_rows[3].astype(jnp.bfloat16), "blk", scatter_dimension=1, tiled=True
        ).astype(jnp.float32),
        lax.psum_scatter(
            by_rows[4].astype(jnp.bfloat16), "blk", scatter_dimension=1, tiled=True
        ).astype(jnp.float32),
        lax.psum_scatter(
            by_rows[5].astype(jnp.bfloat16), "blk", scatter_dimension=1, tiled=True
        ).astype(jnp.float32),
        lax.psum_scatter(
            by_rows[6].astype(jnp.bfloat16), "blk", scatter_dimension=1, tiled=True
        ).astype(jnp.float32),
    )
    return (
        output,
        grad_patches,
        gain_total[0],
        final_shards[0],
        final_shards[1],
        final_shards[2],
        final_shards[3],
        gain_total[1],
        final_shards[4],
        final_shards[5],
        final_shards[6],
    )


VMEM = 24 << 20


def swap_items(values, items, bits):
    return lax.ppermute(values, "items", [(place, place ^ bits) for place in range(items)])


def swap_blocks(values):
    return lax.ppermute(values, "blk", [(0, 1), (1, 0)])


def join(own, other, axis, later):
    width = own.shape[axis]
    shape = list(own.shape)
    shape[axis] = 2 * width
    whole = jnp.zeros(shape, own.dtype)
    whole = lax.dynamic_update_slice_in_dim(whole, own, later * width, axis)
    return lax.dynamic_update_slice_in_dim(whole, other, (1 - later) * width, axis)


def after(*values):
    return lax.optimization_barrier(values)


class Place:
    def __init__(self, items):
        self.items = items
        self.levels = items.bit_length() - 1
        self.index = lax.axis_index("items")
        self.block = lax.axis_index("blk")
        self.far = list(range(self.levels - 2))

    def find(self, step):
        if step == "blk":
            return self.levels + 1, self.block
        return step, (self.index >> (self.levels - 1 - step)) & 1

    def shaped(self, shard):
        return shard.reshape((1,) * self.levels + shard.shape)

    def send(self, values, step):
        return swap_blocks(values) if step == "blk" else swap_items(values, self.items, 1 << (self.levels - 1 - step))

    def meet(self, whole, other, step):
        axis, mine = self.find(step)
        return join(whole, other, axis, mine)

    def send_far(self, whole):
        return [swap_items(whole, self.items, 4 * apart) for apart in range(1, self.items // 4)]

    def meet_far(self, whole, others):
        deep, mine = self.items // 4, self.index // 4
        joined = jnp.zeros((deep,) + whole.shape[len(self.far) :], whole.dtype)
        for apart, part in enumerate([whole] + list(others)):
            part = part.reshape((1,) + joined.shape[1:])
            joined = lax.dynamic_update_slice_in_dim(joined, part, mine ^ apart, 0)
        return joined.reshape((2,) * len(self.far) + joined.shape[1:])

    def part_of(self, whole, rows):
        return whole.reshape((2,) * self.levels + (rows, whole.shape[-1]))

    def cuts(self, part, step):
        axis, mine = self.find(step)
        width = part.shape[axis] // 2
        kept = lax.dynamic_slice_in_dim(part, mine * width, width, axis)
        return kept, lax.dynamic_slice_in_dim(part, (1 - mine) * width, width, axis)

    def halves(self, part, step):
        kept, sent = self.cuts(part, step)
        return kept, self.send(sent, step)


    def halves_far(self, part):
        deep, mine = self.items // 4, self.index // 4
        part = part.reshape((deep,) + part.shape[len(self.far) :])

        def cut(spot):
            return lax.dynamic_slice_in_dim(part, spot, 1, 0)

        return cut(mine), [swap_items(cut(mine ^ apart), self.items, 4 * apart) for apart in range(1, deep)]


def flat(whole):
    return whole.reshape(-1, whole.shape[-1])


def add(kept, other):
    return (kept.astype(jnp.float32) + other.astype(jnp.float32)).astype(jnp.bfloat16)


def own_lanes(values, head):
    lanes = lax.broadcasted_iota(jnp.int32, values.shape, 1)
    return jnp.where(lanes // HEAD == head, values, jnp.zeros_like(values))


def dot_nt(left, right):
    return lax.dot_general(left, right, (((1,), (1,)), ((), ())), preferred_element_type=jnp.float32)


def dot_tn(left, right):
    return lax.dot_general(left, right, (((0,), (0,)), ((), ())), preferred_element_type=jnp.float32)


def dot_nn(left, right):
    return jnp.dot(left, right, preferred_element_type=jnp.float32)


def turned(values):
    return values.astype(jnp.float32).T


def key_bias(where_ref, length):
    places = lax.broadcasted_iota(jnp.int32, (length, 1), 0) + where_ref[1]
    places = jnp.where(places < length, places, places - length)
    return jnp.where(places < where_ref[0], 0.0, -1000000000.0)


def attend_kernel(count_ref, q_ref, k_ref, v_ref, out_ref, log_ref):
    keys, values = k_ref[...], turned(v_ref[...])
    bias = key_bias(count_ref, keys.shape[0])
    lanes = lax.broadcasted_iota(jnp.int32, values.shape, 0)
    total = 0.0
    for head in range(out_ref.shape[1] // HEAD):
        scores = dot_nt(keys, own_lanes(q_ref[...], head)) + bias
        largest = jnp.max(scores, 0, keepdims=True)
        shifted = jnp.exp(scores - largest)
        summed = jnp.sum(shifted, 0, keepdims=True)
        head_values = jnp.where(lanes // HEAD == head, values, 0.0).astype(jnp.bfloat16)
        total = total + dot_nn(head_values, shifted.astype(jnp.bfloat16)) * (1.0 / summed)
        log_ref[0, head : head + 1, :] = largest + jnp.log(summed)
    out_ref[...] = total.T.astype(jnp.bfloat16)


def attend(where, qkv, part):
    length, groups = qkv.shape[0], qkv.shape[1] // 384
    rows, width = length // 2, groups * 128
    return pl.pallas_call(
        attend_kernel,
        grid=(groups,),
        in_specs=[
            pl.BlockSpec(memory_space=pltpu.SMEM),
            pl.BlockSpec((rows, 128), lambda g: (part, g)),
            pl.BlockSpec((length, 128), lambda g: (0, groups + g)),
            pl.BlockSpec((length, 128), lambda g: (0, 2 * groups + g)),
        ],
        out_specs=[
            pl.BlockSpec((rows, 128), lambda g: (0, g)),
            pl.BlockSpec((1, 128 // HEAD, rows), lambda g: (g, 0, 0)),
        ],
        out_shape=[
            jax.ShapeDtypeStruct((rows, width), jnp.bfloat16),
            jax.ShapeDtypeStruct((groups, 128 // HEAD, rows), jnp.float32),
        ],
        compiler_params=pltpu.CompilerParams(vmem_limit_bytes=VMEM),
        cost_estimate=pl.CostEstimate(flops=4 * rows * length * width, bytes_accessed=4 * length * width, transcendentals=rows * length),
        name="attend",
    )(where, qkv, qkv, qkv)


def attend_back_kernel(where_ref, q_ref, k_ref, v_ref, out_ref, log_ref, grad_ref, *refs):
    keys, values = k_ref[...], v_ref[...]
    dq_ref, dk_ref, dv_ref = refs[-3:]
    bias = key_bias(where_ref, keys.shape[0])
    turned_keys = turned(keys)
    lanes = lax.broadcasted_iota(jnp.int32, turned_keys.shape, 0)
    weighed = (grad_ref[...].astype(jnp.float32) * out_ref[...].astype(jnp.float32)).T
    grad_q = 0.0
    grad_k, grad_v = [ref[...] for ref in refs[:-3]] or (0.0, 0.0)
    for head in range(dq_ref.shape[1] // HEAD):
        q_head = own_lanes(q_ref[...], head)
        grad_head = own_lanes(grad_ref[...], head)
        delta = jnp.sum(weighed[head * HEAD : (head + 1) * HEAD], 0, keepdims=True)
        scores = dot_nt(keys, q_head) + bias
        chances = jnp.exp(scores - log_ref[0, head : head + 1, :])
        grad_scores = (chances * (dot_nt(values, grad_head) - delta)).astype(jnp.bfloat16)
        head_keys = jnp.where(lanes // HEAD == head, turned_keys, 0.0).astype(jnp.bfloat16)
        grad_q = grad_q + dot_nn(head_keys, grad_scores)
        grad_k = grad_k + dot_nn(grad_scores, q_head)
        grad_v = grad_v + dot_nn(chances.astype(jnp.bfloat16), grad_head)
    dq_ref[...] = grad_q.T.astype(jnp.bfloat16)
    dk_ref[...] = grad_k.astype(dk_ref.dtype)
    dv_ref[...] = grad_v.astype(dv_ref.dtype)


def attend_back(where, qkv, attended, logs, grad, part, *sums):
    length, groups = qkv.shape[0], qkv.shape[1] // 384
    rows, width = grad.shape
    kind = jnp.bfloat16 if sums else jnp.float32
    tall = pl.BlockSpec((length, 128), lambda g: (0, g))
    wide = pl.BlockSpec((rows, 128), lambda g: (0, g))
    return pl.pallas_call(
        attend_back_kernel,
        grid=(groups,),
        in_specs=[
            pl.BlockSpec(memory_space=pltpu.SMEM),
            pl.BlockSpec((rows, 128), lambda g: (part, g)),
            pl.BlockSpec((length, 128), lambda g: (0, groups + g)),
            pl.BlockSpec((length, 128), lambda g: (0, 2 * groups + g)),
            wide,
            pl.BlockSpec((1, 128 // HEAD, rows), lambda g: (g, 0, 0)),
            wide,
        ]
        + [tall] * len(sums),
        out_specs=[wide, tall, tall],
        out_shape=[
            jax.ShapeDtypeStruct((rows, width), jnp.bfloat16),
            jax.ShapeDtypeStruct((length, width), kind),
            jax.ShapeDtypeStruct((length, width), kind),
        ],
        compiler_params=pltpu.CompilerParams(vmem_limit_bytes=VMEM),
        cost_estimate=pl.CostEstimate(flops=rows * length * width, bytes_accessed=4 * length * width, transcendentals=rows * length // 4),
        name="attend_back",
    )(where, qkv, qkv, qkv, attended, logs, grad, *sums)


def by_heads(
    items,
    patches,
    grid,
    norm_attn,
    w_query,
    w_key,
    w_value,
    w_out,
    norm_mlp,
    w_gate,
    w_up,
    w_down,
    cotangent,
):
    place = Place(items)
    block, far, y, core = place.block, place.far, place.levels - 2, place.levels - 1
    row_count, model_width = patches.shape[1:]
    half = model_width // 2
    count = (grid[0, 0] * grid[0, 1]).astype(jnp.int32)
    where = jnp.stack([count, block * row_count])
    own_rows, own_cot = patches[0], cotangent[0]
    shard_rows, down_rows = w_query.shape[0], w_down.shape[0]

    def advance(held, steps):
        moved = [whole if step is None else place.send(whole, step) for whole, step in zip(held, steps)]
        moved = after(*moved)
        return [
            other if step is None else place.meet(whole, other, step)
            for whole, other, step in zip(held, moved, steps)
        ]

    other_rows = swap_blocks(own_rows)
    w_qkv = sum(
        jnp.pad(shard, ((0, 0), (which * half, (2 - which) * half)))
        for which, shard in enumerate((w_query, w_key, w_value))
    )
    down = jnp.concatenate([w_down, w_out], 0)
    w_qkv, gate, up, down = [place.shaped(shard) for shard in (w_qkv, w_gate, w_up, down)]

    far_qkv, down_blk, gate = after(place.send_far(w_qkv), place.send(down, "blk"), gate)
    w_qkv = place.meet_far(w_qkv, far_qkv)
    down = place.meet(down, down_blk, "blk")
    down, out = down[..., :down_rows, :], down[..., down_rows:, :]
    qkv_y, down_y = place.send(w_qkv, y), place.send(down, y)
    gate, up = advance([gate, up], [far[0], far[0]])
    gate_far, up_far = place.send(gate, far[1]), place.send(up, far[1])
    qkv_y, gate_far, up_far, down_y, out = after(qkv_y, gate_far, up_far, down_y, out)
    w_qkv = place.meet(w_qkv, qkv_y, y)
    down = place.meet(down, down_y, y)
    gate, up = place.meet(gate, gate_far, far[1]), place.meet(up, up_far, far[1])
    for step in far[2:]:
        gate, up, out = advance([gate, up, out], [step] * 3)
    w_qkv, out = advance([w_qkv, out], [core, far[0]])
    w_qkv = flat(w_qkv)

    gate_blk, up_y, out_far = place.send(gate, "blk"), place.send(up, y), place.send(out, far[1])
    down_far = place.send(down, far[0])
    all_rows = jnp.concatenate([own_rows, other_rows], 0)
    all_normed = rms_norm(all_rows.astype(jnp.float32), norm_attn).astype(jnp.bfloat16)
    w_qkv, gate_blk, up_y = after(w_qkv, gate_blk, up_y)
    gate = place.meet(gate, gate_blk, "blk")
    up = place.meet(up, up_y, y)
    gate_y, up_blk = place.send(gate, y), place.send(up, "blk")
    qkv = dot_nn(all_normed, w_qkv).astype(jnp.bfloat16)
    attended_there, logs_there = attend(where, qkv, 1)
    attended_there, qkv_here, out_far = after(attended_there, qkv, out_far)
    out = place.meet(out, out_far, far[1])
    attended_other = swap_blocks(attended_there)
    attended_here, logs_here = attend(where, qkv_here, 0)
    out_y = place.send(out, y)
    attended_here, down_far = after(attended_here, down_far)
    down = place.meet(down, down_far, far[0])
    down_far = place.send(down, far[1])
    (attended_other,) = after(attended_other)
    attended = join(attended_here, attended_other, 1, block)
    out = place.meet(out, out_y, y)
    gate = place.meet(gate, gate_y, y)
    up = place.meet(up, up_blk, "blk")
    full_out, full_gate, full_up = [
        flat(place.meet(whole, place.send(whole, core), core)) for whole in (out, gate, up)
    ]
    patch_rows = own_rows.astype(jnp.float32)
    middle = patch_rows + dot_nn(attended, full_out)
    normed_mlp = rms_norm(middle, norm_mlp).astype(jnp.bfloat16)
    gate_in = dot_nn(normed_mlp, full_gate)
    upward = dot_nn(normed_mlp, full_up)
    activated = jax.nn.gelu(gate_in, approximate=True)
    hidden = (activated * upward).astype(jnp.bfloat16)
    hidden, down_far = after(hidden, down_far)
    down = place.meet(down, down_far, far[1])
    for step in far[2:]:
        (down,) = advance([down], [step])
    full_down = flat(place.meet(down, place.send(down, core), core))
    output = (middle + dot_nn(hidden, full_down)).astype(jnp.bfloat16)
    grad_down = dot_tn(hidden, own_cot).astype(jnp.bfloat16)
    core_down = place.halves(place.part_of(grad_down, down_rows), core)
    grad_hidden = dot_nt(own_cot, full_down)
    unused_gelu, gelu_back = jax.vjp(lambda inner: jax.nn.gelu(inner, approximate=True), gate_in)
    grad_gate_in = gelu_back(grad_hidden * upward)[0].astype(jnp.bfloat16)
    grad_upward = (grad_hidden * activated).astype(jnp.bfloat16)
    grad_normed_mlp = dot_nt(grad_gate_in, full_gate) + dot_nt(grad_upward, full_up)
    unused_norm, second_back = jax.vjp(rms_norm, middle, norm_mlp)
    grad_middle_part, gain_mlp = second_back(grad_normed_mlp)
    grad_middle = own_cot.astype(jnp.float32) + grad_middle_part
    branch_grad = grad_middle.astype(jnp.bfloat16)
    grad_attended = dot_nt(branch_grad, full_out).astype(jnp.bfloat16)
    heads_here = lax.dynamic_slice_in_dim(grad_attended, block * half, half, 1)
    heads_sent = lax.dynamic_slice_in_dim(grad_attended, (1 - block) * half, half, 1)
    heads_there = swap_blocks(heads_sent)
    heads_sent, normed_mlp, attended = after(heads_sent, normed_mlp, attended)
    far_down = place.halves(add(*core_down), far[-1])
    grad_gate = dot_tn(normed_mlp, grad_gate_in).astype(jnp.bfloat16)
    grad_up = dot_tn(normed_mlp, grad_upward).astype(jnp.bfloat16)
    grad_out = dot_tn(attended, branch_grad).astype(jnp.bfloat16)
    cores = [place.halves(place.part_of(grad, shard_rows), core) for grad in (grad_gate, grad_up, grad_out)]
    part_gate, part_up, part_out = [add(*pair) for pair in cores]

    near = far[::-1]
    wide = place.halves(part_gate, y), place.halves(part_up, "blk"), place.halves(part_out, "blk")
    heads_here, unused_out = after(heads_here, part_out)
    queries_here, *sums = attend_back(where, qkv, attended_here, logs_here, heads_here, 0)
    sums, heads_there, far_down = after(sums, heads_there, far_down)
    far_down = place.halves(add(*far_down), near[1])
    queries_there, grad_keys, grad_values = attend_back(where, qkv, attended_there, logs_there, heads_there, 1, *sums)
    queries_there, grad_keys, grad_values, wide = after(queries_there, grad_keys, grad_values, wide)
    part_gate, part_up, part_out = [add(*pair) for pair in wide]

    wide = place.halves(part_gate, "blk"), place.halves(part_up, y)
    grad_queries = jnp.concatenate([queries_here, queries_there], 0)
    grad_qkv = jnp.concatenate([grad_queries, grad_keys, grad_values], 1)
    grad_w_qkv = dot_tn(all_normed, grad_qkv).astype(jnp.bfloat16)
    core_qkv = place.halves(place.part_of(grad_w_qkv, shard_rows), core)
    grad_all_normed = dot_nt(grad_qkv, w_qkv)
    unused_all, gain_back = jax.vjp(lambda gain: rms_norm(all_rows.astype(jnp.float32), gain), norm_attn)
    gains = jnp.stack([gain_back(grad_all_normed)[0], gain_mlp])
    core_qkv, wide, far_down, gains_core = after(core_qkv, wide, far_down, place.send(gains, core))
    gains = gains + gains_core
    part_qkv = add(*core_qkv)
    part_gate = jnp.concatenate([add(*pair) for pair in wide], -1)
    out_y = place.halves(part_out, y)

    gains = gains + swap_blocks(gains)
    rows_sent, gains = after(grad_all_normed[row_count:].astype(jnp.bfloat16), gains)
    rows_other = swap_blocks(rows_sent)
    moving = place.halves(part_qkv, y), place.halves(part_gate, near[0])
    part_out = add(*out_y)
    moving, gains_y, out_far = after(moving, place.send(gains, y), place.halves(part_out, near[0]))
    part_out, part_down = add(*out_far), add(*far_down)
    gains = gains + gains_y
    part_qkv, part_gate = [add(*pair) for pair in moving]

    moving = place.halves(part_qkv, near[0]), place.halves(part_gate, near[1]), place.halves(part_down, y)
    out_far = place.halves(part_out, near[1])
    moving, rows_other, gains_far, out_far = after(moving, rows_other, place.send(gains, near[0]), out_far)
    part_out = add(*out_far)
    gains = gains + gains_far
    part_qkv, part_gate, part_down = [add(*pair) for pair in moving]

    for step in near[2:]:
        part_gate, part_down = [add(*place.halves(part, step)) for part in (part_gate, part_down)]
    part_down = add(*place.halves(part_down, "blk"))
    for step in near[2:]:
        part_out = add(*place.halves(part_out, step))
    for step in near[1:]:
        (pair,) = after(place.halves(part_qkv, step))
        part_qkv = add(*pair)
        gains = gains + place.send(gains, step)
    grad_normed = grad_all_normed[:row_count] + rows_other.astype(jnp.float32)
    unused_first, first_back = jax.vjp(rms_norm, patch_rows, norm_attn)
    grad_rows_part, unused_gain = first_back(grad_normed)
    grad_patches = (grad_middle + grad_rows_part).astype(jnp.bfloat16)
    shard_qkv, shard_gate, shard_down = [flat(part).astype(jnp.float32) for part in (part_qkv, part_gate, part_down)]
    inner = w_gate.shape[1]
    return (
        output[None],
        grad_patches[None],
        gains[0],
        shard_qkv[:, :half],
        shard_qkv[:, half : 2 * half],
        shard_qkv[:, 2 * half :],
        flat(part_out).astype(jnp.float32),
        gains[1],
        shard_gate[:, :inner],
        shard_gate[:, inner : 2 * inner],
        shard_down,
    )


def local(items, blocks, patches, *rest):
    items_here, row_count, model_width = patches.shape
    fits = (
        blocks == 2
        and items_here == 1
        and items >= 16
        and items & (items - 1) == 0
        and row_count % 128 == 0
        and model_width % 256 == 0
    )
    if fits:
        return by_heads(items, patches, *rest)
    return general(patches, *rest)


def solution(mesh):
    placed = (
        P("items", "blk", None),
        P("items", None),
        P(),
        P("items", "blk"),
        P("items", "blk"),
        P("items", "blk"),
        P("items", "blk"),
        P(),
        P("items", "blk"),
        P("items", "blk"),
        P("items", "blk"),
        P("items", "blk", None),
    )
    return jax.shard_map(
        functools.partial(local, mesh.shape["items"], mesh.shape["blk"]),
        mesh=mesh,
        in_specs=placed,
        out_specs=(
            P("items", "blk", None),
            P("items", "blk", None),
            P(),
            P("items", "blk"),
            P("items", "blk"),
            P("items", "blk"),
            P("items", "blk"),
            P(),
            P("items", "blk"),
            P("items", "blk"),
            P("items", "blk"),
        ),
        check_vma=False,
    )
```

```python
import functools

import jax
import jax.numpy as jnp
from jax import lax
from jax.experimental import pallas as pl
from jax.experimental.pallas import tpu as pltpu
from jax.sharding import PartitionSpec as P

HEAD = 64


EPSILON = 1e-06


def rms_norm(values, gain):
    return values * lax.rsqrt(jnp.mean(values * values, -1, keepdims=True) + EPSILON) * gain


def product(formula, left, right):
    return jnp.einsum(formula, left, right, preferred_element_type=jnp.float32)


def masked_scores(query_heads, key_part, first_key, counts):
    scores = product("iqhd,ikhd->ihqk", query_heads, key_part)
    places = first_key + jnp.arange(key_part.shape[1], dtype=jnp.int32)
    allowed = places[None, :] < counts[:, None]
    return jnp.where(allowed[:, None, None, :], scores, -1000000000.0)


def general(
    patches,
    grid,
    norm_attn,
    w_query,
    w_key,
    w_value,
    w_out,
    norm_mlp,
    w_gate,
    w_up,
    w_down,
    cotangent,
):
    columns = (
        lax.all_gather(w_query, "blk", axis=1, tiled=True),
        lax.all_gather(w_key, "blk", axis=1, tiled=True),
        lax.all_gather(w_value, "blk", axis=1, tiled=True),
        lax.all_gather(w_out, "blk", axis=1, tiled=True),
        lax.all_gather(w_gate, "blk", axis=1, tiled=True),
        lax.all_gather(w_up, "blk", axis=1, tiled=True),
        lax.all_gather(w_down, "blk", axis=1, tiled=True),
    )
    full_query, full_key, full_value, full_out, full_gate, full_up, full_down = (
        lax.all_gather(columns[0], "items", axis=0, tiled=True),
        lax.all_gather(columns[1], "items", axis=0, tiled=True),
        lax.all_gather(columns[2], "items", axis=0, tiled=True),
        lax.all_gather(columns[3], "items", axis=0, tiled=True),
        lax.all_gather(columns[4], "items", axis=0, tiled=True),
        lax.all_gather(columns[5], "items", axis=0, tiled=True),
        lax.all_gather(columns[6], "items", axis=0, tiled=True),
    )
    items_here, row_count, model_width = patches.shape
    head_count = model_width // HEAD
    blocks = lax.axis_size("blk")
    counts = grid[:, 0] * grid[:, 1]
    patch_rows = patches.astype(jnp.float32)
    normed = rms_norm(patch_rows, norm_attn).astype(jnp.bfloat16)
    queries = product("ird,de->ire", normed, full_query).astype(jnp.bfloat16)
    key_rows = product("ird,de->ire", normed, full_key).astype(jnp.bfloat16)
    value_rows = product("ird,de->ire", normed, full_value).astype(jnp.bfloat16)
    query_heads = queries.reshape(items_here, row_count, head_count, HEAD)

    def split_part(piece, shard_index):
        part_rows = lax.dynamic_slice_in_dim(piece, shard_index * row_count, row_count, 1)
        return part_rows.reshape(items_here, row_count, head_count, HEAD)

    stat_shape = (items_here, head_count, row_count)
    start_stats = (jnp.full(stat_shape, -1e30, jnp.float32), jnp.zeros(stat_shape, jnp.float32))
    carried = start_stats
    key_piece = lax.all_gather(key_rows, "blk", axis=1, tiled=True)
    shards = key_piece.shape[1] // row_count

    def stats_one_shard(running, shard_index):
        running_max, running_sum = running
        key_part = split_part(key_piece, shard_index)
        scores = masked_scores(query_heads, key_part, shard_index * row_count, counts)
        new_max = jnp.maximum(running_max, jnp.max(scores, -1))
        new_sum = running_sum * jnp.exp(running_max - new_max) + jnp.sum(
            jnp.exp(scores - new_max[..., None]), -1
        )
        return ((new_max, new_sum), None)

    carried, unused = lax.scan(stats_one_shard, carried, jnp.arange(shards, dtype=jnp.int32))
    totals = carried
    log_total = totals[0] + jnp.log(totals[1])
    start_values = jnp.zeros((items_here, head_count, row_count, HEAD), jnp.float32)
    carried = start_values
    values_key_piece = lax.all_gather(key_rows, "blk", axis=1, tiled=True)
    value_piece = lax.all_gather(value_rows, "blk", axis=1, tiled=True)
    shards = values_key_piece.shape[1] // row_count

    def values_one_shard(accumulated, shard_index):
        key_part = split_part(values_key_piece, shard_index)
        value_part = split_part(value_piece, shard_index)
        scores = masked_scores(query_heads, key_part, shard_index * row_count, counts)
        weights_low = jnp.exp(scores - log_total[..., None]).astype(jnp.bfloat16)
        return (accumulated + product("ihqk,ikhd->ihqd", weights_low, value_part), None)

    carried, unused = lax.scan(values_one_shard, carried, jnp.arange(shards, dtype=jnp.int32))
    attended = carried.transpose(0, 2, 1, 3).reshape(items_here, row_count, model_width)
    attended_low = attended.astype(jnp.bfloat16)
    middle = patch_rows + product("ird,de->ire", attended_low, full_out)
    normed_mlp = rms_norm(middle, norm_mlp).astype(jnp.bfloat16)
    gate_in = product("ird,df->irf", normed_mlp, full_gate)
    upward = product("ird,df->irf", normed_mlp, full_up)
    activated = jax.nn.gelu(gate_in, approximate=True)
    hidden = (activated * upward).astype(jnp.bfloat16)
    output = (middle + product("irf,fd->ird", hidden, full_down)).astype(jnp.bfloat16)
    grad_down = product("irf,ird->fd", hidden, cotangent)
    grad_hidden = product("ird,fd->irf", cotangent, full_down)
    unused_gelu, gelu_back = jax.vjp(lambda inner: jax.nn.gelu(inner, approximate=True), gate_in)
    grad_gate_in = gelu_back(grad_hidden * upward)[0].astype(jnp.bfloat16)
    grad_upward = (grad_hidden * activated).astype(jnp.bfloat16)
    grad_gate = product("ird,irf->df", normed_mlp, grad_gate_in)
    grad_up = product("ird,irf->df", normed_mlp, grad_upward)
    grad_normed_mlp = product("irf,df->ird", grad_gate_in, full_gate) + product(
        "irf,df->ird", grad_upward, full_up
    )
    unused_norm, second_back = jax.vjp(rms_norm, middle, norm_mlp)
    grad_middle_part, grad_norm_mlp = second_back(grad_normed_mlp)
    grad_middle = cotangent.astype(jnp.float32) + grad_middle_part
    branch_grad = grad_middle.astype(jnp.bfloat16)
    grad_out = product("ird,ire->de", attended_low, branch_grad)
    grad_attended = product("ire,de->ird", branch_grad, full_out).astype(jnp.bfloat16)
    grad_heads = grad_attended.reshape(items_here, row_count, head_count, HEAD)
    delta = jnp.einsum(
        "iqhd,iqhd->ihq",
        grad_heads.astype(jnp.float32),
        attended.reshape(items_here, row_count, head_count, HEAD),
    )
    gathered_keys, gathered_values = (
        lax.all_gather(key_rows, "blk", axis=1, tiled=True),
        lax.all_gather(value_rows, "blk", axis=1, tiled=True),
    )
    query_start = jnp.zeros((items_here, row_count, head_count, HEAD), jnp.float32)

    def back_shard(grad_query, shard_index):
        key_part = split_part(gathered_keys, shard_index)
        value_part = split_part(gathered_values, shard_index)
        scores = masked_scores(query_heads, key_part, shard_index * row_count, counts)
        chances = jnp.exp(scores - log_total[..., None])
        grad_chances = product("iqhd,ikhd->ihqk", grad_heads, value_part)
        grad_scores = (chances * (grad_chances - delta[..., None])).astype(jnp.bfloat16)
        grad_query = grad_query + product("ihqk,ikhd->iqhd", grad_scores, key_part)
        key_term = product("ihqk,iqhd->ikhd", grad_scores, query_heads)
        value_term = product("ihqk,iqhd->ikhd", chances.astype(jnp.bfloat16), grad_heads)
        return (
            grad_query,
            (
                key_term.reshape(items_here, row_count, model_width),
                value_term.reshape(items_here, row_count, model_width),
            ),
        )

    grad_query, key_value_terms = lax.scan(
        back_shard, query_start, jnp.arange(blocks, dtype=jnp.int32)
    )
    key_sum, value_sum = (
        lax.psum_scatter(
            key_value_terms[0].astype(jnp.bfloat16), "blk", scatter_dimension=0, tiled=True
        ).astype(jnp.float32),
        lax.psum_scatter(
            key_value_terms[1].astype(jnp.bfloat16), "blk", scatter_dimension=0, tiled=True
        ).astype(jnp.float32),
    )
    grad_keys = key_sum[0].astype(jnp.bfloat16)
    grad_values = value_sum[0].astype(jnp.bfloat16)
    grad_queries = grad_query.reshape(items_here, row_count, model_width).astype(jnp.bfloat16)
    grad_wq = product("ird,ire->de", normed, grad_queries)
    grad_wk = product("ird,ire->de", normed, grad_keys)
    grad_wv = product("ird,ire->de", normed, grad_values)
    grad_normed = (
        product("ire,de->ird", grad_queries, full_query)
        + product("ire,de->ird", grad_keys, full_key)
        + product("ire,de->ird", grad_values, full_value)
    )
    unused_first, first_back = jax.vjp(rms_norm, patch_rows, norm_attn)
    grad_rows_part, grad_norm_attn = first_back(grad_normed)
    grad_patches = (grad_middle + grad_rows_part).astype(jnp.bfloat16)
    gain_total = lax.psum((grad_norm_attn, grad_norm_mlp), ("items", "blk"))
    by_rows = (
        lax.psum_scatter(
            grad_wq.astype(jnp.bfloat16), "items", scatter_dimension=0, tiled=True
        ).astype(jnp.float32),
        lax.psum_scatter(
            grad_wk.astype(jnp.bfloat16), "items", scatter_dimension=0, tiled=True
        ).astype(jnp.float32),
        lax.psum_scatter(
            grad_wv.astype(jnp.bfloat16), "items", scatter_dimension=0, tiled=True
        ).astype(jnp.float32),
        lax.psum_scatter(
            grad_out.astype(jnp.bfloat16), "items", scatter_dimension=0, tiled=True
        ).astype(jnp.float32),
        lax.psum_scatter(
            grad_gate.astype(jnp.bfloat16), "items", scatter_dimension=0, tiled=True
        ).astype(jnp.float32),
        lax.psum_scatter(
            grad_up.astype(jnp.bfloat16), "items", scatter_dimension=0, tiled=True
        ).astype(jnp.float32),
        lax.psum_scatter(
            grad_down.astype(jnp.bfloat16), "items", scatter_dimension=0, tiled=True
        ).astype(jnp.float32),
    )
    final_shards = (
        lax.psum_scatter(
            by_rows[0].astype(jnp.bfloat16), "blk", scatter_dimension=1, tiled=True
        ).astype(jnp.float32),
        lax.psum_scatter(
            by_rows[1].astype(jnp.bfloat16), "blk", scatter_dimension=1, tiled=True
        ).astype(jnp.float32),
        lax.psum_scatter(
            by_rows[2].astype(jnp.bfloat16), "blk", scatter_dimension=1, tiled=True
        ).astype(jnp.float32),
        lax.psum_scatter(
            by_rows[3].astype(jnp.bfloat16), "blk", scatter_dimension=1, tiled=True
        ).astype(jnp.float32),
        lax.psum_scatter(
            by_rows[4].astype(jnp.bfloat16), "blk", scatter_dimension=1, tiled=True
        ).astype(jnp.float32),
        lax.psum_scatter(
            by_rows[5].astype(jnp.bfloat16), "blk", scatter_dimension=1, tiled=True
        ).astype(jnp.float32),
        lax.psum_scatter(
            by_rows[6].astype(jnp.bfloat16), "blk", scatter_dimension=1, tiled=True
        ).astype(jnp.float32),
    )
    return (
        output,
        grad_patches,
        gain_total[0],
        final_shards[0],
        final_shards[1],
        final_shards[2],
        final_shards[3],
        gain_total[1],
        final_shards[4],
        final_shards[5],
        final_shards[6],
    )


VMEM = 24 << 20


def swap_items(values, items, bits):
    return lax.ppermute(values, "items", [(place, place ^ bits) for place in range(items)])


def swap_blocks(values):
    return lax.ppermute(values, "blk", [(0, 1), (1, 0)])


def join(own, other, axis, later):
    width = own.shape[axis]
    shape = list(own.shape)
    shape[axis] = 2 * width
    whole = jnp.zeros(shape, own.dtype)
    whole = lax.dynamic_update_slice_in_dim(whole, own, later * width, axis)
    return lax.dynamic_update_slice_in_dim(whole, other, (1 - later) * width, axis)


def after(*values):
    return lax.optimization_barrier(values)


class Place:
    def __init__(self, items):
        self.items = items
        self.levels = items.bit_length() - 1
        self.index = lax.axis_index("items")
        self.block = lax.axis_index("blk")
        self.far = list(range(self.levels - 2))

    def find(self, step):
        if step == "blk":
            return self.levels + 1, self.block
        return step, (self.index >> (self.levels - 1 - step)) & 1

    def shaped(self, shard):
        return shard.reshape((1,) * self.levels + shard.shape)

    def send(self, values, step):
        return swap_blocks(values) if step == "blk" else swap_items(values, self.items, 1 << (self.levels - 1 - step))

    def meet(self, whole, other, step):
        axis, mine = self.find(step)
        return join(whole, other, axis, mine)

    def send_far(self, whole):
        return [swap_items(whole, self.items, 4 * apart) for apart in range(1, self.items // 4)]

    def meet_far(self, whole, others):
        deep, mine = self.items // 4, self.index // 4
        joined = jnp.zeros((deep,) + whole.shape[len(self.far) :], whole.dtype)
        for apart, part in enumerate([whole] + list(others)):
            part = part.reshape((1,) + joined.shape[1:])
            joined = lax.dynamic_update_slice_in_dim(joined, part, mine ^ apart, 0)
        return joined.reshape((2,) * len(self.far) + joined.shape[1:])

    def part_of(self, whole, rows):
        return whole.reshape((2,) * self.levels + (rows, whole.shape[-1]))

    def cuts(self, part, step):
        axis, mine = self.find(step)
        width = part.shape[axis] // 2
        kept = lax.dynamic_slice_in_dim(part, mine * width, width, axis)
        return kept, lax.dynamic_slice_in_dim(part, (1 - mine) * width, width, axis)

    def halves(self, part, step):
        kept, sent = self.cuts(part, step)
        return kept, self.send(sent, step)


    def halves_far(self, part):
        deep, mine = self.items // 4, self.index // 4
        part = part.reshape((deep,) + part.shape[len(self.far) :])

        def cut(spot):
            return lax.dynamic_slice_in_dim(part, spot, 1, 0)

        return cut(mine), [swap_items(cut(mine ^ apart), self.items, 4 * apart) for apart in range(1, deep)]


def flat(whole):
    return whole.reshape(-1, whole.shape[-1])


def add(kept, other):
    return (kept.astype(jnp.float32) + other.astype(jnp.float32)).astype(jnp.bfloat16)


def own_lanes(values, head):
    lanes = lax.broadcasted_iota(jnp.int32, values.shape, 1)
    return jnp.where(lanes // HEAD == head, values, jnp.zeros_like(values))


def dot_nt(left, right):
    return lax.dot_general(left, right, (((1,), (1,)), ((), ())), preferred_element_type=jnp.float32)


def dot_tn(left, right):
    return lax.dot_general(left, right, (((0,), (0,)), ((), ())), preferred_element_type=jnp.float32)


def dot_nn(left, right):
    return jnp.dot(left, right, preferred_element_type=jnp.float32)


def turned(values):
    return values.astype(jnp.float32).T


def key_bias(where_ref, length):
    places = lax.broadcasted_iota(jnp.int32, (length, 1), 0) + where_ref[1]
    places = jnp.where(places < length, places, places - length)
    return jnp.where(places < where_ref[0], 0.0, -1000000000.0)


def attend_kernel(count_ref, q_ref, k_ref, v_ref, out_ref, log_ref):
    keys, values = k_ref[...], turned(v_ref[...])
    bias = key_bias(count_ref, keys.shape[0])
    lanes = lax.broadcasted_iota(jnp.int32, values.shape, 0)
    total = 0.0
    for head in range(out_ref.shape[1] // HEAD):
        scores = dot_nt(keys, own_lanes(q_ref[...], head)) + bias
        largest = jnp.max(scores, 0, keepdims=True)
        shifted = jnp.exp(scores - largest)
        summed = jnp.sum(shifted, 0, keepdims=True)
        head_values = jnp.where(lanes // HEAD == head, values, 0.0).astype(jnp.bfloat16)
        total = total + dot_nn(head_values, shifted.astype(jnp.bfloat16)) * (1.0 / summed)
        log_ref[0, head : head + 1, :] = largest + jnp.log(summed)
    out_ref[...] = total.T.astype(jnp.bfloat16)


def attend(where, qkv, part):
    length, groups = qkv.shape[0], qkv.shape[1] // 384
    rows, width = length // 2, groups * 128
    return pl.pallas_call(
        attend_kernel,
        grid=(groups,),
        in_specs=[
            pl.BlockSpec(memory_space=pltpu.SMEM),
            pl.BlockSpec((rows, 128), lambda g: (part, g)),
            pl.BlockSpec((length, 128), lambda g: (0, groups + g)),
            pl.BlockSpec((length, 128), lambda g: (0, 2 * groups + g)),
        ],
        out_specs=[
            pl.BlockSpec((rows, 128), lambda g: (0, g)),
            pl.BlockSpec((1, 128 // HEAD, rows), lambda g: (g, 0, 0)),
        ],
        out_shape=[
            jax.ShapeDtypeStruct((rows, width), jnp.bfloat16),
            jax.ShapeDtypeStruct((groups, 128 // HEAD, rows), jnp.float32),
        ],
        compiler_params=pltpu.CompilerParams(vmem_limit_bytes=VMEM),
        cost_estimate=pl.CostEstimate(flops=4 * rows * length * width, bytes_accessed=4 * length * width, transcendentals=rows * length),
        name="attend",
    )(where, qkv, qkv, qkv)


def attend_back_kernel(where_ref, q_ref, k_ref, v_ref, out_ref, log_ref, grad_ref, *refs):
    keys, values = k_ref[...], v_ref[...]
    dq_ref, dk_ref, dv_ref = refs[-3:]
    bias = key_bias(where_ref, keys.shape[0])
    turned_keys = turned(keys)
    lanes = lax.broadcasted_iota(jnp.int32, turned_keys.shape, 0)
    weighed = (grad_ref[...].astype(jnp.float32) * out_ref[...].astype(jnp.float32)).T
    grad_q = 0.0
    grad_k, grad_v = [ref[...] for ref in refs[:-3]] or (0.0, 0.0)
    for head in range(dq_ref.shape[1] // HEAD):
        q_head = own_lanes(q_ref[...], head)
        grad_head = own_lanes(grad_ref[...], head)
        delta = jnp.sum(weighed[head * HEAD : (head + 1) * HEAD], 0, keepdims=True)
        scores = dot_nt(keys, q_head) + bias
        chances = jnp.exp(scores - log_ref[0, head : head + 1, :])
        grad_scores = (chances * (dot_nt(values, grad_head) - delta)).astype(jnp.bfloat16)
        head_keys = jnp.where(lanes // HEAD == head, turned_keys, 0.0).astype(jnp.bfloat16)
        grad_q = grad_q + dot_nn(head_keys, grad_scores)
        grad_k = grad_k + dot_nn(grad_scores, q_head)
        grad_v = grad_v + dot_nn(chances.astype(jnp.bfloat16), grad_head)
    dq_ref[...] = grad_q.T.astype(jnp.bfloat16)
    dk_ref[...] = grad_k.astype(dk_ref.dtype)
    dv_ref[...] = grad_v.astype(dv_ref.dtype)


def attend_back(where, qkv, attended, logs, grad, part, *sums):
    length, groups = qkv.shape[0], qkv.shape[1] // 384
    rows, width = grad.shape
    kind = jnp.bfloat16 if sums else jnp.float32
    tall = pl.BlockSpec((length, 128), lambda g: (0, g))
    wide = pl.BlockSpec((rows, 128), lambda g: (0, g))
    return pl.pallas_call(
        attend_back_kernel,
        grid=(groups,),
        in_specs=[
            pl.BlockSpec(memory_space=pltpu.SMEM),
            pl.BlockSpec((rows, 128), lambda g: (part, g)),
            pl.BlockSpec((length, 128), lambda g: (0, groups + g)),
            pl.BlockSpec((length, 128), lambda g: (0, 2 * groups + g)),
            wide,
            pl.BlockSpec((1, 128 // HEAD, rows), lambda g: (g, 0, 0)),
            wide,
        ]
        + [tall] * len(sums),
        out_specs=[wide, tall, tall],
        out_shape=[
            jax.ShapeDtypeStruct((rows, width), jnp.bfloat16),
            jax.ShapeDtypeStruct((length, width), kind),
            jax.ShapeDtypeStruct((length, width), kind),
        ],
        compiler_params=pltpu.CompilerParams(vmem_limit_bytes=VMEM),
        cost_estimate=pl.CostEstimate(flops=rows * length * width, bytes_accessed=4 * length * width, transcendentals=rows * length // 4),
        name="attend_back",
    )(where, qkv, qkv, qkv, attended, logs, grad, *sums)


def by_heads(
    items,
    patches,
    grid,
    norm_attn,
    w_query,
    w_key,
    w_value,
    w_out,
    norm_mlp,
    w_gate,
    w_up,
    w_down,
    cotangent,
):
    place = Place(items)
    block, far, y, core = place.block, place.far, place.levels - 2, place.levels - 1
    row_count, model_width = patches.shape[1:]
    half = model_width // 2
    count = (grid[0, 0] * grid[0, 1]).astype(jnp.int32)
    where = jnp.stack([count, block * row_count])
    own_rows, own_cot = patches[0], cotangent[0]
    shard_rows, down_rows = w_query.shape[0], w_down.shape[0]

    def advance(held, steps):
        moved = [whole if step is None else place.send(whole, step) for whole, step in zip(held, steps)]
        moved = after(*moved)
        return [
            other if step is None else place.meet(whole, other, step)
            for whole, other, step in zip(held, moved, steps)
        ]

    other_rows = swap_blocks(own_rows)
    w_qkv = sum(
        jnp.pad(shard, ((0, 0), (which * half, (2 - which) * half)))
        for which, shard in enumerate((w_query, w_key, w_value))
    )
    down = jnp.concatenate([w_down, w_out], 0)
    w_qkv, gate, up, down = [place.shaped(shard) for shard in (w_qkv, w_gate, w_up, down)]

    far_qkv, down_blk, gate = after(place.send_far(w_qkv), place.send(down, "blk"), gate)
    w_qkv = place.meet_far(w_qkv, far_qkv)
    down = place.meet(down, down_blk, "blk")
    down, out = down[..., :down_rows, :], down[..., down_rows:, :]
    qkv_y, down_y = place.send(w_qkv, y), place.send(down, y)
    gate, up = advance([gate, up], [far[0], far[0]])
    gate_far, up_far = place.send(gate, far[1]), place.send(up, far[1])
    qkv_y, gate_far, up_far, down_y, out = after(qkv_y, gate_far, up_far, down_y, out)
    w_qkv = place.meet(w_qkv, qkv_y, y)
    down = place.meet(down, down_y, y)
    gate, up = place.meet(gate, gate_far, far[1]), place.meet(up, up_far, far[1])
    for step in far[2:]:
        gate, up, out = advance([gate, up, out], [step] * 3)
    w_qkv, out = advance([w_qkv, out], [core, far[0]])
    w_qkv = flat(w_qkv)

    gate_blk, up_y, out_far = place.send(gate, "blk"), place.send(up, y), place.send(out, far[1])
    down_far = place.send(down, far[0])
    all_rows = jnp.concatenate([own_rows, other_rows], 0)
    all_normed = rms_norm(all_rows.astype(jnp.float32), norm_attn).astype(jnp.bfloat16)
    w_qkv, gate_blk, up_y = after(w_qkv, gate_blk, up_y)
    gate = place.meet(gate, gate_blk, "blk")
    up = place.meet(up, up_y, y)
    gate_y, up_blk = place.send(gate, y), place.send(up, "blk")
    qkv = dot_nn(all_normed, w_qkv).astype(jnp.bfloat16)
    attended_there, logs_there = attend(where, qkv, 1)
    attended_there, qkv_here, out_far = after(attended_there, qkv, out_far)
    out = place.meet(out, out_far, far[1])
    attended_other = swap_blocks(attended_there)
    attended_here, logs_here = attend(where, qkv_here, 0)
    out_y = place.send(out, y)
    attended_here, down_far = after(attended_here, down_far)
    down = place.meet(down, down_far, far[0])
    down_far = place.send(down, far[1])
    (attended_other,) = after(attended_other)
    attended = join(attended_here, attended_other, 1, block)
    out = place.meet(out, out_y, y)
    gate = place.meet(gate, gate_y, y)
    up = place.meet(up, up_blk, "blk")
    full_out, full_gate, full_up = [
        flat(place.meet(whole, place.send(whole, core), core)) for whole in (out, gate, up)
    ]
    patch_rows = own_rows.astype(jnp.float32)
    middle = patch_rows + dot_nn(attended, full_out)
    normed_mlp = rms_norm(middle, norm_mlp).astype(jnp.bfloat16)
    gate_in = dot_nn(normed_mlp, full_gate)
    upward = dot_nn(normed_mlp, full_up)
    activated = jax.nn.gelu(gate_in, approximate=True)
    hidden = (activated * upward).astype(jnp.bfloat16)
    hidden, down_far = after(hidden, down_far)
    down = place.meet(down, down_far, far[1])
    for step in far[2:]:
        (down,) = advance([down], [step])
    full_down = flat(place.meet(down, place.send(down, core), core))
    output = (middle + dot_nn(hidden, full_down)).astype(jnp.bfloat16)
    grad_down = dot_tn(hidden, own_cot).astype(jnp.bfloat16)
    core_down = place.halves(place.part_of(grad_down, down_rows), core)
    grad_hidden = dot_nt(own_cot, full_down)
    unused_gelu, gelu_back = jax.vjp(lambda inner: jax.nn.gelu(inner, approximate=True), gate_in)
    grad_gate_in = gelu_back(grad_hidden * upward)[0].astype(jnp.bfloat16)
    grad_upward = (grad_hidden * activated).astype(jnp.bfloat16)
    grad_normed_mlp = dot_nt(grad_gate_in, full_gate) + dot_nt(grad_upward, full_up)
    unused_norm, second_back = jax.vjp(rms_norm, middle, norm_mlp)
    grad_middle_part, gain_mlp = second_back(grad_normed_mlp)
    grad_middle = own_cot.astype(jnp.float32) + grad_middle_part
    branch_grad = grad_middle.astype(jnp.bfloat16)
    grad_attended = dot_nt(branch_grad, full_out).astype(jnp.bfloat16)
    heads_here = lax.dynamic_slice_in_dim(grad_attended, block * half, half, 1)
    heads_sent = lax.dynamic_slice_in_dim(grad_attended, (1 - block) * half, half, 1)
    heads_there = swap_blocks(heads_sent)
    heads_sent, normed_mlp, attended = after(heads_sent, normed_mlp, attended)
    far_down = place.halves(add(*core_down), far[-1])
    grad_gate = dot_tn(normed_mlp, grad_gate_in).astype(jnp.bfloat16)
    grad_up = dot_tn(normed_mlp, grad_upward).astype(jnp.bfloat16)
    grad_out = dot_tn(attended, branch_grad).astype(jnp.bfloat16)
    cores = [place.halves(place.part_of(grad, shard_rows), core) for grad in (grad_gate, grad_up, grad_out)]
    part_gate, part_up, part_out = [add(*pair) for pair in cores]

    near = far[::-1]
    wide = place.halves(part_gate, y), place.halves(part_up, "blk"), place.halves(part_out, "blk")
    heads_here, unused_out = after(heads_here, part_out)
    queries_here, *sums = attend_back(where, qkv, attended_here, logs_here, heads_here, 0)
    sums, heads_there, far_down = after(sums, heads_there, far_down)
    far_down = place.halves(add(*far_down), near[1])
    queries_there, grad_keys, grad_values = attend_back(where, qkv, attended_there, logs_there, heads_there, 1, *sums)
    queries_there, grad_keys, grad_values, wide = after(queries_there, grad_keys, grad_values, wide)
    part_gate, part_up, part_out = [add(*pair) for pair in wide]

    wide = place.halves(part_gate, "blk"), place.halves(part_up, y)
    grad_queries = jnp.concatenate([queries_here, queries_there], 0)
    grad_qkv = jnp.concatenate([grad_queries, grad_keys, grad_values], 1)
    grad_w_qkv = dot_tn(all_normed, grad_qkv).astype(jnp.bfloat16)
    core_qkv = place.halves(place.part_of(grad_w_qkv, shard_rows), core)
    grad_all_normed = dot_nt(grad_qkv, w_qkv)
    unused_all, gain_back = jax.vjp(lambda gain: rms_norm(all_rows.astype(jnp.float32), gain), norm_attn)
    gains = jnp.stack([gain_back(grad_all_normed)[0], gain_mlp])
    core_qkv, wide, far_down, gains_core = after(core_qkv, wide, far_down, place.send(gains, core))
    gains = gains + gains_core
    part_qkv = add(*core_qkv)
    part_gate = jnp.concatenate([add(*pair) for pair in wide], -1)
    out_y = place.halves(part_out, y)

    gains = gains + swap_blocks(gains)
    rows_sent, gains = after(grad_all_normed[row_count:].astype(jnp.bfloat16), gains)
    rows_other = swap_blocks(rows_sent)
    moving = place.halves(part_qkv, y), place.halves(part_gate, near[0])
    part_out = add(*out_y)
    moving, gains_y, out_far = after(moving, place.send(gains, y), place.halves(part_out, near[0]))
    part_out, part_down = add(*out_far), add(*far_down)
    gains = gains + gains_y
    part_qkv, part_gate = [add(*pair) for pair in moving]

    moving = place.halves(part_qkv, near[0]), place.halves(part_gate, near[1]), place.halves(part_down, y)
    out_far = place.halves(part_out, near[1])
    moving, rows_other, gains_far, out_far = after(moving, rows_other, place.send(gains, near[0]), out_far)
    part_out = add(*out_far)
    gains = gains + gains_far
    part_qkv, part_gate, part_down = [add(*pair) for pair in moving]

    for step in near[2:]:
        part_gate, part_down = [add(*place.halves(part, step)) for part in (part_gate, part_down)]
    part_down = add(*place.halves(part_down, "blk"))
    for step in near[2:]:
        part_out = add(*place.halves(part_out, step))
    for step in near[1:]:
        pair, gains_far = after(place.halves(part_qkv, step), place.send(gains, step))
        part_qkv = add(*pair)
        gains = gains + gains_far
    grad_normed = grad_all_normed[:row_count] + rows_other.astype(jnp.float32)
    unused_first, first_back = jax.vjp(rms_norm, patch_rows, norm_attn)
    grad_rows_part, unused_gain = first_back(grad_normed)
    grad_patches = (grad_middle + grad_rows_part).astype(jnp.bfloat16)
    shard_qkv, shard_gate, shard_down = [flat(part).astype(jnp.float32) for part in (part_qkv, part_gate, part_down)]
    inner = w_gate.shape[1]
    return (
        output[None],
        grad_patches[None],
        gains[0],
        shard_qkv[:, :half],
        shard_qkv[:, half : 2 * half],
        shard_qkv[:, 2 * half :],
        flat(part_out).astype(jnp.float32),
        gains[1],
        shard_gate[:, :inner],
        shard_gate[:, inner : 2 * inner],
        shard_down,
    )


def local(items, blocks, patches, *rest):
    items_here, row_count, model_width = patches.shape
    fits = (
        blocks == 2
        and items_here == 1
        and items >= 16
        and items & (items - 1) == 0
        and row_count % 128 == 0
        and model_width % 256 == 0
    )
    if fits:
        return by_heads(items, patches, *rest)
    return general(patches, *rest)


def solution(mesh):
    placed = (
        P("items", "blk", None),
        P("items", None),
        P(),
        P("items", "blk"),
        P("items", "blk"),
        P("items", "blk"),
        P("items", "blk"),
        P(),
        P("items", "blk"),
        P("items", "blk"),
        P("items", "blk"),
        P("items", "blk", None),
    )
    return jax.shard_map(
        functools.partial(local, mesh.shape["items"], mesh.shape["blk"]),
        mesh=mesh,
        in_specs=placed,
        out_specs=(
            P("items", "blk", None),
            P("items", "blk", None),
            P(),
            P("items", "blk"),
            P("items", "blk"),
            P("items", "blk"),
            P("items", "blk"),
            P(),
            P("items", "blk"),
            P("items", "blk"),
            P("items", "blk"),
        ),
        check_vma=False,
    )
```
